32 devices in a mesh: ctx: 8 (over z, x), wshard: 4 (over y, core).
Axes of the slice: x: 2, y: 2, z: 4, core: 2. Of those that a mesh axis runs over, the one named last changes fastest.
Arguments:
- tokens: bfloat16 [4, 4096, 1024], P('wshard', 'ctx'), may hold values from -6 to 6
- cotangent: bfloat16 [4, 4096, 1024], P('wshard', 'ctx'), may hold values from -6 to 6
- doc_lengths: int32 [4, 4], P('wshard'), may hold values from 1 to 4093, as said below
- decay: float32 [4, 24, 4096], P('wshard', None, 'ctx')
- norm_gain: bfloat16 [1024], P('wshard'), may hold values from 0.25 to 1.75
- in_proj: bfloat16 [1024, 3328], P('wshard'), may hold values from -0.1875 to 0.1875
- conv_weight: bfloat16 [4, 1792], P(None, 'wshard'), may hold values from -3 to 3
- conv_bias: bfloat16 [1792], P('wshard'), may hold values from -3 to 3
- skip_gain: bfloat16 [24], P('wshard'), may hold values from 0.5 to 1.5
- mixer_gain: bfloat16 [1536], P('wshard'), may hold values from 0.25 to 1.75
- mixer_out: bfloat16 [1536, 1024], P('wshard'), may hold values from -0.15625 to 0.15625
- query_proj: bfloat16 [1024, 512], P('wshard'), may hold values from -0.1875 to 0.1875
- key_value_projection: bfloat16 [1024, 256], P('wshard'), may hold values from -0.1875 to 0.1875
- attn_out: bfloat16 [512, 1024], P('wshard'), may hold values from -3 to 3
- ffn_gain: bfloat16 [1024], P('wshard'), may hold values from 0.25 to 1.75
- gate_up: bfloat16 [1024, 4096], P('wshard'), may hold values from -0.1875 to 0.1875
- down_proj: bfloat16 [2048, 1024], P('wshard'), may hold values from -0.125 to 0.125
Outputs:
- layer_out: bfloat16 [4, 4096, 1024], P('wshard', 'ctx')
- tokens_grad: float32 [4, 4096, 1024], P('wshard', 'ctx')
- norm_gain_grad: float32 [1024], P('wshard')
- in_proj_grad: float32 [1024, 3328], P('wshard')
- conv_weight_grad: float32 [4, 1792], P(None, 'wshard')
- conv_bias_grad: float32 [1792], P('wshard')
- skip_gain_grad: float32 [24], P('wshard')
- mixer_gain_grad: float32 [1536], P('wshard')
- mixer_out_grad: float32 [1536, 1024], P('wshard')
- query_proj_grad: float32 [1024, 512], P('wshard')
- keyval_proj_grad: float32 [1024, 256], P('wshard')
- attn_out_grad: float32 [512, 1024], P('wshard')
- ffn_gain_grad: float32 [1024], P('wshard')
- gate_up_grad: float32 [1024, 4096], P('wshard')
- down_proj_grad: float32 [2048, 1024], P('wshard')
The draws below stay inside these ranges and needn't reach their ends.
Inputs may be any that keep to these rules, and one draw needn't show every extreme that they name: `doc_lengths`: each row sums to 4096; in every group one document, never the first or the last, begins on the group's first device and ends on its last; in the first group every other document has length 1.
All inputs are finite; a program needn't handle non-finite values.
Results may differ from the reference program's by a relative error of at most 0.025.
The reference program's roundings to bfloat16 on the way count: a program that leaves them out, or rounds other values in their place, can miss the bound.
Values may be sent and summed in bfloat16 or wider, within the bound.
No kernel may reach another device: no remote copies, remote signals or barrier semaphores. Data moves between devices by JAX's collectives and lax.ppermute only.
A program may use at most 256 MiB of HBM per device.

```python
import math
import jax
import jax.numpy as jnp
from jax import lax

MODEL_WIDTH = 1024
FF = 2048
QUERY_HEADS = 8
KEY_VALUE_HEADS = 2
HEAD_SIZE = 64
HM = 24
PM = 64
NS = 128
KW = 4
TOK_DEV = 512
DOCS = 4
TOKEN_STREAMS = 4
STREAM_LENGTH = 4096
DSSM = 1536
XBC = 1792
PROJ = 3328


def draw_doc_lengths(key, part):
    key = jax.random.fold_in(key, 11)
    first, second = jax.random.split(key)
    short = jax.random.randint(first, (TOKEN_STREAMS, DOCS), 1, TOK_DEV // 2)
    leading = jnp.arange(TOKEN_STREAMS, dtype=jnp.int32)[:, None] == 0
    short = jnp.where(leading, 1, short)
    span_at = jax.random.randint(second, (TOKEN_STREAMS, 1), 1, DOCS - 1)
    slots = jnp.arange(DOCS, dtype=jnp.int32)[None, :]
    spanning = slots == span_at
    others = jnp.sum(jnp.where(spanning, 0, short), axis=1, keepdims=True)
    return jnp.where(spanning, STREAM_LENGTH - others, short).astype(jnp.int32)


def draw_decay(key, part):
    key = jax.random.fold_in(key, 5)
    key_matrix = jax.random.split(key, 6)
    slow_share = 0.5
    slow = jax.random.uniform(key_matrix[0], (TOKEN_STREAMS, HM, 1)) < slow_share
    slow_rate = jnp.exp(jax.random.uniform(key_matrix[1], (TOKEN_STREAMS, HM, 1), minval=math.log(0.1), maxval=0.0)) / STREAM_LENGTH
    fast_rate = 1.0 / jax.random.uniform(key_matrix[2], (TOKEN_STREAMS, HM, 1), minval=30.0, maxval=50.0)
    rough = jnp.exp(jax.random.uniform(key_matrix[3], (TOKEN_STREAMS, HM, STREAM_LENGTH), minval=-math.log(2.0), maxval=math.log(2.0)))
    token_spurt = jax.random.randint(key_matrix[4], (TOKEN_STREAMS, 1, STREAM_LENGTH), 0, STREAM_LENGTH // 2) == 0
    split_point = jax.random.uniform(key_matrix[5], (TOKEN_STREAMS, 1, STREAM_LENGTH), minval=0.5, maxval=0.8)
    decay_speed = jnp.where(slow, slow_rate, fast_rate) * rough
    return (jnp.exp(-decay_speed) * jnp.where(token_spurt, split_point, 1.0)).astype(jnp.float32)


def block_levels(rng, shape, pieces, smallest, largest):
    level = 1.0
    for axis_at, blocks in pieces:
        steps = jax.random.uniform(jax.random.fold_in(jax.random.fold_in(rng, 6), axis_at), (blocks,), jnp.float32, smallest / len(pieces), largest / len(pieces))
        level = level * jnp.repeat(jnp.exp(steps), shape[axis_at] // blocks).reshape((-1,) + (1,) * (len(shape) - 1 - axis_at))
    return level


def noise(stream_key, shape, deviation, bound, shards=(), kind=jnp.bfloat16):
    result = deviation * jax.random.normal(stream_key, shape, jnp.float32)
    if shards:
        result = result * block_levels(stream_key, shape, shards, -0.22, 0.18)
    return jnp.clip(result, -bound, bound).astype(kind)


def setup_inputs(seed: int = 0) -> dict:
    keys = jax.random.split(jax.random.key(seed), 18)
    return {
        "tokens": noise(keys[0], (TOKEN_STREAMS, STREAM_LENGTH, MODEL_WIDTH), 1.0, 6.0, ((0, 4), (1, 8))),
        "cotangent": noise(keys[1], (TOKEN_STREAMS, STREAM_LENGTH, MODEL_WIDTH), 1.0, 6.0, ((0, 4), (1, 8))),
        "doc_lengths": draw_doc_lengths(jax.random.fold_in(keys[17], 71), 0),
        "decay": draw_decay(jax.random.fold_in(keys[17], 71), 0),
        "norm_gain": jnp.clip(1.0 + 0.15 * jax.random.normal(keys[4], (MODEL_WIDTH,), jnp.float32), 0.25, 1.75).astype(jnp.bfloat16),
        "in_proj": noise(keys[5], (MODEL_WIDTH, PROJ), MODEL_WIDTH ** -0.5, 0.1875, ((0, 4),)),
        "conv_weight": noise(keys[6], (KW, XBC), KW ** -0.5, 3.0, ((1, 4),)),
        "conv_bias": noise(keys[7], (XBC,), 0.5, 3.0, ((0, 4),)),
        "skip_gain": jnp.clip(0.5 + 1.0 * jax.random.uniform(keys[8], (HM,), jnp.float32) ** block_levels(keys[8], (HM,), ((0, 4),), -0.2, 0.2), 0.5, 1.5).astype(jnp.bfloat16),
        "mixer_gain": jnp.clip(1.0 + 0.15 * jax.random.normal(keys[9], (DSSM,), jnp.float32), 0.25, 1.75).astype(jnp.bfloat16),
        "mixer_out": noise(keys[10], (DSSM, MODEL_WIDTH), DSSM ** -0.5, 0.15625, ((0, 4),)),
        "query_proj": noise(keys[11], (MODEL_WIDTH, QUERY_HEADS * HEAD_SIZE), MODEL_WIDTH ** -0.5, 0.1875, ((0, 4),)),
        "key_value_projection": noise(keys[12], (MODEL_WIDTH, 2 * KEY_VALUE_HEADS * HEAD_SIZE), MODEL_WIDTH ** -0.5, 0.1875, ((0, 4),)),
        "attn_out": noise(keys[13], (QUERY_HEADS * HEAD_SIZE, MODEL_WIDTH), 4 ** -0.5, 3.0, ((0, 4),)),
        "ffn_gain": jnp.clip(1.0 + 0.15 * jax.random.normal(keys[14], (MODEL_WIDTH,), jnp.float32), 0.25, 1.75).astype(jnp.bfloat16),
        "gate_up": noise(keys[15], (MODEL_WIDTH, 2 * FF), MODEL_WIDTH ** -0.5, 0.1875, ((0, 4),)),
        "down_proj": noise(keys[16], (FF, MODEL_WIDTH), FF ** -0.5, 0.125, ((0, 4),)),
    }


@jax.custom_vjp
def reduced_precision(v):
    return lax.optimization_barrier(v.astype(jnp.bfloat16)).astype(jnp.float32)

@jax.custom_vjp
def low_back(v):
    return v

def low_keep(v):
    return (reduced_precision(v), None)

def low_pass(kept, grad):
    return (grad,)

def back_keep(v):
    return (v, None)

def back_low(kept, grad):
    return (reduced_precision(grad),)
reduced_precision.defvjp(low_keep, low_pass)
low_back.defvjp(back_keep, back_low)
eps_norm = 1e-05
rope_base = 100000000000.0
mask_fill_value = -1e+30
highest = lax.Precision.HIGHEST

def exact_dot(left, right):
    return jnp.dot(left, right, precision=highest)

def exact_sum(form, left, right):
    return jnp.einsum(form, left, right, precision=highest)

def rms_scale(value, gain):
    return value * lax.rsqrt(lax.optimization_barrier(jnp.mean(value * value, axis=-1, keepdims=True)) + eps_norm) * gain

def doc_numbers(lengths, position_index):
    ends = jnp.cumsum(lengths)[:-1]
    tally_count = lax.optimization_barrier(jnp.sum((position_index[:, None] >= ends[None, :]).astype(jnp.int32), axis=1))
    return jnp.where(position_index >= 0, tally_count, -1).astype(jnp.int32)

def rotary_apply(value, position_index):
    half = value.shape[-1] // 2
    freq = rope_base ** (-jnp.arange(half, dtype=jnp.float32) / half)
    angle = position_index.astype(jnp.float32)[:, None] * freq[None, :]
    cosine = jnp.cos(angle)[:, None, :]
    sine = jnp.sin(angle)[:, None, :]
    first = value[..., :half]
    second = value[..., half:]
    return jnp.concatenate([first * cosine - second * sine, second * cosine + first * sine], axis=-1)

def mixer_conv(pre, conv_weight, conv_bias, lengths, docs, position_index):
    tally_count = pre.shape[0]
    padded = jnp.concatenate([jnp.zeros((KW - 1, pre.shape[1]), jnp.float32), pre], axis=0)
    total = conv_bias[None, :]
    for tap in range(KW):
        same = (doc_numbers(lengths, position_index - (KW - 1) + tap) == docs).astype(jnp.float32)
        total = total + conv_weight[tap][None, :] * padded[tap:tap + tally_count] * same[:, None]
    return jax.nn.silu(total)

def ssd_block(state, xs, bs, cs, log_decay, docs, doc_prev):
    tally_count = xs.shape[0]
    running = jnp.cumsum(log_decay, axis=1)
    order = jnp.arange(tally_count)
    causal = ((order[:, None] >= order[None, :]) & (docs[:, None] == docs[None, :]))[None]
    decay_map = jnp.where(causal, jnp.exp(jnp.where(causal, running[:, :, None] - running[:, None, :], 0.0)), 0.0)
    products = low_back(exact_dot(cs, bs.T))
    weights = reduced_precision(products[None] * decay_map)
    local = exact_sum('hts,shp->thp', weights, xs)
    entry = jnp.where((docs == doc_prev)[None, :], jnp.exp(running), 0.0)
    inner = exact_sum('tn,hpn->thp', cs, state) * entry.T[:, :, None]
    mixed = low_back(local + inner)
    tail = jnp.where((docs == docs[-1])[None, :], jnp.exp(running[:, -1:] - running), 0.0)
    fresh = exact_sum('shp,sn->hpn', xs * tail.T[:, :, None], bs)
    gain = jnp.where(docs[-1] == doc_prev, jnp.exp(running[:, -1]), 0.0)
    return (gain[:, None, None] * state + fresh, mixed)

def attention(query_matrix, key_matrix, value_matrix, docs, position_index):
    tally_count = query_matrix.shape[0]
    span_width = min(512, tally_count)
    gathered_heads = query_matrix.reshape(tally_count, KEY_VALUE_HEADS, QUERY_HEADS // KEY_VALUE_HEADS, HEAD_SIZE)

    def one_block(begin_offset):
        row_listing = lax.dynamic_slice_in_dim(gathered_heads, begin_offset, span_width, 0)
        query_pos = lax.dynamic_slice_in_dim(position_index, begin_offset, span_width, 0)
        query_doc = lax.dynamic_slice_in_dim(docs, begin_offset, span_width, 0)
        scores = low_back(exact_sum('qgrd,kgd->grqk', row_listing, key_matrix) * HEAD_SIZE ** (-0.5))
        mask = (position_index[None, :] <= query_pos[:, None]) & (docs[None, :] == query_doc[:, None])
        top = lax.optimization_barrier(jnp.max(jnp.where(mask, scores, mask_fill_value), axis=-1, keepdims=True))
        expo = jnp.where(mask, jnp.exp(jnp.where(mask, scores - top, 0.0)), 0.0)
        probs = reduced_precision(expo / lax.optimization_barrier(jnp.sum(expo, axis=-1, keepdims=True)))
        return exact_sum('grqk,kgd->qgrd', probs, value_matrix).reshape(span_width, QUERY_HEADS * HEAD_SIZE)
    starts = jnp.arange(tally_count // span_width, dtype=jnp.int32) * span_width
    return lax.map(jax.checkpoint(one_block), starts).reshape(tally_count, QUERY_HEADS * HEAD_SIZE)

def layer(tokens, params, docs, position_index, lengths, log_decay):
    norm_gain, in_proj, conv_weight, conv_bias, skip_gain, mixer_gain, mixer_out, query_proj, key_value_projection, attn_out, ffn_gain, gate_up, down_proj = params
    tally_count = tokens.shape[0]
    normed = reduced_precision(rms_scale(tokens, norm_gain))
    projected = low_back(exact_dot(normed, in_proj))
    gate_z = projected[:, :DSSM]
    pre_conv = reduced_precision(projected[:, DSSM:])
    conv_out = reduced_precision(mixer_conv(pre_conv, conv_weight, conv_bias, lengths, docs, position_index))
    xs = conv_out[:, :DSSM].reshape(tally_count, HM, PM)
    bs = conv_out[:, DSSM:DSSM + NS]
    cs = conv_out[:, DSSM + NS:]
    blocks = tally_count // TOK_DEV
    starts = jnp.arange(blocks, dtype=jnp.int32) * TOK_DEV
    prev = doc_numbers(lengths, starts - 1)

    def step(state, piece):
        return ssd_block(state, piece[0], piece[1], piece[2], piece[3], piece[4], piece[5])
    scanned = (xs.reshape(blocks, TOK_DEV, HM, PM), bs.reshape(blocks, TOK_DEV, NS), cs.reshape(blocks, TOK_DEV, NS), log_decay.reshape(HM, blocks, TOK_DEV).transpose(1, 0, 2), docs.reshape(blocks, TOK_DEV), prev)
    state_zero = jnp.zeros((HM, PM, NS), jnp.float32)
    _, mixed = lax.scan(jax.checkpoint(step), state_zero, scanned)
    mixed = mixed.reshape(tally_count, HM, PM) + skip_gain[None, :, None] * xs
    gated = reduced_precision(rms_scale(mixed.reshape(tally_count, DSSM) * jax.nn.silu(gate_z), mixer_gain))
    mamba = low_back(exact_dot(gated, mixer_out))
    query_matrix = reduced_precision(rotary_apply(low_back(exact_dot(normed, query_proj)).reshape(tally_count, QUERY_HEADS, HEAD_SIZE), position_index))
    key_value_pair = low_back(exact_dot(normed, key_value_projection))
    key_matrix = reduced_precision(rotary_apply(key_value_pair[:, :KEY_VALUE_HEADS * HEAD_SIZE].reshape(tally_count, KEY_VALUE_HEADS, HEAD_SIZE), position_index))
    value_matrix = reduced_precision(key_value_pair[:, KEY_VALUE_HEADS * HEAD_SIZE:].reshape(tally_count, KEY_VALUE_HEADS, HEAD_SIZE))
    heads = reduced_precision(low_back(attention(query_matrix, key_matrix, value_matrix, docs, position_index)))
    attn = low_back(exact_dot(heads, attn_out))
    middle = tokens + attn + mamba
    normed2 = reduced_precision(rms_scale(middle, ffn_gain))
    gate_up_v = low_back(exact_dot(normed2, gate_up))
    activated = reduced_precision(jax.nn.silu(gate_up_v[:, :FF]) * gate_up_v[:, FF:])
    return middle + low_back(exact_dot(activated, down_proj))

def reference(tokens, cotangent, doc_lengths, decay, norm_gain, in_proj, conv_weight, conv_bias, skip_gain, mixer_gain, mixer_out, query_proj, key_value_projection, attn_out, ffn_gain, gate_up, down_proj):
    params = tuple((w.astype(jnp.float32) for w in (norm_gain, in_proj, conv_weight, conv_bias, skip_gain, mixer_gain, mixer_out, query_proj, key_value_projection, attn_out, ffn_gain, gate_up, down_proj)))
    position_index = jnp.arange(STREAM_LENGTH, dtype=jnp.int32)
    outputs = []
    input_grads = []
    totals = None
    for group in range(TOKEN_STREAMS):
        lengths = doc_lengths[group]
        docs = doc_numbers(lengths, position_index)
        log_decay = jnp.log(decay[group])

        def forward(source, weights):
            return layer(source, weights, docs, position_index, lengths, log_decay)
        value, pull = jax.vjp(forward, tokens[group].astype(jnp.float32), params)
        source_grad, param_grads = pull(cotangent[group].astype(jnp.float32))
        outputs.append(value.astype(jnp.bfloat16))
        input_grads.append(source_grad)
        if totals is None:
            totals = param_grads
        else:
            totals = jax.tree.map(jnp.add, totals, param_grads)
    return (jnp.stack(outputs), jnp.stack(input_grads), totals[0], totals[1], totals[2], totals[3], totals[4], totals[5], totals[6], totals[7], totals[8], totals[9], totals[10], totals[11], totals[12])
```

```python
from functools import partial

import jax
import jax.numpy as jnp
from jax import lax
from jax.experimental import pallas as pl
from jax.experimental.pallas import tpu as pltpu
from jax.sharding import PartitionSpec as P

FF = 2048
QUERY_HEADS = 8
KEY_VALUE_HEADS = 2
HEAD_SIZE = 64
HM = 24
PM = 64
NS = 128
KW = 4
DSSM = 1536

eps_norm = 1e-05
rope_base = 100000000000.0
mask_fill_value = -1e30
highest = lax.Precision.HIGHEST
MESH_AXES = ("ctx", "wshard")


def exchange(block, ctx_flip, shard_flip):
    blocks, shards = lax.axis_size("ctx"), lax.axis_size("wshard")
    route = [
        (c * shards + w, (c ^ ctx_flip) * shards + (w ^ shard_flip))
        for c in range(blocks)
        for w in range(shards)
    ]
    return lax.ppermute(block, MESH_AXES, route)


def from_behind(block, axis, distance):
    devices = range(lax.axis_size(axis))
    route = [(i - distance, i) for i in devices if i - distance in devices]
    return lax.ppermute(block, axis, route)


def swap_mirrored(block):
    count = lax.axis_size("ctx")
    return lax.ppermute(block, "ctx", [(i, count - 1 - i) for i in range(count)])


def place(pieces):
    total = sum(piece.shape[0] for _, piece in pieces)
    whole = jnp.zeros((total,) + pieces[0][1].shape[1:], pieces[0][1].dtype)
    for start, piece in pieces:
        whole = lax.dynamic_update_slice_in_dim(whole, piece, start, 0)
    return whole


def gather_shards(shard):
    rows = shard.shape[0]
    half = rows // 2
    w = lax.axis_index("wshard")
    side = lax.axis_index("ctx") % 2
    mine = lax.dynamic_slice_in_dim(shard, side * half, half, 0)
    beside = exchange(shard, 0, 1)
    across = exchange(mine, 0, 2)
    across_rest = exchange(across, 1, 0)
    far = exchange(across, 0, 1)
    far_rest = exchange(across_rest, 0, 1)
    here, there = side * half, (1 - side) * half
    return place(
        [
            (w * rows, shard),
            ((w ^ 1) * rows, beside),
            ((w ^ 2) * rows + here, across),
            ((w ^ 2) * rows + there, across_rest),
            ((w ^ 3) * rows + here, far),
            ((w ^ 3) * rows + there, far_rest),
        ]
    )


def gather_small(shard):
    rows = shard.shape[0]
    w = lax.axis_index("wshard")
    return place(
        [(w * rows, shard)]
        + [((w ^ flip) * rows, exchange(shard, 0, flip)) for flip in (1, 2, 3)]
    )


def add_low(first, *others):
    total = first.astype(jnp.float32)
    for other in others:
        total = total + other.astype(jnp.float32)
    return total.astype(jnp.bfloat16)


def ctx_sum(block):
    position = lax.axis_index("ctx")
    bits = []
    bit = 1
    while bit < lax.axis_size("ctx"):
        bits.append(bit)
        bit *= 2
    for bit in bits:
        half = block.shape[0] // 2
        up = (position // bit) % 2
        got = exchange(lax.dynamic_slice_in_dim(block, (1 - up) * half, half, 0), bit, 0)
        block = add_low(lax.dynamic_slice_in_dim(block, up * half, half, 0), got)
    for bit in reversed(bits):
        up = (position // bit) % 2
        got = exchange(block, bit, 0)
        block = jnp.where(
            up == 0, jnp.concatenate([block, got], axis=0), jnp.concatenate([got, block], axis=0)
        )
    return block.astype(jnp.float32)


def shard_pieces(array, axis):
    w = lax.axis_index("wshard")
    size = array.shape[axis] // 4

    def piece(flip):
        return lax.dynamic_slice_in_dim(array, (w ^ flip) * size, size, axis)

    return jnp.concatenate([piece(1), piece(3)], axis=axis), piece(2), piece(0)


def shard_sum(beside, across, own):
    rows = own.shape[0]
    got = exchange(beside.astype(jnp.bfloat16), 0, 1)
    got_across = exchange(add_low(across, got[rows:]), 0, 2)
    return add_low(own, got[:rows], got_across)


def weight_grad(left, right, axis=1):
    products = [
        lax.dot_general(
            piece, right, (((1 - axis,), (0,)), ((), ())), preferred_element_type=jnp.float32
        )
        for piece in shard_pieces(left, axis)
    ]
    return shard_sum(*products)


def mixed_dot(left, right):
    return jnp.dot(left, right, preferred_element_type=jnp.float32)


def rms_scale(value, gain):
    return value * lax.rsqrt(jnp.mean(value * value, axis=-1, keepdims=True) + eps_norm) * gain


def doc_numbers(lengths, position_index):
    ends = jnp.cumsum(lengths)[:-1]
    tally_count = jnp.sum((position_index[:, None] >= ends[None, :]).astype(jnp.int32), axis=1)
    return jnp.where(position_index >= 0, tally_count, -1)


def turn(value, position_index):
    half = value.shape[-2] // 2
    freq = rope_base ** (-jnp.arange(half, dtype=jnp.float32) / half)
    angle = freq[:, None] * position_index.astype(jnp.float32)[None, :]
    cosine = jnp.cos(angle)
    sine = jnp.sin(angle)
    first = value[..., :half, :]
    second = value[..., half:, :]
    return jnp.concatenate(
        [first * cosine - second * sine, second * cosine + first * sine], axis=-2
    )


def conv_local(taps, extended, weight, bias):
    tally_count = extended.shape[0] - (KW - 1)
    total = bias[None, :]
    for tap in range(KW):
        total = (
            total + weight[tap][None, :] * extended[tap : tap + tally_count] * taps[tap][:, None]
        )
    return jax.nn.silu(total)


def gate_norm(mixed, gate_z, gain):
    return rms_scale(mixed * jax.nn.silu(gate_z), gain)


def swiglu(gate_up_v):
    return jax.nn.silu(gate_up_v[:, :FF]) * gate_up_v[:, FF:]


def split_three(value):
    high = value.astype(jnp.bfloat16)
    rest = value - high.astype(jnp.float32)
    middle = rest.astype(jnp.bfloat16)
    low = (rest - middle.astype(jnp.float32)).astype(jnp.bfloat16)
    return [high, middle, low]


def nt_dot(left, right):
    return lax.dot_general(left, right, (((1,), (1,)), ((), ())), preferred_element_type=jnp.float32)


def causal_tile(scores, group, width):
    rows = lax.broadcasted_iota(jnp.int32, scores.shape, 0)
    columns = lax.broadcasted_iota(jnp.int32, scores.shape, 1)
    return jnp.where(rows <= lax.rem(columns, width) + group * width, scores, mask_fill_value)


def load_extended(extended, lower, value_ref, side_ref):
    for group in range(2):
        extended[group] = jnp.zeros(extended.shape[1:], extended.dtype)
        extended[group, lower : lower + HEAD_SIZE, :] = value_ref[group, 0]
        extended[group, 128:144, :] = side_ref[group, 0]


def attend_forward_body(
    width, blocks, pair_ref, side_ref, query_ref, query_side_ref, heads_ref, log_ref, query_x, peak, total
):
    step = pl.program_id(1)

    @pl.when(step == 0)
    def start():
        load_extended(query_x, 0, query_ref, query_side_ref)
        peak[...] = jnp.full(peak.shape, mask_fill_value, jnp.float32)
        total[...] = jnp.zeros(total.shape, jnp.float32)

    @pl.when(step <= jnp.maximum(blocks[0], blocks[1]))
    def work():
        keys = jnp.concatenate([pair_ref[0, 0], side_ref[...]], axis=1)
        values = keys.T[HEAD_SIZE:144]

        def tile(group, masked):
            scores = mixed_dot(keys, query_x[group])
            if masked:
                scores = causal_tile(scores, group, width)
            old = peak[group]
            new = jnp.maximum(old, jnp.max(scores, axis=0, keepdims=True))
            probs = jnp.exp(scores - new)
            total[group] = total[group] * jnp.exp(old - new) + mixed_dot(
                values, probs.astype(jnp.bfloat16)
            )
            peak[group] = new

        for group in range(2):
            pl.when(step < blocks[group])(partial(tile, group, False))
            pl.when(step == blocks[group])(partial(tile, group, True))

    @pl.when(step == pl.num_programs(1) - 1)
    def finish():
        for group in range(2):
            weight = total[group, HEAD_SIZE + 8 : HEAD_SIZE + 9, :]
            heads_ref[group, 0] = total[group, :HEAD_SIZE, :] / weight
            log_ref[group, 0] = peak[group] + jnp.log(weight)


def attend_backward_body(
    width,
    blocks,
    pair_ref,
    side_ref,
    query_ref,
    query_side_ref,
    grad_ref,
    grad_side_ref,
    query_grad_ref,
    pair_grad_ref,
    query_x,
    grad_x,
    pair_acc,
):
    step = pl.program_id(1)

    @pl.when(step == 0)
    def start():
        load_extended(query_x, 0, query_ref, query_side_ref)
        load_extended(grad_x, HEAD_SIZE, grad_ref, grad_side_ref)
        query_grad_ref[...] = jnp.zeros(query_grad_ref.shape, jnp.float32)

    pair_acc[...] = jnp.zeros(pair_acc.shape, jnp.float32)

    @pl.when(step <= jnp.maximum(blocks[0], blocks[1]))
    def work():
        pair = pair_ref[0, 0]
        keys = jnp.concatenate([pair, side_ref[...]], axis=1)
        turned = pair.T[:HEAD_SIZE]

        def tile(group, masked):
            scores = mixed_dot(keys, query_x[group])
            if masked:
                scores = causal_tile(scores, group, width)
            probs = jnp.exp(scores)
            low = (probs * mixed_dot(keys, grad_x[group])).astype(jnp.bfloat16)
            pair_acc[...] += nt_dot(low, query_x[group, :128, :]) + nt_dot(
                probs.astype(jnp.bfloat16), grad_x[group, :128, :]
            )
            query_grad_ref[group, 0] += mixed_dot(turned, low)

        for group in range(2):
            pl.when(step < blocks[group])(partial(tile, group, False))
            pl.when(step == blocks[group])(partial(tile, group, True))

    pair_grad_ref[0, 0] = pair_acc[...].astype(jnp.bfloat16)


def attention_calls(rows, count):
    width = rows // 2
    span = width * (QUERY_HEADS // KEY_VALUE_HEADS)

    def last(blocks):
        return jnp.maximum(blocks[0], blocks[1])

    pair_spec = pl.BlockSpec(
        (1, 1, rows, 128), lambda g, k, blocks: (jnp.minimum(k, last(blocks)), g, 0, 0)
    )
    side_spec = pl.BlockSpec((rows, 128), lambda g, k, blocks: (jnp.minimum(k, last(blocks)), 0))

    def per_group(height):
        return pl.BlockSpec((2, 1, height, span), lambda g, k, blocks: (0, g, 0, 0))

    elements = KEY_VALUE_HEADS * (count + 1) * rows * span
    params = pltpu.CompilerParams(
        dimension_semantics=("arbitrary", "arbitrary"), vmem_limit_bytes=48 * 1024 * 1024
    )
    forward = pl.pallas_call(
        partial(attend_forward_body, width),
        grid_spec=pltpu.PrefetchScalarGridSpec(
            num_scalar_prefetch=1,
            grid=(KEY_VALUE_HEADS, count),
            in_specs=[pair_spec, side_spec, per_group(HEAD_SIZE), per_group(16)],
            out_specs=[per_group(HEAD_SIZE), per_group(1)],
            scratch_shapes=[
                pltpu.VMEM((2, 256, span), jnp.bfloat16),
                pltpu.VMEM((2, 1, span), jnp.float32),
                pltpu.VMEM((2, 144 - HEAD_SIZE, span), jnp.float32),
            ],
        ),
        out_shape=[
            jax.ShapeDtypeStruct((2, KEY_VALUE_HEADS, HEAD_SIZE, span), jnp.float32),
            jax.ShapeDtypeStruct((2, KEY_VALUE_HEADS, 1, span), jnp.float32),
        ],
        compiler_params=params,
        cost_estimate=pl.CostEstimate(
            flops=elements * 512, bytes_accessed=8 * rows * 1024 * count, transcendentals=elements
        ),
        name="attend_forward",
    )
    backward = pl.pallas_call(
        partial(attend_backward_body, width),
        grid_spec=pltpu.PrefetchScalarGridSpec(
            num_scalar_prefetch=1,
            grid=(KEY_VALUE_HEADS, count),
            in_specs=[
                pair_spec,
                side_spec,
                per_group(HEAD_SIZE),
                per_group(16),
                per_group(HEAD_SIZE),
                per_group(16),
            ],
            out_specs=[
                per_group(HEAD_SIZE),
                pl.BlockSpec((1, 1, rows, 128), lambda g, k, blocks: (k, g, 0, 0)),
            ],
            scratch_shapes=[
                pltpu.VMEM((2, 256, span), jnp.bfloat16),
                pltpu.VMEM((2, 256, span), jnp.bfloat16),
                pltpu.VMEM((rows, 128), jnp.float32),
            ],
        ),
        out_shape=[
            jax.ShapeDtypeStruct((2, KEY_VALUE_HEADS, HEAD_SIZE, span), jnp.float32),
            jax.ShapeDtypeStruct((count, KEY_VALUE_HEADS, rows, 128), jnp.bfloat16),
        ],
        compiler_params=params,
        cost_estimate=pl.CostEstimate(
            flops=elements * 1280, bytes_accessed=8 * rows * 1024 * count, transcendentals=elements
        ),
        name="attend_backward",
    )
    return forward, backward


def pick(pair):
    lane = lax.broadcasted_iota(jnp.int32, (pair.shape[0], 2 * PM), 1)
    return jnp.where(lane < PM, pair[:, 0:1], pair[:, 1:2])


def outer_body(rows_ref, left_ref, right_ref, out_ref):
    for at in range(rows_ref.shape[0]):
        scale = pick(rows_ref[at])
        left = left_ref[:, at * 128 : (at + 1) * 128].astype(jnp.float32) * scale
        out_ref[at * 128 : (at + 1) * 128, :] = lax.dot_general(
            left.astype(jnp.bfloat16),
            right_ref[...],
            (((0,), (0,)), ((), ())),
            preferred_element_type=jnp.float32,
        ).astype(out_ref.dtype)


def mixed_body(
    skip_ref, x_ref, b_ref, c_ref, column_ref, row_ref, entry_ref, docs_column, docs_row, state_ref, out_ref, fill, products
):
    rows = x_ref.shape[0]
    half = rows // 2

    @pl.when(pl.program_id(0) == 0)
    def start():
        at = lax.broadcasted_iota(jnp.int32, (rows, rows), 0)
        source = lax.broadcasted_iota(jnp.int32, (rows, rows), 1)
        same = (at >= source) & (docs_column[...] == docs_row[...])
        fill[...] = jnp.where(same, 0.0, mask_fill_value)
        products[...] = nt_dot(c_ref[...], b_ref[...])

    x = x_ref[...]
    lane = lax.broadcasted_iota(jnp.int32, (half, 2 * PM), 1)
    for block in range(2):
        here = slice(block * half, (block + 1) * half)
        width = (block + 1) * half
        parts = []
        for head in range(2):
            decay = jnp.exp(
                (column_ref[0, here, head : head + 1] - row_ref[0, head : head + 1, :width])
                + fill[here, :width]
            )
            weights = (products[here, :width] * decay).astype(jnp.bfloat16)
            parts.append(mixed_dot(weights, x[:width]))
        local = jnp.where(lane < PM, parts[0], parts[1])
        inner = nt_dot(c_ref[here, :], state_ref[...].astype(jnp.bfloat16))
        out_ref[here, :] = (
            local + inner * pick(entry_ref[0, here, :]) + x[here].astype(jnp.float32) * skip_ref[0]
        )


def mixed_grad_body(
    skip_ref,
    x_ref,
    b_ref,
    c_ref,
    column_ref,
    row_ref,
    entry_ref,
    tail_ref,
    docs_column,
    docs_row,
    state_ref,
    state_grad_ref,
    grad_ref,
    out_ref,
    skip_grad_ref,
    fill,
    products,
    scores,
    b_grad,
    c_grad,
):
    rows = x_ref.shape[0]
    half = rows // 2
    step = pl.program_id(0)
    pairs = HM // 2

    @pl.when(step == 0)
    def start():
        source = lax.broadcasted_iota(jnp.int32, (rows, rows), 0)
        at = lax.broadcasted_iota(jnp.int32, (rows, rows), 1)
        same = (at >= source) & (docs_column[...] == docs_row[...])
        fill[...] = jnp.where(same, 0.0, mask_fill_value)
        products[...] = nt_dot(b_ref[...], c_ref[...])
        scores[...] = jnp.zeros(scores.shape, jnp.float32)
        b_grad[...] = jnp.zeros(b_grad.shape, jnp.float32)
        c_grad[...] = jnp.zeros(c_grad.shape, jnp.float32)

    @pl.when(step < pairs)
    def work():
        x = x_ref[...]
        x_f = x.astype(jnp.float32)
        grad = grad_ref[...]
        low = grad.astype(jnp.bfloat16)
        lane = lax.broadcasted_iota(jnp.int32, (half, 2 * PM), 1)
        lane_all = lax.broadcasted_iota(jnp.int32, (rows, 2 * PM), 1)
        skip_grad_ref[0] = jnp.sum(grad * x_f, axis=0, keepdims=True)
        state_grad = state_grad_ref[...].astype(jnp.bfloat16)
        tail = pick(tail_ref[0])
        b_grad[...] += mixed_dot((x_f * tail).astype(jnp.bfloat16), state_grad)
        entered = (low.astype(jnp.float32) * pick(entry_ref[0])).astype(jnp.bfloat16)
        c_grad[...] += mixed_dot(entered, state_ref[...].astype(jnp.bfloat16))
        passed = nt_dot(b_ref[...], state_grad) * tail + grad * skip_ref[0]
        chosen = [
            jnp.where((lane_all < PM) == (head == 0), x_f, 0.0).astype(jnp.bfloat16)
            for head in range(2)
        ]
        for block in range(2):
            here = slice(block * half, (block + 1) * half)
            start_at = block * half
            parts = []
            for head in range(2):
                decay = jnp.exp(
                    (row_ref[0, head : head + 1, start_at:] - column_ref[0, here, head : head + 1])
                    + fill[here, start_at:]
                )
                weights = (products[here, start_at:] * decay).astype(jnp.bfloat16)
                parts.append(mixed_dot(weights, low[start_at:]))
                scores[here, start_at:] += nt_dot(chosen[head][here], low[start_at:]) * decay
            out_ref[here, :] = jnp.where(lane < PM, parts[0], parts[1]) + passed[here]

    @pl.when(step == pairs)
    def give_b():
        out_ref[...] = b_grad[...] + mixed_dot(scores[...].astype(jnp.bfloat16), c_ref[...])

    @pl.when(step == pairs + 1)
    def give_c():
        out_ref[...] = c_grad[...] + lax.dot_general(
            scores[...].astype(jnp.bfloat16),
            b_ref[...],
            (((0,), (0,)), ((), ())),
            preferred_element_type=jnp.float32,
        )


def mixer_calls(rows):
    pairs = HM // 2
    wide = 2 * PM
    params = pltpu.CompilerParams(
        dimension_semantics=("arbitrary",), vmem_limit_bytes=48 * 1024 * 1024
    )

    def capped(p):
        return jnp.minimum(p, pairs - 1)

    def outer(right_at):
        each = 2
        return pl.pallas_call(
            outer_body,
            grid=(pairs // each,),
            in_specs=[
                pl.BlockSpec((each, rows, 2), lambda p: (p, 0, 0)),
                pl.BlockSpec((rows, each * wide), lambda p: (0, p)),
                pl.BlockSpec((rows, NS), lambda p: (0, right_at)),
            ],
            out_specs=pl.BlockSpec((each * wide, NS), lambda p: (p, 0)),
            out_shape=jax.ShapeDtypeStruct((DSSM, NS), jnp.bfloat16),
            compiler_params=params,
            cost_estimate=pl.CostEstimate(
                flops=2 * rows * DSSM * NS, bytes_accessed=6 * rows * DSSM, transcendentals=0
            ),
            name="state_outer",
        )

    x_spec = pl.BlockSpec((rows, wide), lambda p: (0, capped(p)))
    b_spec = pl.BlockSpec((rows, NS), lambda p: (0, DSSM // NS))
    c_spec = pl.BlockSpec((rows, NS), lambda p: (0, DSSM // NS + 1))
    column_spec = pl.BlockSpec((1, rows, 2), lambda p: (capped(p), 0, 0))
    row_spec = pl.BlockSpec((1, 2, rows), lambda p: (capped(p), 0, 0))
    skip_spec = pl.BlockSpec((1, 1, wide), lambda p: (capped(p), 0, 0))
    state_spec = pl.BlockSpec((wide, NS), lambda p: (capped(p), 0))
    docs_specs = [pl.BlockSpec((rows, 1), lambda p: (0, 0)), pl.BlockSpec((1, rows), lambda p: (0, 0))]
    square = pltpu.VMEM((rows, rows), jnp.float32)
    narrow = pltpu.VMEM((rows, NS), jnp.float32)
    forward = pl.pallas_call(
        mixed_body,
        grid=(pairs,),
        in_specs=[skip_spec, x_spec, b_spec, c_spec, column_spec, row_spec, column_spec]
        + docs_specs
        + [state_spec],
        out_specs=pl.BlockSpec((rows, wide), lambda p: (0, p)),
        out_shape=jax.ShapeDtypeStruct((rows, DSSM), jnp.float32),
        scratch_shapes=[square, square],
        compiler_params=params,
        cost_estimate=pl.CostEstimate(
            flops=4 * rows * rows * DSSM, bytes_accessed=8 * rows * DSSM, transcendentals=HM * rows * rows
        ),
        name="mixer_forward",
    )
    backward = pl.pallas_call(
        mixed_grad_body,
        grid=(pairs + 2,),
        in_specs=[skip_spec, x_spec, b_spec, c_spec, column_spec, row_spec, column_spec, column_spec]
        + docs_specs
        + [state_spec, state_spec, x_spec],
        out_specs=[
            pl.BlockSpec((rows, wide), lambda p: (0, p)),
            pl.BlockSpec((1, 1, wide), lambda p: (capped(p), 0, 0)),
        ],
        out_shape=[
            jax.ShapeDtypeStruct((rows, DSSM + 2 * NS), jnp.float32),
            jax.ShapeDtypeStruct((pairs, 1, wide), jnp.float32),
        ],
        scratch_shapes=[square, square, square, narrow, narrow],
        compiler_params=params,
        cost_estimate=pl.CostEstimate(
            flops=8 * rows * rows * DSSM, bytes_accessed=12 * rows * DSSM, transcendentals=HM * rows * rows
        ),
        name="mixer_backward",
    )
    return outer, forward, backward


def chain(parts, gains, reverse):
    count, position = lax.axis_size("ctx"), lax.axis_index("ctx")
    factor = jnp.ones((HM,), jnp.float32)
    total = jnp.zeros((HM, PM, NS), jnp.float32)
    for at in range(count) if reverse else reversed(range(count)):
        reached = at > position if reverse else at < position
        part = parts[at].reshape(HM, PM, NS).astype(jnp.float32)
        total = total + jnp.where(reached, factor, 0.0)[:, None, None] * part
        factor = factor * jnp.where(reached, gains[at], 1.0)
    return total.reshape(DSSM, NS)


def pack_small(norm, conv_weight, conv_bias, skip, mixer, ffn, shards):
    pieces = [
        norm.reshape(shards, -1),
        conv_weight.reshape(KW, shards, -1).transpose(1, 0, 2).reshape(shards, -1),
        conv_bias.reshape(shards, -1),
        mixer.reshape(shards, -1),
        ffn.reshape(shards, -1),
        skip.reshape(shards, -1),
    ]
    packed = jnp.concatenate(pieces, axis=1)
    packed = jnp.pad(packed, ((0, 0), (0, 4096 - packed.shape[1])))
    return packed.reshape(shards * 32, 128)


def unpack_small(packed, model, channels, heads, shards):
    packed = packed.reshape(shards, 4096)
    sizes = [model, KW * channels, channels, DSSM, model, heads]
    parts, start = [], 0
    for size in sizes:
        width = size // 4
        parts.append(packed[:, start : start + width])
        start += width
    norm, conv_weight, conv_bias, mixer, ffn, skip = parts
    conv_weight = conv_weight.reshape(shards, KW, -1).transpose(1, 0, 2).reshape(KW, -1)
    return (
        norm.reshape(-1),
        conv_weight,
        conv_bias.reshape(-1),
        skip.reshape(-1),
        mixer.reshape(-1),
        ffn.reshape(-1),
    )


def per_device(
    tokens,
    cotangent,
    doc_lengths,
    decay,
    norm_gain,
    in_proj,
    conv_weight,
    conv_bias,
    skip_gain,
    mixer_gain,
    mixer_out,
    query_proj,
    key_value_projection,
    attn_out,
    ffn_gain,
    gate_up,
    down_proj,
):
    rows, model = tokens.shape[1:]
    width = rows // 2
    shards = lax.axis_size("wshard")
    channels = conv_bias.shape[0] * shards
    count, block_at = lax.axis_size("ctx"), lax.axis_index("ctx")
    sequence_total = rows * count
    heads_per_group = QUERY_HEADS // KEY_VALUE_HEADS
    scale = HEAD_SIZE ** (-0.5)
    attend_forward, attend_backward = attention_calls(rows, count)
    state_outer, mixer_forward, mixer_backward = mixer_calls(rows)

    small = gather_small(
        pack_small(norm_gain, conv_weight, conv_bias, skip_gain, mixer_gain, ffn_gain, 1)
    )
    norm_w, conv_w, conv_b, skip_w, mixer_g, ffn_g = (
        part.astype(jnp.float32) for part in unpack_small(small, model, channels, HM, shards)
    )
    attn_pair_w = gather_shards(jnp.concatenate([query_proj, key_value_projection], axis=1))
    in_w = gather_shards(in_proj)
    mixer_w = gather_shards(mixer_out)
    attn_w = gather_shards(attn_out)
    gate_up_w = gather_shards(gate_up)
    down_w = gather_shards(down_proj)
    query_w = attn_pair_w[:, : QUERY_HEADS * HEAD_SIZE]
    keyval_w = attn_pair_w[:, QUERY_HEADS * HEAD_SIZE :]

    lengths = doc_lengths[0]
    doc_count = lengths.shape[0]
    position_index = block_at * rows + jnp.arange(rows, dtype=jnp.int32)
    docs = doc_numbers(lengths, position_index)
    doc_prev = doc_numbers(lengths, position_index[:1] - 1)[0]
    log_decay = jnp.log(decay[0])
    source = tokens[0].astype(jnp.float32)
    normed, norm_pull = jax.vjp(rms_scale, source, norm_w)
    normed_b = normed.astype(jnp.bfloat16)

    turned_q = turn(
        lax.dot_general(
            query_w, normed_b, (((0,), (1,)), ((), ())), preferred_element_type=jnp.float32
        ).reshape(QUERY_HEADS, HEAD_SIZE, rows),
        position_index,
    ).astype(jnp.bfloat16)
    key_value_pair = lax.dot_general(
        keyval_w, normed_b, (((0,), (1,)), ((), ())), preferred_element_type=jnp.float32
    ).reshape(2, KEY_VALUE_HEADS, HEAD_SIZE, rows)
    keys_b = turn(key_value_pair[0], position_index).astype(jnp.bfloat16)
    values_b = key_value_pair[1].astype(jnp.bfloat16)
    pairs = lax.all_gather(
        jnp.concatenate([keys_b, values_b], axis=1).transpose(0, 2, 1), "ctx"
    )

    def to_groups(array):
        return (
            array.reshape(KEY_VALUE_HEADS, heads_per_group, HEAD_SIZE, 2, width)
            .transpose(3, 0, 2, 1, 4)
            .reshape(2, KEY_VALUE_HEADS, HEAD_SIZE, heads_per_group * width)
        )

    def from_groups(array):
        return (
            array.reshape(2, KEY_VALUE_HEADS, HEAD_SIZE, heads_per_group, width)
            .transpose(1, 3, 2, 0, 4)
            .reshape(QUERY_HEADS * HEAD_SIZE, rows)
        )

    def balance(array):
        return jnp.stack([array[0], swap_mirrored(array[1])])

    query_x = balance(to_groups(turned_q) * jnp.asarray(scale, jnp.bfloat16))
    mirrored = count - 1 - block_at
    group_blocks = jnp.stack([block_at, mirrored]).astype(jnp.int32)
    group_positions = jnp.stack(
        [
            block_at * rows + jnp.arange(width, dtype=jnp.int32),
            mirrored * rows + width + jnp.arange(width, dtype=jnp.int32),
        ]
    )
    group_docs = jnp.stack([doc_numbers(lengths, group_positions[at]) for at in range(2)])
    key_docs = doc_numbers(lengths, jnp.arange(sequence_total, dtype=jnp.int32))
    lane = jnp.arange(128)[None, :]
    key_side = ((key_docs[:, None] == lane) | ((lane >= 8) & (lane < 11))).astype(jnp.bfloat16)
    doc_rows = jnp.where(
        jnp.arange(doc_count)[None, :, None] == group_docs[:, None, :], 0.0, mask_fill_value
    ).astype(jnp.bfloat16)
    doc_rows = jnp.tile(doc_rows, (1, 1, heads_per_group))[:, None]
    doc_rows = jnp.broadcast_to(doc_rows, (2, KEY_VALUE_HEADS) + doc_rows.shape[2:])

    def side_rows(first, extra):
        first = jnp.pad(first, ((0, 0), (0, 0), (0, 8 - first.shape[2]), (0, 0)))
        if extra is None:
            return jnp.pad(first, ((0, 0), (0, 0), (0, 8), (0, 0)))
        extra = jnp.concatenate(split_three(-extra), axis=2)
        return jnp.concatenate(
            [first, jnp.pad(extra, ((0, 0), (0, 0), (0, 5), (0, 0)))], axis=2
        )

    projected = mixed_dot(normed_b, in_w)
    gate_z = projected[:, :DSSM]
    pre_b = projected[:, DSSM:].astype(jnp.bfloat16)
    rim = from_behind(pre_b[rows - (KW - 1) :], "ctx", 1)
    extended = jnp.concatenate([rim, pre_b], axis=0).astype(jnp.float32)
    taps = jnp.stack(
        [
            (doc_numbers(lengths, position_index - (KW - 1) + tap) == docs).astype(jnp.float32)
            for tap in range(KW)
        ]
    )
    conv_f, conv_pull = jax.vjp(partial(conv_local, taps), extended, conv_w, conv_b)
    conv_b16 = conv_f.astype(jnp.bfloat16)
    order = jnp.arange(rows)
    running = jnp.dot(
        log_decay, (order[:, None] <= order[None, :]).astype(jnp.float32), precision=highest
    )
    entry = jnp.where((docs == doc_prev)[None, :], jnp.exp(running), 0.0)
    tail = jnp.where((docs == docs[-1])[None, :], jnp.exp(running[:, -1:] - running), 0.0)
    carry_gain = jnp.where(docs[-1] == doc_prev, jnp.exp(running[:, -1]), 0.0)

    def columns(array):
        return array.reshape(HM // 2, 2, rows).transpose(0, 2, 1)

    running_rows = running.reshape(HM // 2, 2, rows)
    running_columns, entry_columns, tail_columns = columns(running), columns(entry), columns(tail)
    skip_wide = jnp.repeat(skip_w, PM).reshape(HM // 2, 1, 2 * PM)
    docs_column, docs_row = docs[:, None], docs[None, :]
    fresh = state_outer(DSSM // NS)(tail_columns, conv_b16, conv_b16)
    gain_rows = jnp.pad(jnp.stack(split_three(carry_gain)), ((0, 13), (0, NS - HM)))
    collected = lax.all_gather(jnp.concatenate([fresh, gain_rows], axis=0), "ctx")
    gains = jnp.sum(collected[:, DSSM : DSSM + 3, :HM].astype(jnp.float32), axis=1)
    state_in = chain(collected[:, :DSSM], gains, False)

    doc_side = side_rows(doc_rows, None)
    heads_x, log_x = attend_forward(group_blocks, pairs, key_side, query_x, doc_side)
    heads_t = from_groups(balance(heads_x.astype(jnp.bfloat16)))

    mixed = mixer_forward(
        skip_wide,
        conv_b16,
        conv_b16,
        conv_b16,
        running_columns,
        running_rows,
        entry_columns,
        docs_column,
        docs_row,
        state_in,
    )
    gated, gate_pull = jax.vjp(gate_norm, mixed, gate_z, mixer_g)
    gated_b = gated.astype(jnp.bfloat16)
    mamba = mixed_dot(gated_b, mixer_w)
    attn = lax.dot_general(
        heads_t, attn_w, (((0,), (0,)), ((), ())), preferred_element_type=jnp.float32
    )
    middle = source + attn + mamba
    normed2, ffn_pull = jax.vjp(rms_scale, middle, ffn_g)
    normed2_b = normed2.astype(jnp.bfloat16)
    gate_up_v = mixed_dot(normed2_b, gate_up_w)
    activated, act_pull = jax.vjp(swiglu, gate_up_v)
    activated_b = activated.astype(jnp.bfloat16)
    layer_out = (middle + mixed_dot(activated_b, down_w)).astype(jnp.bfloat16)

    out_low = cotangent[0]
    down_share = ctx_sum(weight_grad(activated_b, out_low))
    (gate_up_grad_v,) = act_pull(nt_dot(out_low, down_w))
    gate_up_low = gate_up_grad_v.astype(jnp.bfloat16)
    gate_up_share = ctx_sum(weight_grad(normed2_b, gate_up_low))
    middle_norm_grad, ffn_gain_grad = ffn_pull(nt_dot(gate_up_low, gate_up_w))
    middle_grad = out_low.astype(jnp.float32) + middle_norm_grad
    middle_low = middle_grad.astype(jnp.bfloat16)
    heads_low = nt_dot(attn_w, middle_low).astype(jnp.bfloat16)
    grad_x = balance(to_groups(heads_low))
    gated_grad = nt_dot(middle_low, mixer_w)
    mixed_grad, gate_z_grad, mixer_gain_grad = gate_pull(gated_grad)
    upward = state_outer(DSSM // NS + 1)(entry_columns, mixed_grad.astype(jnp.bfloat16), conv_b16)
    state_out_grad = chain(lax.all_gather(upward, "ctx"), gains, True)
    attn_share = ctx_sum(weight_grad(heads_t, middle_low, 0))
    mixer_share = ctx_sum(weight_grad(gated_b, middle_low))
    gate_z_low = gate_z_grad.astype(jnp.bfloat16)
    in_share_z = ctx_sum(weight_grad(normed_b, gate_z_low))

    delta = jnp.sum(grad_x.astype(jnp.float32) * heads_x, axis=2, keepdims=True)
    query_grad_x, pairs_grad = attend_backward(
        group_blocks,
        pairs,
        key_side,
        query_x,
        side_rows(doc_rows, log_x),
        grad_x,
        side_rows(jnp.zeros_like(doc_rows), delta),
    )
    pair_grad = (
        lax.psum_scatter(pairs_grad, "ctx", scatter_dimension=0)
        .astype(jnp.float32)
        .transpose(0, 2, 1)
    )
    query_back = jnp.stack(
        [
            turn(
                query_grad_x[at].reshape(KEY_VALUE_HEADS, HEAD_SIZE, heads_per_group * width),
                -jnp.tile(group_positions[at], heads_per_group),
            )
            for at in range(2)
        ]
    )
    query_low = from_groups(balance((query_back * scale).astype(jnp.bfloat16)))

    conv_grad, skip_parts = mixer_backward(
        skip_wide,
        conv_b16,
        conv_b16,
        conv_b16,
        running_columns,
        running_rows,
        entry_columns,
        tail_columns,
        docs_column,
        docs_row,
        state_in,
        state_out_grad,
        mixed_grad,
    )
    skip_grad = jnp.sum(skip_parts.reshape(HM, PM), axis=1)
    extended_grad, conv_weight_grad, conv_bias_grad = conv_pull(conv_grad)
    from_above = from_behind(extended_grad[: KW - 1], "ctx", -1)
    pre_grad = extended_grad[KW - 1 :] + jnp.pad(from_above, ((rows - (KW - 1), 0), (0, 0)))
    pre_low = pre_grad.astype(jnp.bfloat16)
    in_share_pre = ctx_sum(weight_grad(normed_b, pre_low))
    projected_low = jnp.concatenate([gate_z_low, pre_low], axis=1)
    normed_grad = nt_dot(projected_low, in_w)

    keys_low = turn(pair_grad[:, :HEAD_SIZE], -position_index)
    keyval_low = jnp.concatenate(
        [
            keys_low.reshape(KEY_VALUE_HEADS * HEAD_SIZE, rows),
            pair_grad[:, HEAD_SIZE:].reshape(KEY_VALUE_HEADS * HEAD_SIZE, rows),
        ],
        axis=0,
    ).astype(jnp.bfloat16)
    attn_pair_low = jnp.concatenate([query_low, keyval_low], axis=0).T
    attn_pair_share = ctx_sum(weight_grad(normed_b, attn_pair_low))
    normed_grad = normed_grad + nt_dot(attn_pair_low, attn_pair_w)
    source_grad, norm_grad = norm_pull(normed_grad)
    tokens_grad = (middle_grad + source_grad)[None]

    small_grad = pack_small(
        norm_grad, conv_weight_grad, conv_bias_grad, skip_grad, mixer_gain_grad, ffn_gain_grad, shards
    )
    small_share = ctx_sum(shard_sum(*shard_pieces(small_grad, 0)))
    norm_share, conv_w_share, conv_b_share, skip_share, mixer_g_share, ffn_share = unpack_small(
        small_share, model, channels, HM, 1
    )
    return (
        layer_out[None],
        tokens_grad,
        norm_share,
        jnp.concatenate([in_share_z, in_share_pre], axis=1),
        conv_w_share,
        conv_b_share,
        skip_share,
        mixer_g_share,
        mixer_share,
        attn_pair_share[:, : QUERY_HEADS * HEAD_SIZE],
        attn_pair_share[:, QUERY_HEADS * HEAD_SIZE :],
        attn_share,
        ffn_share,
        gate_up_share,
        down_share,
    )


def solution(mesh):
    in_specs = (
        P("wshard", "ctx", None),
        P("wshard", "ctx", None),
        P("wshard", None),
        P("wshard", None, "ctx"),
        P("wshard"),
        P("wshard", None),
        P(None, "wshard"),
        P("wshard"),
        P("wshard"),
        P("wshard"),
        P("wshard", None),
        P("wshard", None),
        P("wshard", None),
        P("wshard", None),
        P("wshard"),
        P("wshard", None),
        P("wshard", None),
    )
    out_specs = (
        P("wshard", "ctx", None),
        P("wshard", "ctx", None),
        P("wshard"),
        P("wshard", None),
        P(None, "wshard"),
        P("wshard"),
        P("wshard"),
        P("wshard"),
        P("wshard", None),
        P("wshard", None),
        P("wshard", None),
        P("wshard", None),
        P("wshard"),
        P("wshard", None),
        P("wshard", None),
    )
    return jax.shard_map(
        per_device, mesh=mesh, in_specs=in_specs, out_specs=out_specs, check_vma=False
    )
```

```python
from functools import partial

import jax
import jax.numpy as jnp
from jax import lax
from jax.experimental import pallas as pl
from jax.experimental.pallas import tpu as pltpu
from jax.sharding import PartitionSpec as P

FF = 2048
QUERY_HEADS = 8
KEY_VALUE_HEADS = 2
HEAD_SIZE = 64
HM = 24
PM = 64
NS = 128
KW = 4
DSSM = 1536

eps_norm = 1e-05
rope_base = 100000000000.0
mask_fill_value = -1e30
highest = lax.Precision.HIGHEST
MESH_AXES = ("ctx", "wshard")


def exchange(block, ctx_flip, shard_flip):
    blocks, shards = lax.axis_size("ctx"), lax.axis_size("wshard")
    route = [
        (c * shards + w, (c ^ ctx_flip) * shards + (w ^ shard_flip))
        for c in range(blocks)
        for w in range(shards)
    ]
    return lax.ppermute(block, MESH_AXES, route)


def from_behind(block, axis, distance):
    devices = range(lax.axis_size(axis))
    route = [(i - distance, i) for i in devices if i - distance in devices]
    return lax.ppermute(block, axis, route)


def swap_mirrored(block):
    count = lax.axis_size("ctx")
    return lax.ppermute(block, "ctx", [(i, count - 1 - i) for i in range(count)])


def assemble_body(routes, at_ref, *refs):
    pieces, wholes, semaphores = refs[: len(routes)], refs[len(routes) : -1], refs[-1]
    copies = []
    for piece, route in zip(pieces, routes):
        for target, source, size in route:
            start = pl.multiple_of(at_ref[len(copies)], 16)
            copy = pltpu.make_async_copy(
                piece.at[pl.ds(source, size), :],
                wholes[target].at[pl.ds(start, size), :],
                semaphores.at[len(copies)],
            )
            copy.start()
            copies.append(copy)
    for copy in copies:
        copy.wait()


def assemble(pieces, sizes):
    routes, starts = [], []
    for piece, places in pieces:
        route, source = [], 0
        for target, start, size in places:
            route.append((target, source, size))
            starts.append(start)
            source += size
        routes.append(route)
    columns, kind = pieces[0][0].shape[1], pieces[0][0].dtype
    anywhere = pl.BlockSpec(memory_space=pl.ANY)
    return pl.pallas_call(
        partial(assemble_body, routes),
        in_specs=[pl.BlockSpec(memory_space=pltpu.SMEM)] + [anywhere] * len(pieces),
        out_specs=[anywhere] * len(sizes),
        out_shape=[jax.ShapeDtypeStruct((size, columns), kind) for size in sizes],
        scratch_shapes=[pltpu.SemaphoreType.DMA((len(starts),))],
        cost_estimate=pl.CostEstimate(
            flops=0, bytes_accessed=4 * columns * sum(sizes), transcendentals=0
        ),
        name="assemble",
    )(jnp.stack([jnp.asarray(start, jnp.int32) for start in starts]), *[p for p, _ in pieces])


def gather_first(shard):
    rows = shard.shape[0]
    relayed = rows * 5 // 256 * 16
    w = lax.axis_index("wshard")
    side = lax.axis_index("ctx") % 2
    across = exchange(lax.dynamic_slice_in_dim(shard, side * relayed, relayed, 0), 0, 2)
    across_direct = exchange(shard[2 * relayed :], 0, 2)
    beside = exchange(shard, 0, 1)
    across_relayed = exchange(across, 1, 0)
    parts = [
        (across, side * relayed, relayed),
        (across_direct, 2 * relayed, rows - 2 * relayed),
        (across_relayed, (1 - side) * relayed, relayed),
    ]
    pieces = [(shard, [(0, w * rows, rows)]), (beside, [(0, (w ^ 1) * rows, rows)])]
    for part, start, size in parts:
        pieces.append((part, [(0, (w ^ 2) * rows + start, size)]))
        pieces.append((exchange(part, 0, 1), [(0, (w ^ 3) * rows + start, size)]))
    return assemble(pieces, [4 * rows])[0], across_direct


def gather_shards(stacked, sizes, after):
    stacked, _ = lax.optimization_barrier((stacked, after))
    w = lax.axis_index("wshard")
    across = exchange(stacked, 0, 2)
    parts = [(stacked, 0), (exchange(stacked, 0, 1), 1), (across, 2), (exchange(across, 0, 1), 3)]
    return assemble(
        [
            (part, [(at, (w ^ flip) * size, size) for at, size in enumerate(sizes)])
            for part, flip in parts
        ],
        [4 * size for size in sizes],
    )


def add_low(first, *others):
    total = first.astype(jnp.float32)
    for other in others:
        total = total + other.astype(jnp.float32)
    return total.astype(jnp.bfloat16)


def lay_side_by_side(blocks, rows):
    parts = []
    for block in blocks:
        for start in range(0, block.shape[0], rows):
            part = block[start : start + rows]
            parts.append(jnp.pad(part, ((0, rows - part.shape[0]), (0, 0))))
    return jnp.concatenate(parts, axis=1)


def take_apart(array, shapes):
    rows, start, blocks = array.shape[0], 0, []
    for height, columns in shapes:
        parts = []
        for _ in range(0, height, rows):
            parts.append(array[: min(height, rows), start : start + columns])
            start += columns
        blocks.append(parts[0] if len(parts) == 1 else jnp.concatenate(parts, axis=0))
    return blocks


def ctx_sum(blocks, rows, turn_at):
    side = lax.axis_index("ctx") % 2
    count = lax.axis_size("ctx")
    whole = lay_side_by_side(blocks, rows)
    half = rows // 2
    got = exchange(lax.dynamic_slice_in_dim(whole, (1 - side) * half, half, 0), 1, 0)
    mine = add_low(lax.dynamic_slice_in_dim(whole, side * half, half, 0), got)
    lines = [list(range(start, count, 2)) for start in range(2)]
    lines = [lines, lines[::-1], [line[::-1] for line in lines]][turn_at]
    mine = lax.psum(mine, "ctx", axis_index_groups=lines)
    got = exchange(mine, 1, 0)
    whole = jnp.where(
        side == 0, jnp.concatenate([mine, got], axis=0), jnp.concatenate([got, mine], axis=0)
    ).astype(jnp.float32)
    return take_apart(whole, [block.shape for block in blocks])


def shard_pieces(array, axis):
    w = lax.axis_index("wshard")
    size = array.shape[axis] // 4

    def piece(flip):
        return lax.dynamic_slice_in_dim(array, (w ^ flip) * size, size, axis)

    return jnp.concatenate([piece(1), piece(3)], axis=axis), piece(2), piece(0)


def shard_sum(beside, across, own):
    rows = own.shape[0]
    got = exchange(beside.astype(jnp.bfloat16), 0, 1)
    got_across = exchange(add_low(across, got[rows:]), 0, 2)
    return add_low(own, got[:rows], got_across)


def split_products(left, right, axis=1):
    return [
        lax.dot_general(
            piece, right, (((1 - axis,), (0,)), ((), ())), preferred_element_type=jnp.float32
        )
        for piece in shard_pieces(left, axis)
    ]


def weight_grad(left, right):
    return shard_sum(*split_products(left, right))


def mixed_dot(left, right):
    return jnp.dot(left, right, preferred_element_type=jnp.float32)


def rms_scale(value, gain):
    return value * lax.rsqrt(jnp.mean(value * value, axis=-1, keepdims=True) + eps_norm) * gain


def doc_numbers(lengths, position_index):
    ends = jnp.cumsum(lengths)[:-1]
    tally_count = jnp.sum((position_index[:, None] >= ends[None, :]).astype(jnp.int32), axis=1)
    return jnp.where(position_index >= 0, tally_count, -1)


def turn(value, position_index):
    half = value.shape[-2] // 2
    freq = rope_base ** (-jnp.arange(half, dtype=jnp.float32) / half)
    angle = freq[:, None] * position_index.astype(jnp.float32)[None, :]
    cosine = jnp.cos(angle)
    sine = jnp.sin(angle)
    first = value[..., :half, :]
    second = value[..., half:, :]
    return jnp.concatenate(
        [first * cosine - second * sine, second * cosine + first * sine], axis=-2
    )


def conv_local(taps, extended, weight, bias):
    tally_count = extended.shape[0] - (KW - 1)
    total = bias[None, :]
    for tap in range(KW):
        total = (
            total + weight[tap][None, :] * extended[tap : tap + tally_count] * taps[tap][:, None]
        )
    return jax.nn.silu(total)


def gate_norm(mixed, gate_z, gain):
    return rms_scale(mixed * jax.nn.silu(gate_z), gain)


def swiglu(gate_up_v):
    return jax.nn.silu(gate_up_v[:, :FF]) * gate_up_v[:, FF:]


def split_three(value):
    high = value.astype(jnp.bfloat16)
    rest = value - high.astype(jnp.float32)
    middle = rest.astype(jnp.bfloat16)
    low = (rest - middle.astype(jnp.float32)).astype(jnp.bfloat16)
    return [high, middle, low]


def nt_dot(left, right):
    return lax.dot_general(left, right, (((1,), (1,)), ((), ())), preferred_element_type=jnp.float32)


def causal_tile(scores, group, width):
    rows = lax.broadcasted_iota(jnp.int32, scores.shape, 0)
    columns = lax.broadcasted_iota(jnp.int32, scores.shape, 1)
    return jnp.where(rows <= lax.rem(columns, width) + group * width, scores, mask_fill_value)


def load_extended(extended, lower, value_ref, side_ref):
    for group in range(2):
        extended[group] = jnp.zeros(extended.shape[1:], extended.dtype)
        extended[group, lower : lower + HEAD_SIZE, :] = value_ref[group, 0]
        extended[group, 128:144, :] = side_ref[group, 0]


def attend_forward_body(
    width, blocks, pair_ref, side_ref, query_ref, query_side_ref, heads_ref, log_ref, query_x, peak, total
):
    step = pl.program_id(1)

    @pl.when(step == 0)
    def start():
        load_extended(query_x, 0, query_ref, query_side_ref)
        peak[...] = jnp.full(peak.shape, mask_fill_value, jnp.float32)
        total[...] = jnp.zeros(total.shape, jnp.float32)

    @pl.when(step <= jnp.maximum(blocks[0], blocks[1]))
    def work():
        keys = jnp.concatenate([pair_ref[0, 0], side_ref[...]], axis=1)
        values = keys.T[HEAD_SIZE:144]

        def tile(group, masked):
            scores = mixed_dot(keys, query_x[group])
            if masked:
                scores = causal_tile(scores, group, width)
            old = peak[group]
            new = jnp.maximum(old, jnp.max(scores, axis=0, keepdims=True))
            probs = jnp.exp(scores - new)
            total[group] = total[group] * jnp.exp(old - new) + mixed_dot(
                values, probs.astype(jnp.bfloat16)
            )
            peak[group] = new

        for group in range(2):
            pl.when(step < blocks[group])(partial(tile, group, False))
            pl.when(step == blocks[group])(partial(tile, group, True))

    @pl.when(step == pl.num_programs(1) - 1)
    def finish():
        for group in range(2):
            weight = total[group, HEAD_SIZE + 8 : HEAD_SIZE + 9, :]
            heads_ref[group, 0] = total[group, :HEAD_SIZE, :] / weight
            log_ref[group, 0] = peak[group] + jnp.log(weight)


def attend_backward_body(
    width,
    blocks,
    pair_ref,
    side_ref,
    query_ref,
    query_side_ref,
    grad_ref,
    grad_side_ref,
    query_grad_ref,
    pair_grad_ref,
    query_x,
    grad_x,
    pair_acc,
):
    step = pl.program_id(1)

    @pl.when(step == 0)
    def start():
        load_extended(query_x, 0, query_ref, query_side_ref)
        load_extended(grad_x, HEAD_SIZE, grad_ref, grad_side_ref)
        query_grad_ref[...] = jnp.zeros(query_grad_ref.shape, jnp.float32)

    pair_acc[...] = jnp.zeros(pair_acc.shape, jnp.float32)

    @pl.when(step <= jnp.maximum(blocks[0], blocks[1]))
    def work():
        pair = pair_ref[0, 0]
        keys = jnp.concatenate([pair, side_ref[...]], axis=1)
        turned = pair.T[:HEAD_SIZE]

        def tile(group, masked):
            scores = mixed_dot(keys, query_x[group])
            if masked:
                scores = causal_tile(scores, group, width)
            probs = jnp.exp(scores)
            low = (probs * mixed_dot(keys, grad_x[group])).astype(jnp.bfloat16)
            pair_acc[...] += nt_dot(low, query_x[group, :128, :]) + nt_dot(
                probs.astype(jnp.bfloat16), grad_x[group, :128, :]
            )
            query_grad_ref[group, 0] += mixed_dot(turned, low)

        for group in range(2):
            pl.when(step < blocks[group])(partial(tile, group, False))
            pl.when(step == blocks[group])(partial(tile, group, True))

    pair_grad_ref[0, 0] = pair_acc[...].astype(jnp.bfloat16)


def attention_calls(rows, count):
    width = rows // 2
    span = width * (QUERY_HEADS // KEY_VALUE_HEADS)

    def last(blocks):
        return jnp.maximum(blocks[0], blocks[1])

    pair_spec = pl.BlockSpec(
        (1, 1, rows, 128), lambda g, k, blocks: (jnp.minimum(k, last(blocks)), g, 0, 0)
    )
    side_spec = pl.BlockSpec((rows, 128), lambda g, k, blocks: (jnp.minimum(k, last(blocks)), 0))

    def per_group(height):
        return pl.BlockSpec((2, 1, height, span), lambda g, k, blocks: (0, g, 0, 0))

    elements = KEY_VALUE_HEADS * (count + 1) * rows * span
    params = pltpu.CompilerParams(
        dimension_semantics=("arbitrary", "arbitrary"), vmem_limit_bytes=48 * 1024 * 1024
    )
    forward = pl.pallas_call(
        partial(attend_forward_body, width),
        grid_spec=pltpu.PrefetchScalarGridSpec(
            num_scalar_prefetch=1,
            grid=(KEY_VALUE_HEADS, count),
            in_specs=[pair_spec, side_spec, per_group(HEAD_SIZE), per_group(16)],
            out_specs=[per_group(HEAD_SIZE), per_group(1)],
            scratch_shapes=[
                pltpu.VMEM((2, 256, span), jnp.bfloat16),
                pltpu.VMEM((2, 1, span), jnp.float32),
                pltpu.VMEM((2, 144 - HEAD_SIZE, span), jnp.float32),
            ],
        ),
        out_shape=[
            jax.ShapeDtypeStruct((2, KEY_VALUE_HEADS, HEAD_SIZE, span), jnp.float32),
            jax.ShapeDtypeStruct((2, KEY_VALUE_HEADS, 1, span), jnp.float32),
        ],
        compiler_params=params,
        cost_estimate=pl.CostEstimate(
            flops=elements * 512, bytes_accessed=8 * rows * 1024 * count, transcendentals=elements
        ),
        name="attend_forward",
    )
    backward = pl.pallas_call(
        partial(attend_backward_body, width),
        grid_spec=pltpu.PrefetchScalarGridSpec(
            num_scalar_prefetch=1,
            grid=(KEY_VALUE_HEADS, count),
            in_specs=[
                pair_spec,
                side_spec,
                per_group(HEAD_SIZE),
                per_group(16),
                per_group(HEAD_SIZE),
                per_group(16),
            ],
            out_specs=[
                per_group(HEAD_SIZE),
                pl.BlockSpec((1, 1, rows, 128), lambda g, k, blocks: (k, g, 0, 0)),
            ],
            scratch_shapes=[
                pltpu.VMEM((2, 256, span), jnp.bfloat16),
                pltpu.VMEM((2, 256, span), jnp.bfloat16),
                pltpu.VMEM((rows, 128), jnp.float32),
            ],
        ),
        out_shape=[
            jax.ShapeDtypeStruct((2, KEY_VALUE_HEADS, HEAD_SIZE, span), jnp.float32),
            jax.ShapeDtypeStruct((count, KEY_VALUE_HEADS, rows, 128), jnp.bfloat16),
        ],
        compiler_params=params,
        cost_estimate=pl.CostEstimate(
            flops=elements * 1280, bytes_accessed=8 * rows * 1024 * count, transcendentals=elements
        ),
        name="attend_backward",
    )
    return forward, backward


def pick(pair):
    lane = lax.broadcasted_iota(jnp.int32, (pair.shape[0], 2 * PM), 1)
    return jnp.where(lane < PM, pair[:, 0:1], pair[:, 1:2])


def outer_body(rows_ref, left_ref, right_ref, out_ref):
    for at in range(rows_ref.shape[0]):
        scale = pick(rows_ref[at])
        left = left_ref[:, at * 128 : (at + 1) * 128].astype(jnp.float32) * scale
        out_ref[at * 128 : (at + 1) * 128, :] = lax.dot_general(
            left.astype(jnp.bfloat16),
            right_ref[...],
            (((0,), (0,)), ((), ())),
            preferred_element_type=jnp.float32,
        ).astype(out_ref.dtype)


def mixed_body(
    skip_ref, x_ref, b_ref, c_ref, column_ref, row_ref, entry_ref, docs_column, docs_row, state_ref, out_ref, fill, products
):
    rows = x_ref.shape[0]
    half = rows // 2

    @pl.when(pl.program_id(0) == 0)
    def start():
        at = lax.broadcasted_iota(jnp.int32, (rows, rows), 0)
        source = lax.broadcasted_iota(jnp.int32, (rows, rows), 1)
        same = (at >= source) & (docs_column[...] == docs_row[...])
        fill[...] = jnp.where(same, 0.0, mask_fill_value)
        products[...] = nt_dot(c_ref[...], b_ref[...])

    x = x_ref[...]
    lane = lax.broadcasted_iota(jnp.int32, (half, 2 * PM), 1)
    for block in range(2):
        here = slice(block * half, (block + 1) * half)
        width = (block + 1) * half
        parts = []
        for head in range(2):
            decay = jnp.exp(
                (column_ref[0, here, head : head + 1] - row_ref[0, head : head + 1, :width])
                + fill[here, :width]
            )
            weights = (products[here, :width] * decay).astype(jnp.bfloat16)
            parts.append(mixed_dot(weights, x[:width]))
        local = jnp.where(lane < PM, parts[0], parts[1])
        inner = nt_dot(c_ref[here, :], state_ref[...].astype(jnp.bfloat16))
        out_ref[here, :] = (
            local + inner * pick(entry_ref[0, here, :]) + x[here].astype(jnp.float32) * skip_ref[0]
        )


def mixed_grad_body(
    skip_ref,
    x_ref,
    b_ref,
    c_ref,
    column_ref,
    row_ref,
    entry_ref,
    tail_ref,
    docs_column,
    docs_row,
    state_ref,
    state_grad_ref,
    grad_ref,
    out_ref,
    skip_grad_ref,
    fill,
    products,
    scores,
    b_grad,
    c_grad,
):
    rows = x_ref.shape[0]
    half = rows // 2
    step = pl.program_id(0)
    pairs = HM // 2

    @pl.when(step == 0)
    def start():
        source = lax.broadcasted_iota(jnp.int32, (rows, rows), 0)
        at = lax.broadcasted_iota(jnp.int32, (rows, rows), 1)
        same = (at >= source) & (docs_column[...] == docs_row[...])
        fill[...] = jnp.where(same, 0.0, mask_fill_value)
        products[...] = nt_dot(b_ref[...], c_ref[...])
        scores[...] = jnp.zeros(scores.shape, jnp.float32)
        b_grad[...] = jnp.zeros(b_grad.shape, jnp.float32)
        c_grad[...] = jnp.zeros(c_grad.shape, jnp.float32)

    @pl.when(step < pairs)
    def work():
        x = x_ref[...]
        x_f = x.astype(jnp.float32)
        grad = grad_ref[...]
        low = grad.astype(jnp.bfloat16)
        lane = lax.broadcasted_iota(jnp.int32, (half, 2 * PM), 1)
        lane_all = lax.broadcasted_iota(jnp.int32, (rows, 2 * PM), 1)
        skip_grad_ref[0] = jnp.sum(grad * x_f, axis=0, keepdims=True)
        state_grad = state_grad_ref[...].astype(jnp.bfloat16)
        tail = pick(tail_ref[0])
        b_grad[...] += mixed_dot((x_f * tail).astype(jnp.bfloat16), state_grad)
        entered = (low.astype(jnp.float32) * pick(entry_ref[0])).astype(jnp.bfloat16)
        c_grad[...] += mixed_dot(entered, state_ref[...].astype(jnp.bfloat16))
        passed = nt_dot(b_ref[...], state_grad) * tail + grad * skip_ref[0]
        chosen = [
            jnp.where((lane_all < PM) == (head == 0), x_f, 0.0).astype(jnp.bfloat16)
            for head in range(2)
        ]
        for block in range(2):
            here = slice(block * half, (block + 1) * half)
            start_at = block * half
            parts = []
            for head in range(2):
                decay = jnp.exp(
                    (row_ref[0, head : head + 1, start_at:] - column_ref[0, here, head : head + 1])
                    + fill[here, start_at:]
                )
                weights = (products[here, start_at:] * decay).astype(jnp.bfloat16)
                parts.append(mixed_dot(weights, low[start_at:]))
                scores[here, start_at:] += nt_dot(chosen[head][here], low[start_at:]) * decay
            out_ref[here, :] = jnp.where(lane < PM, parts[0], parts[1]) + passed[here]

    @pl.when(step == pairs)
    def give_b():
        out_ref[...] = b_grad[...] + mixed_dot(scores[...].astype(jnp.bfloat16), c_ref[...])

    @pl.when(step == pairs + 1)
    def give_c():
        out_ref[...] = c_grad[...] + lax.dot_general(
            scores[...].astype(jnp.bfloat16),
            b_ref[...],
            (((0,), (0,)), ((), ())),
            preferred_element_type=jnp.float32,
        )


def mixer_calls(rows):
    pairs = HM // 2
    wide = 2 * PM
    params = pltpu.CompilerParams(
        dimension_semantics=("arbitrary",), vmem_limit_bytes=48 * 1024 * 1024
    )

    def capped(p):
        return jnp.minimum(p, pairs - 1)

    def outer(right_at):
        each = 2
        return pl.pallas_call(
            outer_body,
            grid=(pairs // each,),
            in_specs=[
                pl.BlockSpec((each, rows, 2), lambda p: (p, 0, 0)),
                pl.BlockSpec((rows, each * wide), lambda p: (0, p)),
                pl.BlockSpec((rows, NS), lambda p: (0, right_at)),
            ],
            out_specs=pl.BlockSpec((each * wide, NS), lambda p: (p, 0)),
            out_shape=jax.ShapeDtypeStruct((DSSM, NS), jnp.bfloat16),
            compiler_params=params,
            cost_estimate=pl.CostEstimate(
                flops=2 * rows * DSSM * NS, bytes_accessed=6 * rows * DSSM, transcendentals=0
            ),
            name="state_outer",
        )

    x_spec = pl.BlockSpec((rows, wide), lambda p: (0, capped(p)))
    b_spec = pl.BlockSpec((rows, NS), lambda p: (0, DSSM // NS))
    c_spec = pl.BlockSpec((rows, NS), lambda p: (0, DSSM // NS + 1))
    column_spec = pl.BlockSpec((1, rows, 2), lambda p: (capped(p), 0, 0))
    row_spec = pl.BlockSpec((1, 2, rows), lambda p: (capped(p), 0, 0))
    skip_spec = pl.BlockSpec((1, 1, wide), lambda p: (capped(p), 0, 0))
    state_spec = pl.BlockSpec((wide, NS), lambda p: (capped(p), 0))
    docs_specs = [pl.BlockSpec((rows, 1), lambda p: (0, 0)), pl.BlockSpec((1, rows), lambda p: (0, 0))]
    square = pltpu.VMEM((rows, rows), jnp.float32)
    narrow = pltpu.VMEM((rows, NS), jnp.float32)
    forward = pl.pallas_call(
        mixed_body,
        grid=(pairs,),
        in_specs=[skip_spec, x_spec, b_spec, c_spec, column_spec, row_spec, column_spec]
        + docs_specs
        + [state_spec],
        out_specs=pl.BlockSpec((rows, wide), lambda p: (0, p)),
        out_shape=jax.ShapeDtypeStruct((rows, DSSM), jnp.float32),
        scratch_shapes=[square, square],
        compiler_params=params,
        cost_estimate=pl.CostEstimate(
            flops=4 * rows * rows * DSSM, bytes_accessed=8 * rows * DSSM, transcendentals=HM * rows * rows
        ),
        name="mixer_forward",
    )
    backward = pl.pallas_call(
        mixed_grad_body,
        grid=(pairs + 2,),
        in_specs=[skip_spec, x_spec, b_spec, c_spec, column_spec, row_spec, column_spec, column_spec]
        + docs_specs
        + [state_spec, state_spec, x_spec],
        out_specs=[
            pl.BlockSpec((rows, wide), lambda p: (0, p)),
            pl.BlockSpec((1, 1, wide), lambda p: (capped(p), 0, 0)),
        ],
        out_shape=[
            jax.ShapeDtypeStruct((rows, DSSM + 2 * NS), jnp.float32),
            jax.ShapeDtypeStruct((pairs, 1, wide), jnp.float32),
        ],
        scratch_shapes=[square, square, square, narrow, narrow],
        compiler_params=params,
        cost_estimate=pl.CostEstimate(
            flops=8 * rows * rows * DSSM, bytes_accessed=12 * rows * DSSM, transcendentals=HM * rows * rows
        ),
        name="mixer_backward",
    )
    return outer, forward, backward


def chain(parts, gains, reverse):
    count, position = lax.axis_size("ctx"), lax.axis_index("ctx")
    factor = jnp.ones((HM,), jnp.float32)
    total = jnp.zeros((HM, PM, NS), jnp.float32)
    for at in range(count) if reverse else reversed(range(count)):
        reached = at > position if reverse else at < position
        part = parts[at].reshape(HM, PM, NS).astype(jnp.float32)
        total = total + jnp.where(reached, factor, 0.0)[:, None, None] * part
        factor = factor * jnp.where(reached, gains[at], 1.0)
    return total.reshape(DSSM, NS)


def pack_small(norm, conv_weight, conv_bias, skip, mixer, ffn, shards):
    pieces = [
        norm.reshape(shards, -1),
        conv_weight.reshape(KW, shards, -1).transpose(1, 0, 2).reshape(shards, -1),
        conv_bias.reshape(shards, -1),
        mixer.reshape(shards, -1),
        ffn.reshape(shards, -1),
        skip.reshape(shards, -1),
    ]
    packed = jnp.concatenate(pieces, axis=1)
    packed = jnp.pad(packed, ((0, 0), (0, 4096 - packed.shape[1])))
    return packed.reshape(shards * 32, 128)


def unpack_small(packed, model, channels, heads, shards):
    packed = packed.reshape(shards, 4096)
    sizes = [model, KW * channels, channels, DSSM, model, heads]
    parts, start = [], 0
    for size in sizes:
        width = size // 4
        parts.append(packed[:, start : start + width])
        start += width
    norm, conv_weight, conv_bias, mixer, ffn, skip = parts
    conv_weight = conv_weight.reshape(shards, KW, -1).transpose(1, 0, 2).reshape(KW, -1)
    return (
        norm.reshape(-1),
        conv_weight,
        conv_bias.reshape(-1),
        skip.reshape(-1),
        mixer.reshape(-1),
        ffn.reshape(-1),
    )


def per_device(
    tokens,
    cotangent,
    doc_lengths,
    decay,
    norm_gain,
    in_proj,
    conv_weight,
    conv_bias,
    skip_gain,
    mixer_gain,
    mixer_out,
    query_proj,
    key_value_projection,
    attn_out,
    ffn_gain,
    gate_up,
    down_proj,
):
    rows, model = tokens.shape[1:]
    width = rows // 2
    shards = lax.axis_size("wshard")
    channels = conv_bias.shape[0] * shards
    count, block_at = lax.axis_size("ctx"), lax.axis_index("ctx")
    sequence_total = rows * count
    heads_per_group = QUERY_HEADS // KEY_VALUE_HEADS
    scale = HEAD_SIZE ** (-0.5)
    attend_forward, attend_backward = attention_calls(rows, count)
    state_outer, mixer_forward, mixer_backward = mixer_calls(rows)

    small = lax.all_gather(
        pack_small(norm_gain, conv_weight, conv_bias, skip_gain, mixer_gain, ffn_gain, 1),
        "wshard",
        tiled=True,
    )
    norm_w, conv_w, conv_b, skip_w, mixer_g, ffn_g = (
        part.astype(jnp.float32) for part in unpack_small(small, model, channels, HM, shards)
    )
    first_w, arrived = gather_first(
        jnp.concatenate([in_proj, query_proj, key_value_projection], axis=1)
    )
    projected_width = in_proj.shape[1]
    in_w, attn_pair_w = first_w[:, :projected_width], first_w[:, projected_width:]
    mixer_w, attn_w, down_w = gather_shards(
        jnp.concatenate([mixer_out, attn_out, down_proj], axis=0),
        [mixer_out.shape[0], attn_out.shape[0], down_proj.shape[0]],
        arrived,
    )
    (gate_up_w,) = gather_shards(gate_up, [gate_up.shape[0]], arrived)
    query_w = attn_pair_w[:, : QUERY_HEADS * HEAD_SIZE]
    keyval_w = attn_pair_w[:, QUERY_HEADS * HEAD_SIZE :]

    lengths = doc_lengths[0]
    doc_count = lengths.shape[0]
    position_index = block_at * rows + jnp.arange(rows, dtype=jnp.int32)
    docs = doc_numbers(lengths, position_index)
    doc_prev = doc_numbers(lengths, position_index[:1] - 1)[0]
    log_decay = jnp.log(decay[0])
    source = tokens[0].astype(jnp.float32)
    normed, norm_pull = jax.vjp(rms_scale, source, norm_w)
    normed_b = normed.astype(jnp.bfloat16)

    turned_q = turn(
        lax.dot_general(
            query_w, normed_b, (((0,), (1,)), ((), ())), preferred_element_type=jnp.float32
        ).reshape(QUERY_HEADS, HEAD_SIZE, rows),
        position_index,
    ).astype(jnp.bfloat16)
    key_value_pair = lax.dot_general(
        keyval_w, normed_b, (((0,), (1,)), ((), ())), preferred_element_type=jnp.float32
    ).reshape(2, KEY_VALUE_HEADS, HEAD_SIZE, rows)
    keys_b = turn(key_value_pair[0], position_index).astype(jnp.bfloat16)
    values_b = key_value_pair[1].astype(jnp.bfloat16)
    pairs = lax.all_gather(
        jnp.concatenate([keys_b, values_b], axis=1).transpose(0, 2, 1), "ctx"
    )

    def to_groups(array):
        return (
            array.reshape(KEY_VALUE_HEADS, heads_per_group, HEAD_SIZE, 2, width)
            .transpose(3, 0, 2, 1, 4)
            .reshape(2, KEY_VALUE_HEADS, HEAD_SIZE, heads_per_group * width)
        )

    def from_groups(array):
        return (
            array.reshape(2, KEY_VALUE_HEADS, HEAD_SIZE, heads_per_group, width)
            .transpose(1, 3, 2, 0, 4)
            .reshape(QUERY_HEADS * HEAD_SIZE, rows)
        )

    def balance(array):
        return jnp.stack([array[0], swap_mirrored(array[1])])

    query_x = balance(to_groups(turned_q) * jnp.asarray(scale, jnp.bfloat16))
    mirrored = count - 1 - block_at
    group_blocks = jnp.stack([block_at, mirrored]).astype(jnp.int32)
    group_positions = jnp.stack(
        [
            block_at * rows + jnp.arange(width, dtype=jnp.int32),
            mirrored * rows + width + jnp.arange(width, dtype=jnp.int32),
        ]
    )
    group_docs = jnp.stack([doc_numbers(lengths, group_positions[at]) for at in range(2)])
    key_docs = doc_numbers(lengths, jnp.arange(sequence_total, dtype=jnp.int32))
    lane = jnp.arange(128)[None, :]
    key_side = ((key_docs[:, None] == lane) | ((lane >= 8) & (lane < 11))).astype(jnp.bfloat16)
    doc_rows = jnp.where(
        jnp.arange(doc_count)[None, :, None] == group_docs[:, None, :], 0.0, mask_fill_value
    ).astype(jnp.bfloat16)
    doc_rows = jnp.tile(doc_rows, (1, 1, heads_per_group))[:, None]
    doc_rows = jnp.broadcast_to(doc_rows, (2, KEY_VALUE_HEADS) + doc_rows.shape[2:])

    def side_rows(first, extra):
        first = jnp.pad(first, ((0, 0), (0, 0), (0, 8 - first.shape[2]), (0, 0)))
        if extra is None:
            return jnp.pad(first, ((0, 0), (0, 0), (0, 8), (0, 0)))
        extra = jnp.concatenate(split_three(-extra), axis=2)
        return jnp.concatenate(
            [first, jnp.pad(extra, ((0, 0), (0, 0), (0, 5), (0, 0)))], axis=2
        )

    projected = mixed_dot(normed_b, in_w)
    gate_z = projected[:, :DSSM]
    pre_b = projected[:, DSSM:].astype(jnp.bfloat16)
    rim = from_behind(pre_b[rows - (KW - 1) :], "ctx", 1)
    extended = jnp.concatenate([rim, pre_b], axis=0).astype(jnp.float32)
    taps = jnp.stack(
        [
            (doc_numbers(lengths, position_index - (KW - 1) + tap) == docs).astype(jnp.float32)
            for tap in range(KW)
        ]
    )
    conv_f, conv_pull = jax.vjp(partial(conv_local, taps), extended, conv_w, conv_b)
    conv_b16 = conv_f.astype(jnp.bfloat16)
    order = jnp.arange(rows)
    running = jnp.dot(
        log_decay, (order[:, None] <= order[None, :]).astype(jnp.float32), precision=highest
    )
    entry = jnp.where((docs == doc_prev)[None, :], jnp.exp(running), 0.0)
    tail = jnp.where((docs == docs[-1])[None, :], jnp.exp(running[:, -1:] - running), 0.0)
    carry_gain = jnp.where(docs[-1] == doc_prev, jnp.exp(running[:, -1]), 0.0)

    def columns(array):
        return array.reshape(HM // 2, 2, rows).transpose(0, 2, 1)

    running_rows = running.reshape(HM // 2, 2, rows)
    running_columns, entry_columns, tail_columns = columns(running), columns(entry), columns(tail)
    skip_wide = jnp.repeat(skip_w, PM).reshape(HM // 2, 1, 2 * PM)
    docs_column, docs_row = docs[:, None], docs[None, :]
    fresh = state_outer(DSSM // NS)(tail_columns, conv_b16, conv_b16)
    gain_rows = jnp.pad(jnp.stack(split_three(carry_gain)), ((0, 13), (0, NS - HM)))
    collected = lax.all_gather(jnp.concatenate([fresh, gain_rows], axis=0), "ctx")
    gains = jnp.sum(collected[:, DSSM : DSSM + 3, :HM].astype(jnp.float32), axis=1)
    state_in = chain(collected[:, :DSSM], gains, False)

    doc_side = side_rows(doc_rows, None)
    heads_x, log_x = attend_forward(group_blocks, pairs, key_side, query_x, doc_side)
    heads_t = from_groups(balance(heads_x.astype(jnp.bfloat16)))

    mixed = mixer_forward(
        skip_wide,
        conv_b16,
        conv_b16,
        conv_b16,
        running_columns,
        running_rows,
        entry_columns,
        docs_column,
        docs_row,
        state_in,
    )
    gated, gate_pull = jax.vjp(gate_norm, mixed, gate_z, mixer_g)
    gated_b = gated.astype(jnp.bfloat16)
    mamba = mixed_dot(gated_b, mixer_w)
    attn = lax.dot_general(
        heads_t, attn_w, (((0,), (0,)), ((), ())), preferred_element_type=jnp.float32
    )
    middle = source + attn + mamba
    normed2, ffn_pull = jax.vjp(rms_scale, middle, ffn_g)
    normed2_b = normed2.astype(jnp.bfloat16)
    gate_up_v = mixed_dot(normed2_b, gate_up_w)
    activated, act_pull = jax.vjp(swiglu, gate_up_v)
    activated_b = activated.astype(jnp.bfloat16)
    layer_out = (middle + mixed_dot(activated_b, down_w)).astype(jnp.bfloat16)

    out_low = cotangent[0]
    down_sum = weight_grad(activated_b, out_low)
    (gate_up_grad_v,) = act_pull(nt_dot(out_low, down_w))
    gate_up_low = gate_up_grad_v.astype(jnp.bfloat16)
    gate_up_share, down_share = ctx_sum(
        [weight_grad(normed2_b, gate_up_low), down_sum], model // shards, 0
    )
    middle_norm_grad, ffn_gain_grad = ffn_pull(nt_dot(gate_up_low, gate_up_w))
    middle_grad = out_low.astype(jnp.float32) + middle_norm_grad
    middle_low = middle_grad.astype(jnp.bfloat16)
    heads_low = nt_dot(attn_w, middle_low).astype(jnp.bfloat16)
    grad_x = balance(to_groups(heads_low))
    gated_grad = nt_dot(middle_low, mixer_w)
    mixed_grad, gate_z_grad, mixer_gain_grad = gate_pull(gated_grad)
    upward = state_outer(DSSM // NS + 1)(entry_columns, mixed_grad.astype(jnp.bfloat16), conv_b16)
    state_out_grad = chain(lax.all_gather(upward, "ctx"), gains, True)
    gate_z_low = gate_z_grad.astype(jnp.bfloat16)
    mixer_products = split_products(gated_b, middle_low)
    attn_products = split_products(heads_t, middle_low, 0)
    shard_sizes = [mixer_out.shape[0], attn_out.shape[0]]

    def interleaved(parts):
        return jnp.concatenate(
            [
                part[start * size : (start + 1) * size]
                for start in range(parts[0].shape[0] // shard_sizes[0])
                for part, size in zip(parts, shard_sizes)
            ],
            axis=0,
        ).astype(jnp.bfloat16)

    mixer_attn_sum = shard_sum(
        *[interleaved(parts) for parts in zip(mixer_products, attn_products)]
    )
    mixer_attn_share, in_share_z = ctx_sum(
        [mixer_attn_sum, weight_grad(normed_b, gate_z_low)], model // shards, 1
    )
    mixer_share = mixer_attn_share[: mixer_out.shape[0]]
    attn_share = mixer_attn_share[mixer_out.shape[0] :]

    delta = jnp.sum(grad_x.astype(jnp.float32) * heads_x, axis=2, keepdims=True)
    query_grad_x, pairs_grad = attend_backward(
        group_blocks,
        pairs,
        key_side,
        query_x,
        side_rows(doc_rows, log_x),
        grad_x,
        side_rows(jnp.zeros_like(doc_rows), delta),
    )
    pair_grad = (
        lax.psum_scatter(pairs_grad, "ctx", scatter_dimension=0)
        .astype(jnp.float32)
        .transpose(0, 2, 1)
    )
    query_back = jnp.stack(
        [
            turn(
                query_grad_x[at].reshape(KEY_VALUE_HEADS, HEAD_SIZE, heads_per_group * width),
                -jnp.tile(group_positions[at], heads_per_group),
            )
            for at in range(2)
        ]
    )
    query_low = from_groups(balance((query_back * scale).astype(jnp.bfloat16)))

    conv_grad, skip_parts = mixer_backward(
        skip_wide,
        conv_b16,
        conv_b16,
        conv_b16,
        running_columns,
        running_rows,
        entry_columns,
        tail_columns,
        docs_column,
        docs_row,
        state_in,
        state_out_grad,
        mixed_grad,
    )
    skip_grad = jnp.sum(skip_parts.reshape(HM, PM), axis=1)
    extended_grad, conv_weight_grad, conv_bias_grad = conv_pull(conv_grad)
    from_above = from_behind(extended_grad[: KW - 1], "ctx", -1)
    pre_grad = extended_grad[KW - 1 :] + jnp.pad(from_above, ((rows - (KW - 1), 0), (0, 0)))
    pre_low = pre_grad.astype(jnp.bfloat16)
    in_sum_pre = weight_grad(normed_b, pre_low)
    projected_low = jnp.concatenate([gate_z_low, pre_low], axis=1)
    normed_grad = nt_dot(projected_low, in_w)

    keys_low = turn(pair_grad[:, :HEAD_SIZE], -position_index)
    keyval_low = jnp.concatenate(
        [
            keys_low.reshape(KEY_VALUE_HEADS * HEAD_SIZE, rows),
            pair_grad[:, HEAD_SIZE:].reshape(KEY_VALUE_HEADS * HEAD_SIZE, rows),
        ],
        axis=0,
    ).astype(jnp.bfloat16)
    attn_pair_low = jnp.concatenate([query_low, keyval_low], axis=0).T
    attn_pair_sum = weight_grad(normed_b, attn_pair_low)
    normed_grad = normed_grad + nt_dot(attn_pair_low, attn_pair_w)
    source_grad, norm_grad = norm_pull(normed_grad)
    tokens_grad = (middle_grad + source_grad)[None]

    small_grad = pack_small(
        norm_grad, conv_weight_grad, conv_bias_grad, skip_grad, mixer_gain_grad, ffn_gain_grad, shards
    )
    in_share_pre, attn_pair_share, small_share = ctx_sum(
        [in_sum_pre, attn_pair_sum, shard_sum(*shard_pieces(small_grad, 0))], model // shards, 2
    )
    norm_share, conv_w_share, conv_b_share, skip_share, mixer_g_share, ffn_share = unpack_small(
        small_share, model, channels, HM, 1
    )
    return (
        layer_out[None],
        tokens_grad,
        norm_share,
        jnp.concatenate([in_share_z, in_share_pre], axis=1),
        conv_w_share,
        conv_b_share,
        skip_share,
        mixer_g_share,
        mixer_share,
        attn_pair_share[:, : QUERY_HEADS * HEAD_SIZE],
        attn_pair_share[:, QUERY_HEADS * HEAD_SIZE :],
        attn_share,
        ffn_share,
        gate_up_share,
        down_share,
    )


def solution(mesh):
    in_specs = (
        P("wshard", "ctx", None),
        P("wshard", "ctx", None),
        P("wshard", None),
        P("wshard", None, "ctx"),
        P("wshard"),
        P("wshard", None),
        P(None, "wshard"),
        P("wshard"),
        P("wshard"),
        P("wshard"),
        P("wshard", None),
        P("wshard", None),
        P("wshard", None),
        P("wshard", None),
        P("wshard"),
        P("wshard", None),
        P("wshard", None),
    )
    out_specs = (
        P("wshard", "ctx", None),
        P("wshard", "ctx", None),
        P("wshard"),
        P("wshard", None),
        P(None, "wshard"),
        P("wshard"),
        P("wshard"),
        P("wshard"),
        P("wshard", None),
        P("wshard", None),
        P("wshard", None),
        P("wshard", None),
        P("wshard"),
        P("wshard", None),
        P("wshard", None),
    )
    return jax.shard_map(
        per_device, mesh=mesh, in_specs=in_specs, out_specs=out_specs, check_vma=False
    )
```

```python
from functools import partial

import jax
import jax.numpy as jnp
from jax import lax
from jax.experimental import pallas as pl
from jax.experimental.pallas import tpu as pltpu
from jax.sharding import PartitionSpec as P

FF = 2048
QUERY_HEADS = 8
KEY_VALUE_HEADS = 2
HEAD_SIZE = 64
HM = 24
PM = 64
NS = 128
KW = 4
DSSM = 1536

eps_norm = 1e-05
rope_base = 100000000000.0
mask_fill_value = -1e30
highest = lax.Precision.HIGHEST
MESH_AXES = ("ctx", "wshard")
small_cost = pl.CostEstimate(flops=1024, bytes_accessed=1024, transcendentals=0)


def exchange(block, ctx_flip, shard_flip):
    blocks, shards = lax.axis_size("ctx"), lax.axis_size("wshard")
    route = [
        (c * shards + w, (c ^ ctx_flip) * shards + (w ^ shard_flip))
        for c in range(blocks)
        for w in range(shards)
    ]
    return lax.ppermute(block, MESH_AXES, route)


def from_behind(block, axis, distance):
    devices = range(lax.axis_size(axis))
    route = [(i - distance, i) for i in devices if i - distance in devices]
    return lax.ppermute(block, axis, route)


def swap_mirrored(block):
    count = lax.axis_size("ctx")
    return lax.ppermute(block, "ctx", [(i, count - 1 - i) for i in range(count)])


def tie_body(*refs):
    pass


def tie(value, *after):
    anywhere = pl.BlockSpec(memory_space=pl.ANY)
    return pl.pallas_call(
        tie_body,
        in_specs=[anywhere] * (1 + len(after)),
        out_specs=anywhere,
        out_shape=jax.ShapeDtypeStruct(value.shape, value.dtype),
        input_output_aliases={0: 0},
        cost_estimate=pl.CostEstimate(flops=0, bytes_accessed=0, transcendentals=0),
        name="tie",
    )(value, *after)


def assemble_body(spans, target_ref, *refs):
    out_ref = refs[len(spans)]
    step = pl.program_id(0)
    for piece, (first, size) in zip(refs, spans):

        def put(piece=piece):
            out_ref[...] = piece[...]

        pl.when((step >= first) & (step < first + size))(put)


def assemble(pieces, rows):
    spans, offsets, targets = [], [], []
    for _, source, start, size in pieces:
        spans.append((len(targets), size // rows))
        offsets.append(source // rows)
        targets += [start // rows + at for at in range(size // rows)]
    columns, kind = pieces[0][0].shape[1], pieces[0][0].dtype

    def source_map(offset, first, size):
        return lambda i, target: (offset + jnp.clip(i - first, 0, size - 1), 0)

    return pl.pallas_call(
        partial(assemble_body, spans),
        grid_spec=pltpu.PrefetchScalarGridSpec(
            num_scalar_prefetch=1,
            grid=(len(targets),),
            in_specs=[
                pl.BlockSpec((rows, columns), source_map(offset, first, size))
                for offset, (first, size) in zip(offsets, spans)
            ],
            out_specs=pl.BlockSpec((rows, columns), lambda i, target: (target[i], 0)),
        ),
        out_shape=jax.ShapeDtypeStruct((rows * len(targets), columns), kind),
        compiler_params=pltpu.CompilerParams(
            dimension_semantics=("arbitrary",), vmem_limit_bytes=32 * 1024 * 1024
        ),
        cost_estimate=small_cost,
        name="assemble",
    )(jnp.stack([jnp.asarray(target, jnp.int32) for target in targets]), *[p[0] for p in pieces])


def gather_first(shard, rows):
    part = rows // 4
    w = lax.axis_index("wshard")
    side = lax.axis_index("ctx") % 2
    direct = shard[2 * part :]
    across = exchange(lax.dynamic_slice_in_dim(shard, side * part, part, 0), 0, 2)
    across_direct = exchange(direct, 0, 2)
    beside = exchange(shard, 0, 1)
    across_relayed = exchange(across, 1, 0)
    far, far_direct, far_relayed = (
        exchange(piece, 0, 1) for piece in (across, across_direct, across_relayed)
    )
    pieces = [(shard, 0, w * rows, rows), (beside, 0, (w ^ 1) * rows, rows)]
    for flip, early, late, rest in (
        (2, across, across_relayed, across_direct),
        (3, far, far_relayed, far_direct),
    ):
        start = (w ^ flip) * rows
        pieces.append((early, 0, start + side * part, part))
        pieces.append((late, 0, start + (1 - side) * part, part))
        pieces.append((rest, 0, start + 2 * part, 2 * part))
    tails = [shard[rows], beside[rows], across_direct[2 * part], far_direct[2 * part]]
    small = jnp.zeros((4, shard.shape[1]), shard.dtype)
    for flip, tail in enumerate(tails):
        small = lax.dynamic_update_slice_in_dim(small, tail[None], w ^ flip, 0)
    return assemble(pieces, part), small, across_direct


def start_shards(stacked, after):
    stacked, _ = lax.optimization_barrier((stacked, after))
    return stacked, exchange(stacked, 0, 1), exchange(stacked, 0, 2)


def finish_shards(pieces, sizes, after, rows):
    own, beside, across = pieces
    far = exchange(tie(across, after), 0, 1)
    w = lax.axis_index("wshard")
    wholes, source = [], 0
    for size in sizes:
        wholes.append(
            assemble(
                [
                    (part, source, (w ^ flip) * size, size)
                    for flip, part in enumerate((own, beside, across, far))
                ],
                rows,
            )
        )
        source += size
    return wholes


def add_low(first, *others):
    total = first.astype(jnp.float32)
    for other in others:
        total = total + other.astype(jnp.float32)
    return total.astype(jnp.bfloat16)


def lay_side_by_side(blocks, rows):
    parts = []
    for block in blocks:
        for start in range(0, block.shape[0], rows):
            part = block[start : start + rows]
            parts.append(jnp.pad(part, ((0, rows - part.shape[0]), (0, 0))))
    return jnp.concatenate(parts, axis=1)


def take_apart(array, shapes):
    rows, start, blocks = array.shape[0], 0, []
    for height, columns in shapes:
        parts = []
        for _ in range(0, height, rows):
            parts.append(array[: min(height, rows), start : start + columns])
            start += columns
        blocks.append(parts[0] if len(parts) == 1 else jnp.concatenate(parts, axis=0))
    return blocks


def ctx_half(blocks, rows):
    side = lax.axis_index("ctx") % 2
    whole = lay_side_by_side(blocks, rows)
    half = rows // 2
    got = exchange(lax.dynamic_slice_in_dim(whole, (1 - side) * half, half, 0), 1, 0)
    return add_low(lax.dynamic_slice_in_dim(whole, side * half, half, 0), got), got


def ctx_lines():
    count = lax.axis_size("ctx")
    return [list(range(start, count, 2)) for start in range(2)]


def ctx_finish(mine, shapes, turn_at):
    side = lax.axis_index("ctx") % 2
    lines = ctx_lines()
    if turn_at % 2:
        lines = lines[::-1]
    if turn_at // 2:
        lines = [line[::-1] for line in lines]
    mine = lax.psum(mine, "ctx", axis_index_groups=lines)
    got = exchange(mine, 1, 0)
    whole = jnp.where(
        side == 0, jnp.concatenate([mine, got], axis=0), jnp.concatenate([got, mine], axis=0)
    ).astype(jnp.float32)
    return take_apart(whole, shapes)


def shard_pieces(array, axis):
    w = lax.axis_index("wshard")
    size = array.shape[axis] // 4

    def piece(flip):
        return lax.dynamic_slice_in_dim(array, (w ^ flip) * size, size, axis)

    return jnp.concatenate([piece(1), piece(3)], axis=axis), piece(2), piece(0)


def shard_sum(beside, across, own):
    rows = own.shape[0]
    got = exchange(beside.astype(jnp.bfloat16), 0, 1)
    got_across = exchange(add_low(across, got[rows:]), 0, 2)
    return add_low(own, got[:rows], got_across), got, got_across


def split_products(left, right, axis=1):
    return [
        lax.dot_general(
            piece, right, (((1 - axis,), (0,)), ((), ())), preferred_element_type=jnp.float32
        )
        for piece in shard_pieces(left, axis)
    ]


def weight_grad(left, right):
    return shard_sum(*split_products(left, right))


def mixed_dot(left, right):
    return jnp.dot(left, right, preferred_element_type=jnp.float32)


def rms_scale(value, gain):
    return value * lax.rsqrt(jnp.mean(value * value, axis=-1, keepdims=True) + eps_norm) * gain


def doc_numbers(lengths, position_index):
    ends = jnp.cumsum(lengths)[:-1]
    tally_count = jnp.sum((position_index[:, None] >= ends[None, :]).astype(jnp.int32), axis=1)
    return jnp.where(position_index >= 0, tally_count, -1)


def turn(value, position_index):
    half = value.shape[-2] // 2
    freq = rope_base ** (-jnp.arange(half, dtype=jnp.float32) / half)
    angle = freq[:, None] * position_index.astype(jnp.float32)[None, :]
    cosine = jnp.cos(angle)
    sine = jnp.sin(angle)
    first = value[..., :half, :]
    second = value[..., half:, :]
    return jnp.concatenate(
        [first * cosine - second * sine, second * cosine + first * sine], axis=-2
    )


def conv_local(taps, extended, weight, bias):
    tally_count = extended.shape[0] - (KW - 1)
    total = bias[None, :]
    for tap in range(KW):
        total = (
            total + weight[tap][None, :] * extended[tap : tap + tally_count] * taps[tap][:, None]
        )
    return jax.nn.silu(total)


def gate_norm(mixed, gate_z, gain):
    return rms_scale(mixed * jax.nn.silu(gate_z), gain)


def swiglu(gate_up_v):
    return jax.nn.silu(gate_up_v[:, :FF]) * gate_up_v[:, FF:]


def split_three(value):
    high = value.astype(jnp.bfloat16)
    rest = value - high.astype(jnp.float32)
    middle = rest.astype(jnp.bfloat16)
    low = (rest - middle.astype(jnp.float32)).astype(jnp.bfloat16)
    return [high, middle, low]


def nt_dot(left, right):
    return lax.dot_general(left, right, (((1,), (1,)), ((), ())), preferred_element_type=jnp.float32)


def causal_tile(scores, group, width):
    rows = lax.broadcasted_iota(jnp.int32, scores.shape, 0)
    columns = lax.broadcasted_iota(jnp.int32, scores.shape, 1)
    return jnp.where(rows <= lax.rem(columns, width) + group * width, scores, mask_fill_value)


def load_extended(extended, lower, value_ref, side_ref):
    for group in range(2):
        extended[group] = jnp.zeros(extended.shape[1:], extended.dtype)
        extended[group, lower : lower + HEAD_SIZE, :] = value_ref[group, 0]
        extended[group, 128:144, :] = side_ref[group, 0]


def attend_forward_body(
    width, blocks, pair_ref, side_ref, query_ref, query_side_ref, *refs
):
    heads_ref, log_ref, query_x, peak, total = refs[-5:]
    step = pl.program_id(1)

    @pl.when(step == 0)
    def start():
        load_extended(query_x, 0, query_ref, query_side_ref)
        peak[...] = jnp.full(peak.shape, mask_fill_value, jnp.float32)
        total[...] = jnp.zeros(total.shape, jnp.float32)

    @pl.when(step <= jnp.maximum(blocks[0], blocks[1]))
    def work():
        keys = jnp.concatenate([pair_ref[0, 0], side_ref[...]], axis=1)
        values = keys.T[HEAD_SIZE:144]

        def tile(group, masked):
            scores = mixed_dot(keys, query_x[group])
            if masked:
                scores = causal_tile(scores, group, width)
            old = peak[group]
            new = jnp.maximum(old, jnp.max(scores, axis=0, keepdims=True))
            probs = jnp.exp(scores - new)
            total[group] = total[group] * jnp.exp(old - new) + mixed_dot(
                values, probs.astype(jnp.bfloat16)
            )
            peak[group] = new

        for group in range(2):
            pl.when(step < blocks[group])(partial(tile, group, False))
            pl.when(step == blocks[group])(partial(tile, group, True))

    @pl.when(step == pl.num_programs(1) - 1)
    def finish():
        for group in range(2):
            weight = total[group, HEAD_SIZE + 8 : HEAD_SIZE + 9, :]
            heads_ref[group, 0] = total[group, :HEAD_SIZE, :] / weight
            log_ref[group, 0] = peak[group] + jnp.log(weight)


def attend_backward_body(
    width,
    blocks,
    pair_ref,
    side_ref,
    query_ref,
    query_side_ref,
    grad_ref,
    grad_side_ref,
    *refs,
):
    query_grad_ref, pair_grad_ref, query_x, grad_x, pair_acc = refs[-5:]
    step = pl.program_id(1)

    @pl.when(step == 0)
    def start():
        load_extended(query_x, 0, query_ref, query_side_ref)
        load_extended(grad_x, HEAD_SIZE, grad_ref, grad_side_ref)
        query_grad_ref[...] = jnp.zeros(query_grad_ref.shape, jnp.float32)

    pair_acc[...] = jnp.zeros(pair_acc.shape, jnp.float32)

    @pl.when(step <= jnp.maximum(blocks[0], blocks[1]))
    def work():
        pair = pair_ref[0, 0]
        keys = jnp.concatenate([pair, side_ref[...]], axis=1)
        turned = pair.T[:HEAD_SIZE]

        def tile(group, masked):
            scores = mixed_dot(keys, query_x[group])
            if masked:
                scores = causal_tile(scores, group, width)
            probs = jnp.exp(scores)
            low = (probs * mixed_dot(keys, grad_x[group])).astype(jnp.bfloat16)
            pair_acc[...] += nt_dot(low, query_x[group, :128, :]) + nt_dot(
                probs.astype(jnp.bfloat16), grad_x[group, :128, :]
            )
            query_grad_ref[group, 0] += mixed_dot(turned, low)

        for group in range(2):
            pl.when(step < blocks[group])(partial(tile, group, False))
            pl.when(step == blocks[group])(partial(tile, group, True))

    pair_grad_ref[0, 0] = pair_acc[...].astype(jnp.bfloat16)


def attention_calls(rows, count, anchors):
    width = rows // 2
    span = width * (QUERY_HEADS // KEY_VALUE_HEADS)

    def last(blocks):
        return jnp.maximum(blocks[0], blocks[1])

    pair_spec = pl.BlockSpec(
        (1, 1, rows, 128), lambda g, k, blocks: (jnp.minimum(k, last(blocks)), g, 0, 0)
    )
    side_spec = pl.BlockSpec((rows, 128), lambda g, k, blocks: (jnp.minimum(k, last(blocks)), 0))

    def per_group(height):
        return pl.BlockSpec((2, 1, height, span), lambda g, k, blocks: (0, g, 0, 0))

    anywhere = pl.BlockSpec(memory_space=pl.ANY)
    params = pltpu.CompilerParams(
        dimension_semantics=("arbitrary", "arbitrary"), vmem_limit_bytes=48 * 1024 * 1024
    )
    forward = pl.pallas_call(
        partial(attend_forward_body, width),
        grid_spec=pltpu.PrefetchScalarGridSpec(
            num_scalar_prefetch=1,
            grid=(KEY_VALUE_HEADS, count),
            in_specs=[pair_spec, side_spec, per_group(HEAD_SIZE), per_group(16)]
            + [anywhere] * anchors[0],
            out_specs=[per_group(HEAD_SIZE), per_group(1)],
            scratch_shapes=[
                pltpu.VMEM((2, 256, span), jnp.bfloat16),
                pltpu.VMEM((2, 1, span), jnp.float32),
                pltpu.VMEM((2, 144 - HEAD_SIZE, span), jnp.float32),
            ],
        ),
        out_shape=[
            jax.ShapeDtypeStruct((2, KEY_VALUE_HEADS, HEAD_SIZE, span), jnp.float32),
            jax.ShapeDtypeStruct((2, KEY_VALUE_HEADS, 1, span), jnp.float32),
        ],
        compiler_params=params,
        cost_estimate=small_cost,
        name="attend_forward",
    )
    backward = pl.pallas_call(
        partial(attend_backward_body, width),
        grid_spec=pltpu.PrefetchScalarGridSpec(
            num_scalar_prefetch=1,
            grid=(KEY_VALUE_HEADS, count),
            in_specs=[
                pair_spec,
                side_spec,
                per_group(HEAD_SIZE),
                per_group(16),
                per_group(HEAD_SIZE),
                per_group(16),
            ]
            + [anywhere] * anchors[1],
            out_specs=[
                per_group(HEAD_SIZE),
                pl.BlockSpec((1, 1, rows, 128), lambda g, k, blocks: (k, g, 0, 0)),
            ],
            scratch_shapes=[
                pltpu.VMEM((2, 256, span), jnp.bfloat16),
                pltpu.VMEM((2, 256, span), jnp.bfloat16),
                pltpu.VMEM((rows, 128), jnp.float32),
            ],
        ),
        out_shape=[
            jax.ShapeDtypeStruct((2, KEY_VALUE_HEADS, HEAD_SIZE, span), jnp.float32),
            jax.ShapeDtypeStruct((count, KEY_VALUE_HEADS, rows, 128), jnp.bfloat16),
        ],
        compiler_params=params,
        cost_estimate=small_cost,
        name="attend_backward",
    )
    return forward, backward


def pick(pair):
    lane = lax.broadcasted_iota(jnp.int32, (pair.shape[0], 2 * PM), 1)
    return jnp.where(lane < PM, pair[:, 0:1], pair[:, 1:2])


def outer_body(rows_ref, left_ref, right_ref, *refs):
    out_ref = refs[-1]
    for at in range(rows_ref.shape[0]):
        scale = pick(rows_ref[at])
        left = left_ref[:, at * 128 : (at + 1) * 128].astype(jnp.float32) * scale
        out_ref[at * 128 : (at + 1) * 128, :] = lax.dot_general(
            left.astype(jnp.bfloat16),
            right_ref[...],
            (((0,), (0,)), ((), ())),
            preferred_element_type=jnp.float32,
        ).astype(out_ref.dtype)


def join_body(c_ref, entry_ref, state_ref, local_ref, *refs):
    out_ref = refs[-1]
    for at in range(entry_ref.shape[0]):
        here = slice(at * 2 * PM, (at + 1) * 2 * PM)
        inner = nt_dot(c_ref[...], state_ref[here, :])
        out_ref[:, here] = local_ref[:, here] + inner * pick(entry_ref[at])


def mixed_body(
    skip_ref, x_ref, b_ref, c_ref, column_ref, row_ref, docs_column, docs_row, out_ref, fill, products
):
    rows = x_ref.shape[0]
    half = rows // 2

    @pl.when(pl.program_id(0) == 0)
    def start():
        at = lax.broadcasted_iota(jnp.int32, (rows, rows), 0)
        source = lax.broadcasted_iota(jnp.int32, (rows, rows), 1)
        same = (at >= source) & (docs_column[...] == docs_row[...])
        fill[...] = jnp.where(same, 0.0, mask_fill_value)
        products[...] = nt_dot(c_ref[...], b_ref[...])

    x = x_ref[...]
    lane = lax.broadcasted_iota(jnp.int32, (half, 2 * PM), 1)
    for block in range(2):
        here = slice(block * half, (block + 1) * half)
        width = (block + 1) * half
        parts = []
        for head in range(2):
            decay = jnp.exp(
                (column_ref[0, here, head : head + 1] - row_ref[0, head : head + 1, :width])
                + fill[here, :width]
            )
            weights = (products[here, :width] * decay).astype(jnp.bfloat16)
            parts.append(mixed_dot(weights, x[:width]))
        local = jnp.where(lane < PM, parts[0], parts[1])
        out_ref[here, :] = local + x[here].astype(jnp.float32) * skip_ref[0]


def mixed_grad_body(
    skip_ref,
    x_ref,
    b_ref,
    c_ref,
    column_ref,
    row_ref,
    entry_ref,
    tail_ref,
    docs_column,
    docs_row,
    state_ref,
    state_grad_ref,
    grad_ref,
    *refs,
):
    out_ref, skip_grad_ref, fill, products, scores, b_grad, c_grad = refs[-7:]
    rows = x_ref.shape[0]
    half = rows // 2
    step = pl.program_id(0)
    pairs = HM // 2

    @pl.when(step == 0)
    def start():
        source = lax.broadcasted_iota(jnp.int32, (rows, rows), 0)
        at = lax.broadcasted_iota(jnp.int32, (rows, rows), 1)
        same = (at >= source) & (docs_column[...] == docs_row[...])
        fill[...] = jnp.where(same, 0.0, mask_fill_value)
        products[...] = nt_dot(b_ref[...], c_ref[...])
        scores[...] = jnp.zeros(scores.shape, jnp.float32)
        b_grad[...] = jnp.zeros(b_grad.shape, jnp.float32)
        c_grad[...] = jnp.zeros(c_grad.shape, jnp.float32)

    @pl.when(step < pairs)
    def work():
        x = x_ref[...]
        x_f = x.astype(jnp.float32)
        grad = grad_ref[...]
        low = grad.astype(jnp.bfloat16)
        lane = lax.broadcasted_iota(jnp.int32, (half, 2 * PM), 1)
        lane_all = lax.broadcasted_iota(jnp.int32, (rows, 2 * PM), 1)
        skip_grad_ref[0] = jnp.sum(grad * x_f, axis=0, keepdims=True)
        state_grad = state_grad_ref[...]
        tail = pick(tail_ref[0])
        b_grad[...] += mixed_dot((x_f * tail).astype(jnp.bfloat16), state_grad)
        entered = (low.astype(jnp.float32) * pick(entry_ref[0])).astype(jnp.bfloat16)
        c_grad[...] += mixed_dot(entered, state_ref[...])
        passed = nt_dot(b_ref[...], state_grad) * tail + grad * skip_ref[0]
        chosen = [
            jnp.where((lane_all < PM) == (head == 0), x_f, 0.0).astype(jnp.bfloat16)
            for head in range(2)
        ]
        for block in range(2):
            here = slice(block * half, (block + 1) * half)
            start_at = block * half
            parts = []
            for head in range(2):
                decay = jnp.exp(
                    (row_ref[0, head : head + 1, start_at:] - column_ref[0, here, head : head + 1])
                    + fill[here, start_at:]
                )
                weights = (products[here, start_at:] * decay).astype(jnp.bfloat16)
                parts.append(mixed_dot(weights, low[start_at:]))
                scores[here, start_at:] += nt_dot(chosen[head][here], low[start_at:]) * decay
            out_ref[here, :] = jnp.where(lane < PM, parts[0], parts[1]) + passed[here]

    @pl.when(step == pairs)
    def give_b():
        out_ref[...] = b_grad[...] + mixed_dot(scores[...].astype(jnp.bfloat16), c_ref[...])

    @pl.when(step == pairs + 1)
    def give_c():
        out_ref[...] = c_grad[...] + lax.dot_general(
            scores[...].astype(jnp.bfloat16),
            b_ref[...],
            (((0,), (0,)), ((), ())),
            preferred_element_type=jnp.float32,
        )


def mixer_calls(rows, anchors):
    pairs = HM // 2
    wide = 2 * PM
    params = pltpu.CompilerParams(
        dimension_semantics=("arbitrary",), vmem_limit_bytes=48 * 1024 * 1024
    )

    def capped(p):
        return jnp.minimum(p, pairs - 1)

    anywhere = pl.BlockSpec(memory_space=pl.ANY)

    def join(after):
        each = 4
        wide_spec = pl.BlockSpec((rows, each * wide), lambda p: (0, p))
        return pl.pallas_call(
            join_body,
            grid=(pairs // each,),
            in_specs=[
                pl.BlockSpec((rows, NS), lambda p: (0, DSSM // NS + 1)),
                pl.BlockSpec((each, rows, 2), lambda p: (p, 0, 0)),
                pl.BlockSpec((each * wide, NS), lambda p: (p, 0)),
                wide_spec,
            ]
            + [anywhere] * after,
            out_specs=wide_spec,
            out_shape=jax.ShapeDtypeStruct((rows, DSSM), jnp.float32),
            compiler_params=params,
            cost_estimate=small_cost,
            name="mixer_join",
        )

    def outer(right_at, after):
        each = 2
        return pl.pallas_call(
            outer_body,
            grid=(pairs // each,),
            in_specs=[
                pl.BlockSpec((each, rows, 2), lambda p: (p, 0, 0)),
                pl.BlockSpec((rows, each * wide), lambda p: (0, p)),
                pl.BlockSpec((rows, NS), lambda p: (0, right_at)),
            ]
            + [anywhere] * after,
            out_specs=pl.BlockSpec((each * wide, NS), lambda p: (p, 0)),
            out_shape=jax.ShapeDtypeStruct((DSSM, NS), jnp.bfloat16),
            compiler_params=params,
            cost_estimate=small_cost,
            name="state_outer",
        )

    x_spec = pl.BlockSpec((rows, wide), lambda p: (0, capped(p)))
    b_spec = pl.BlockSpec((rows, NS), lambda p: (0, DSSM // NS))
    c_spec = pl.BlockSpec((rows, NS), lambda p: (0, DSSM // NS + 1))
    column_spec = pl.BlockSpec((1, rows, 2), lambda p: (capped(p), 0, 0))
    row_spec = pl.BlockSpec((1, 2, rows), lambda p: (capped(p), 0, 0))
    skip_spec = pl.BlockSpec((1, 1, wide), lambda p: (capped(p), 0, 0))
    state_spec = pl.BlockSpec((wide, NS), lambda p: (capped(p), 0))
    docs_specs = [pl.BlockSpec((rows, 1), lambda p: (0, 0)), pl.BlockSpec((1, rows), lambda p: (0, 0))]
    square = pltpu.VMEM((rows, rows), jnp.float32)
    narrow = pltpu.VMEM((rows, NS), jnp.float32)
    forward = pl.pallas_call(
        mixed_body,
        grid=(pairs,),
        in_specs=[skip_spec, x_spec, b_spec, c_spec, column_spec, row_spec] + docs_specs,
        out_specs=pl.BlockSpec((rows, wide), lambda p: (0, p)),
        out_shape=jax.ShapeDtypeStruct((rows, DSSM), jnp.float32),
        scratch_shapes=[square, square],
        compiler_params=params,
        cost_estimate=small_cost,
        name="mixer_forward",
    )
    backward = pl.pallas_call(
        mixed_grad_body,
        grid=(pairs + 2,),
        in_specs=[skip_spec, x_spec, b_spec, c_spec, column_spec, row_spec, column_spec, column_spec]
        + docs_specs
        + [state_spec, state_spec, x_spec]
        + [anywhere] * anchors,
        out_specs=[
            pl.BlockSpec((rows, wide), lambda p: (0, p)),
            pl.BlockSpec((1, 1, wide), lambda p: (capped(p), 0, 0)),
        ],
        out_shape=[
            jax.ShapeDtypeStruct((rows, DSSM + 2 * NS), jnp.float32),
            jax.ShapeDtypeStruct((pairs, 1, wide), jnp.float32),
        ],
        scratch_shapes=[square, square, square, narrow, narrow],
        compiler_params=params,
        cost_estimate=small_cost,
        name="mixer_backward",
    )
    return outer, join, forward, backward


def pass_state(part, gains, reverse, after=()):
    count, position = lax.axis_size("ctx"), lax.axis_index("ctx")
    side, line_at = position % 2, position // 2
    half = DSSM // 2
    heads = HM // 2
    mine = lax.dynamic_slice_in_dim(part, side * half, half, 0)
    sent = lax.dynamic_slice_in_dim(part, (1 - side) * half, half, 0)
    if gains is None:
        rows = jnp.pad(jnp.stack(split_three(reverse[1])), ((0, 13), (0, NS - HM)))
        got = exchange(jnp.concatenate([sent, rows], axis=0), 1, 0)
        other = jnp.sum(got[half : half + 3, :HM].astype(jnp.float32), axis=0)
        own = reverse[1]
        got, reverse = got[:half], False
        pair_gain = own * other
    else:
        own, other, line_gains = gains
        got = exchange(sent, 1, 0)
    is_first = (side == 1) if reverse else (side == 0)

    def mine_of(gain):
        chosen = lax.dynamic_slice_in_dim(gain, side * heads, heads, gain.ndim - 1)
        return jnp.repeat(chosen, PM, axis=-1)[..., None]

    own_f, got_f = mine.astype(jnp.float32), got.astype(jnp.float32)
    first = jnp.where(is_first, own_f, got_f)
    second = jnp.where(is_first, got_f, own_f)
    first_gain = jnp.where(is_first, own, other)
    second_gain = jnp.where(is_first, other, own)
    total = (mine_of(second_gain) * first + second).astype(jnp.bfloat16)
    if gains is None:
        rows = jnp.pad(jnp.stack(split_three(pair_gain)), ((0, 13), (0, NS - HM)))
        total = jnp.concatenate([total, rows], axis=0)
    totals = lax.all_gather(total, "ctx", axis_index_groups=ctx_lines())
    if gains is None:
        line_gains = jnp.sum(totals[:, half : half + 3, :HM].astype(jnp.float32), axis=1)
        totals = totals[:, :half]
    factor = jnp.ones((HM,), jnp.float32)
    entering = jnp.zeros((half, NS), jnp.float32)
    lines = range(count // 2)
    for at in lines if reverse else reversed(lines):
        reached = at > line_at if reverse else at < line_at
        weight = mine_of(jnp.where(reached, factor, 0.0))
        entering = entering + weight * totals[at].astype(jnp.float32)
        factor = factor * jnp.where(reached, line_gains[at], 1.0)
    later = mine_of(first_gain) * entering + first
    kept = jnp.where(is_first, entering, later).astype(jnp.bfloat16)
    passed = jnp.where(is_first, later, entering).astype(jnp.bfloat16)
    back = exchange(passed, 1, 0)
    state = jnp.where(
        side == 0, jnp.concatenate([kept, back], axis=0), jnp.concatenate([back, kept], axis=0)
    )
    return state, (own, other, line_gains)


def pack_small(norm, conv_weight, conv_bias, skip, mixer, ffn, shards):
    pieces = [
        norm.reshape(shards, -1),
        conv_weight.reshape(KW, shards, -1).transpose(1, 0, 2).reshape(shards, -1),
        conv_bias.reshape(shards, -1),
        mixer.reshape(shards, -1),
        ffn.reshape(shards, -1),
        skip.reshape(shards, -1),
    ]
    packed = jnp.concatenate(pieces, axis=1)
    packed = jnp.pad(packed, ((0, 0), (0, 4096 - packed.shape[1])))
    return packed.reshape(shards * 32, 128)


def unpack_small(packed, model, channels, heads, shards):
    packed = packed.reshape(shards, 4096)
    sizes = [model, KW * channels, channels, DSSM, model, heads]
    parts, start = [], 0
    for size in sizes:
        width = size // 4
        parts.append(packed[:, start : start + width])
        start += width
    norm, conv_weight, conv_bias, mixer, ffn, skip = parts
    conv_weight = conv_weight.reshape(shards, KW, -1).transpose(1, 0, 2).reshape(KW, -1)
    return (
        norm.reshape(-1),
        conv_weight,
        conv_bias.reshape(-1),
        skip.reshape(-1),
        mixer.reshape(-1),
        ffn.reshape(-1),
    )


def per_device(
    tokens,
    cotangent,
    doc_lengths,
    decay,
    norm_gain,
    in_proj,
    conv_weight,
    conv_bias,
    skip_gain,
    mixer_gain,
    mixer_out,
    query_proj,
    key_value_projection,
    attn_out,
    ffn_gain,
    gate_up,
    down_proj,
):
    rows, model = tokens.shape[1:]
    width = rows // 2
    shards = lax.axis_size("wshard")
    channels = conv_bias.shape[0] * shards
    count, block_at = lax.axis_size("ctx"), lax.axis_index("ctx")
    sequence_total = rows * count
    heads_per_group = QUERY_HEADS // KEY_VALUE_HEADS
    scale = HEAD_SIZE ** (-0.5)
    attend_forward, attend_backward = attention_calls(rows, count, (2, 2))
    state_outer, mixer_join, mixer_forward, mixer_backward = mixer_calls(rows, 4)

    packed = pack_small(norm_gain, conv_weight, conv_bias, skip_gain, mixer_gain, ffn_gain, 1)
    first_shard = jnp.concatenate([in_proj, query_proj, key_value_projection], axis=1)
    packed = jnp.pad(packed.reshape(1, -1), ((0, 15), (0, first_shard.shape[1] - 4096)))
    first_w, small, arrived = gather_first(
        jnp.concatenate([first_shard, packed], axis=0), in_proj.shape[0]
    )
    norm_w, conv_w, conv_b, skip_w, mixer_g, ffn_g = (
        part.astype(jnp.float32)
        for part in unpack_small(small[:, :4096], model, channels, HM, shards)
    )
    projected_width = in_proj.shape[1]
    in_w, attn_pair_w = first_w[:, :projected_width], first_w[:, projected_width:]
    out_pieces = start_shards(
        jnp.concatenate([mixer_out, attn_out, down_proj], axis=0), arrived
    )
    gate_up_pieces = start_shards(gate_up, arrived)
    query_w = attn_pair_w[:, : QUERY_HEADS * HEAD_SIZE]
    keyval_w = attn_pair_w[:, QUERY_HEADS * HEAD_SIZE :]

    lengths = doc_lengths[0]
    doc_count = lengths.shape[0]
    position_index = block_at * rows + jnp.arange(rows, dtype=jnp.int32)
    docs = doc_numbers(lengths, position_index)
    doc_prev = doc_numbers(lengths, position_index[:1] - 1)[0]
    log_decay = jnp.log(decay[0])
    source = tokens[0].astype(jnp.float32)
    normed, norm_pull = jax.vjp(rms_scale, source, norm_w)
    normed_b = normed.astype(jnp.bfloat16)

    turned_q = turn(
        lax.dot_general(
            query_w, normed_b, (((0,), (1,)), ((), ())), preferred_element_type=jnp.float32
        ).reshape(QUERY_HEADS, HEAD_SIZE, rows),
        position_index,
    ).astype(jnp.bfloat16)
    key_value_pair = lax.dot_general(
        keyval_w, normed_b, (((0,), (1,)), ((), ())), preferred_element_type=jnp.float32
    ).reshape(2, KEY_VALUE_HEADS, HEAD_SIZE, rows)
    keys_b = turn(key_value_pair[0], position_index).astype(jnp.bfloat16)
    values_b = key_value_pair[1].astype(jnp.bfloat16)
    pairs = lax.all_gather(
        jnp.concatenate([keys_b, values_b], axis=1).transpose(0, 2, 1), "ctx"
    )

    def to_groups(array):
        return (
            array.reshape(KEY_VALUE_HEADS, heads_per_group, HEAD_SIZE, 2, width)
            .transpose(3, 0, 2, 1, 4)
            .reshape(2, KEY_VALUE_HEADS, HEAD_SIZE, heads_per_group * width)
        )

    def from_groups(array):
        return (
            array.reshape(2, KEY_VALUE_HEADS, HEAD_SIZE, heads_per_group, width)
            .transpose(1, 3, 2, 0, 4)
            .reshape(QUERY_HEADS * HEAD_SIZE, rows)
        )

    def balance(array):
        return jnp.stack([array[0], swap_mirrored(array[1])])

    query_x = balance(to_groups(turned_q) * jnp.asarray(scale, jnp.bfloat16))
    mirrored = count - 1 - block_at
    group_blocks = jnp.stack([block_at, mirrored]).astype(jnp.int32)
    group_positions = jnp.stack(
        [
            block_at * rows + jnp.arange(width, dtype=jnp.int32),
            mirrored * rows + width + jnp.arange(width, dtype=jnp.int32),
        ]
    )
    group_docs = jnp.stack([doc_numbers(lengths, group_positions[at]) for at in range(2)])
    key_docs = doc_numbers(lengths, jnp.arange(sequence_total, dtype=jnp.int32))
    lane = jnp.arange(128)[None, :]
    key_side = ((key_docs[:, None] == lane) | ((lane >= 8) & (lane < 11))).astype(jnp.bfloat16)
    doc_rows = jnp.where(
        jnp.arange(doc_count)[None, :, None] == group_docs[:, None, :], 0.0, mask_fill_value
    ).astype(jnp.bfloat16)
    doc_rows = jnp.tile(doc_rows, (1, 1, heads_per_group))[:, None]
    doc_rows = jnp.broadcast_to(doc_rows, (2, KEY_VALUE_HEADS) + doc_rows.shape[2:])

    def side_rows(first, extra):
        first = jnp.pad(first, ((0, 0), (0, 0), (0, 8 - first.shape[2]), (0, 0)))
        if extra is None:
            return jnp.pad(first, ((0, 0), (0, 0), (0, 8), (0, 0)))
        extra = jnp.concatenate(split_three(-extra), axis=2)
        return jnp.concatenate(
            [first, jnp.pad(extra, ((0, 0), (0, 0), (0, 5), (0, 0)))], axis=2
        )

    projected = mixed_dot(normed_b, in_w)
    gate_z = projected[:, :DSSM]
    pre_b = projected[:, DSSM:].astype(jnp.bfloat16)
    rim = from_behind(pre_b[rows - (KW - 1) :], "ctx", 1)
    extended = jnp.concatenate([rim, pre_b], axis=0).astype(jnp.float32)
    taps = jnp.stack(
        [
            (doc_numbers(lengths, position_index - (KW - 1) + tap) == docs).astype(jnp.float32)
            for tap in range(KW)
        ]
    )
    conv_f, conv_pull = jax.vjp(partial(conv_local, taps), extended, conv_w, conv_b)
    conv_b16 = conv_f.astype(jnp.bfloat16)
    order = jnp.arange(rows)
    running = jnp.dot(
        log_decay, (order[:, None] <= order[None, :]).astype(jnp.float32), precision=highest
    )
    entry = jnp.where((docs == doc_prev)[None, :], jnp.exp(running), 0.0)
    tail = jnp.where((docs == docs[-1])[None, :], jnp.exp(running[:, -1:] - running), 0.0)
    carry_gain = jnp.where(docs[-1] == doc_prev, jnp.exp(running[:, -1]), 0.0)

    def columns(array):
        return array.reshape(HM // 2, 2, rows).transpose(0, 2, 1)

    running_rows = running.reshape(HM // 2, 2, rows)
    running_columns, entry_columns, tail_columns = columns(running), columns(entry), columns(tail)
    skip_wide = jnp.repeat(skip_w, PM).reshape(HM // 2, 1, 2 * PM)
    docs_column, docs_row = docs[:, None], docs[None, :]
    fresh = state_outer(DSSM // NS, 0)(tail_columns, conv_b16, conv_b16)
    state_in, gains = pass_state(fresh, None, (False, carry_gain))

    doc_side = side_rows(doc_rows, None)
    heads_x, log_x = attend_forward(
        group_blocks, pairs, key_side, query_x, doc_side, out_pieces[1], gate_up_pieces[1]
    )
    mixer_w, attn_w, down_w = finish_shards(
        out_pieces,
        [mixer_out.shape[0], attn_out.shape[0], down_proj.shape[0]],
        log_x,
        attn_out.shape[0],
    )
    (gate_up_w,) = finish_shards(gate_up_pieces, [gate_up.shape[0]], log_x, gate_up.shape[0] // 2)
    heads_t = from_groups(balance(heads_x.astype(jnp.bfloat16)))

    local = mixer_forward(
        skip_wide,
        conv_b16,
        conv_b16,
        conv_b16,
        running_columns,
        running_rows,
        docs_column,
        docs_row,
    )
    mixed = mixer_join(0)(conv_b16, entry_columns, state_in, local)
    gated, gate_pull = jax.vjp(gate_norm, mixed, gate_z, mixer_g)
    gated_b = gated.astype(jnp.bfloat16)
    mamba = mixed_dot(gated_b, mixer_w)
    attn = lax.dot_general(
        heads_t, attn_w, (((0,), (0,)), ((), ())), preferred_element_type=jnp.float32
    )
    middle = source + attn + mamba
    normed2, ffn_pull = jax.vjp(rms_scale, middle, ffn_g)
    normed2_b = normed2.astype(jnp.bfloat16)
    gate_up_v = mixed_dot(normed2_b, gate_up_w)
    activated, act_pull = jax.vjp(swiglu, gate_up_v)
    activated_b = activated.astype(jnp.bfloat16)
    layer_out = (middle + mixed_dot(activated_b, down_w)).astype(jnp.bfloat16)

    out_low = cotangent[0]
    down_sum, down_beside, down_across = weight_grad(activated_b, out_low)
    down_half, down_got = ctx_half([down_sum], model // shards)
    (gate_up_grad_v,) = act_pull(nt_dot(out_low, down_w))
    gate_up_low = gate_up_grad_v.astype(jnp.bfloat16)
    gate_up_sum, gate_up_beside, gate_up_across = weight_grad(normed2_b, gate_up_low)
    gate_up_half, gate_up_got = ctx_half([gate_up_sum], model // shards)
    middle_norm_grad, ffn_gain_grad = ffn_pull(nt_dot(gate_up_low, gate_up_w))
    middle_grad = out_low.astype(jnp.float32) + middle_norm_grad
    middle_low = middle_grad.astype(jnp.bfloat16)
    heads_low = nt_dot(attn_w, middle_low).astype(jnp.bfloat16)
    grad_x = balance(to_groups(heads_low))
    gated_grad = nt_dot(middle_low, mixer_w)
    mixed_grad, gate_z_grad, mixer_gain_grad = gate_pull(gated_grad)
    upward = state_outer(DSSM // NS + 1, 2)(
        entry_columns, mixed_grad.astype(jnp.bfloat16), conv_b16, down_beside, gate_up_beside
    )
    state_out_grad, _ = pass_state(upward, gains, True)
    gate_z_low = gate_z_grad.astype(jnp.bfloat16)
    mixer_products = split_products(gated_b, middle_low)
    attn_products = split_products(heads_t, middle_low, 0)
    shard_sizes = [mixer_out.shape[0], attn_out.shape[0]]

    def interleaved(parts):
        return jnp.concatenate(
            [
                part[start * size : (start + 1) * size]
                for start in range(parts[0].shape[0] // shard_sizes[0])
                for part, size in zip(parts, shard_sizes)
            ],
            axis=0,
        ).astype(jnp.bfloat16)

    mixer_attn_sum, mixer_beside, mixer_across = shard_sum(
        *[interleaved(parts) for parts in zip(mixer_products, attn_products)]
    )
    in_sum_z, in_z_beside, in_z_across = weight_grad(normed_b, gate_z_low)
    mixer_half, mixer_got = ctx_half([mixer_attn_sum, in_sum_z], model // shards)

    delta = jnp.sum(grad_x.astype(jnp.float32) * heads_x, axis=2, keepdims=True)
    query_grad_x, pairs_grad = attend_backward(
        group_blocks,
        pairs,
        key_side,
        query_x,
        side_rows(doc_rows, log_x),
        grad_x,
        side_rows(jnp.zeros_like(doc_rows), delta),
        down_across,
        mixer_beside,
    )
    pair_grad = (
        lax.psum_scatter(pairs_grad, "ctx", scatter_dimension=0)
        .astype(jnp.float32)
        .transpose(0, 2, 1)
    )
    query_back = jnp.stack(
        [
            turn(
                query_grad_x[at].reshape(KEY_VALUE_HEADS, HEAD_SIZE, heads_per_group * width),
                -jnp.tile(group_positions[at], heads_per_group),
            )
            for at in range(2)
        ]
    )
    query_low = from_groups(balance((query_back * scale).astype(jnp.bfloat16)))

    conv_grad, skip_parts = mixer_backward(
        skip_wide,
        conv_b16,
        conv_b16,
        conv_b16,
        running_columns,
        running_rows,
        entry_columns,
        tail_columns,
        docs_column,
        docs_row,
        state_in,
        state_out_grad,
        mixed_grad,
        gate_up_across,
        in_z_beside,
        down_got,
        mixer_across,
    )
    skip_grad = jnp.sum(skip_parts.reshape(HM, PM), axis=1)
    extended_grad, conv_weight_grad, conv_bias_grad = conv_pull(conv_grad)
    from_above = from_behind(extended_grad[: KW - 1], "ctx", -1)
    pre_grad = extended_grad[KW - 1 :] + jnp.pad(from_above, ((rows - (KW - 1), 0), (0, 0)))
    pre_low = tie(pre_grad.astype(jnp.bfloat16), gate_up_got, in_z_across)
    in_sum_pre, _, _ = weight_grad(normed_b, pre_low)
    projected_low = jnp.concatenate([gate_z_low, pre_low], axis=1)
    normed_grad = nt_dot(projected_low, in_w)

    keys_low = turn(pair_grad[:, :HEAD_SIZE], -position_index)
    keyval_low = jnp.concatenate(
        [
            keys_low.reshape(KEY_VALUE_HEADS * HEAD_SIZE, rows),
            pair_grad[:, HEAD_SIZE:].reshape(KEY_VALUE_HEADS * HEAD_SIZE, rows),
        ],
        axis=0,
    ).astype(jnp.bfloat16)
    attn_pair_low = jnp.concatenate([query_low, keyval_low], axis=0).T
    attn_pair_sum, _, _ = weight_grad(normed_b, attn_pair_low)
    normed_grad = normed_grad + nt_dot(attn_pair_low, attn_pair_w)
    source_grad, norm_grad = norm_pull(normed_grad)
    tokens_grad = (middle_grad + source_grad)[None]

    small_grad = pack_small(
        norm_grad, conv_weight_grad, conv_bias_grad, skip_grad, mixer_gain_grad, ffn_gain_grad, shards
    )
    small_sum, _, _ = shard_sum(*shard_pieces(small_grad, 0))
    last_half, _ = ctx_half([in_sum_pre, attn_pair_sum, small_sum], model // shards)
    (down_share,) = ctx_finish(down_half, [down_sum.shape], 0)
    (gate_up_share,) = ctx_finish(gate_up_half, [gate_up_sum.shape], 1)
    mixer_attn_share, in_share_z = ctx_finish(
        tie(mixer_half, gate_up_half), [mixer_attn_sum.shape, in_sum_z.shape], 2
    )
    mixer_share = mixer_attn_share[: mixer_out.shape[0]]
    attn_share = mixer_attn_share[mixer_out.shape[0] :]
    in_share_pre, attn_pair_share, small_share = ctx_finish(
        tie(last_half, mixer_half),
        [in_sum_pre.shape, attn_pair_sum.shape, small_sum.shape],
        3,
    )
    norm_share, conv_w_share, conv_b_share, skip_share, mixer_g_share, ffn_share = unpack_small(
        small_share, model, channels, HM, 1
    )
    return (
        layer_out[None],
        tokens_grad,
        norm_share,
        jnp.concatenate([in_share_z, in_share_pre], axis=1),
        conv_w_share,
        conv_b_share,
        skip_share,
        mixer_g_share,
        mixer_share,
        attn_pair_share[:, : QUERY_HEADS * HEAD_SIZE],
        attn_pair_share[:, QUERY_HEADS * HEAD_SIZE :],
        attn_share,
        ffn_share,
        gate_up_share,
        down_share,
    )


def solution(mesh):
    in_specs = (
        P("wshard", "ctx", None),
        P("wshard", "ctx", None),
        P("wshard", None),
        P("wshard", None, "ctx"),
        P("wshard"),
        P("wshard", None),
        P(None, "wshard"),
        P("wshard"),
        P("wshard"),
        P("wshard"),
        P("wshard", None),
        P("wshard", None),
        P("wshard", None),
        P("wshard", None),
        P("wshard"),
        P("wshard", None),
        P("wshard", None),
    )
    out_specs = (
        P("wshard", "ctx", None),
        P("wshard", "ctx", None),
        P("wshard"),
        P("wshard", None),
        P(None, "wshard"),
        P("wshard"),
        P("wshard"),
        P("wshard"),
        P("wshard", None),
        P("wshard", None),
        P("wshard", None),
        P("wshard", None),
        P("wshard"),
        P("wshard", None),
        P("wshard", None),
    )
    return jax.shard_map(
        per_device, mesh=mesh, in_specs=in_specs, out_specs=out_specs, check_vma=False
    )
```

```python
from functools import partial

import jax
import jax.numpy as jnp
from jax import lax
from jax.experimental import pallas as pl
from jax.experimental.pallas import tpu as pltpu
from jax.sharding import PartitionSpec as P

FF = 2048
QUERY_HEADS = 8
KEY_VALUE_HEADS = 2
HEAD_SIZE = 64
HM = 24
PM = 64
NS = 128
KW = 4
DSSM = 1536

eps_norm = 1e-05
rope_base = 100000000000.0
mask_fill_value = -1e30
highest = lax.Precision.HIGHEST
MESH_AXES = ("ctx", "wshard")
small_cost = pl.CostEstimate(flops=1024, bytes_accessed=1024, transcendentals=0)


def exchange(block, ctx_flip, shard_flip):
    blocks, shards = lax.axis_size("ctx"), lax.axis_size("wshard")
    route = [
        (c * shards + w, (c ^ ctx_flip) * shards + (w ^ shard_flip))
        for c in range(blocks)
        for w in range(shards)
    ]
    return lax.ppermute(block, MESH_AXES, route)


def from_behind(block, axis, distance):
    devices = range(lax.axis_size(axis))
    route = [(i - distance, i) for i in devices if i - distance in devices]
    return lax.ppermute(block, axis, route)


def swap_mirrored(block):
    count = lax.axis_size("ctx")
    return lax.ppermute(block, "ctx", [(i, count - 1 - i) for i in range(count)])


def tie_body(*refs):
    pass


def tie(value, *after):
    anywhere = pl.BlockSpec(memory_space=pl.ANY)
    return pl.pallas_call(
        tie_body,
        in_specs=[anywhere] * (1 + len(after)),
        out_specs=anywhere,
        out_shape=jax.ShapeDtypeStruct(value.shape, value.dtype),
        input_output_aliases={0: 0},
        cost_estimate=pl.CostEstimate(flops=0, bytes_accessed=0, transcendentals=0),
        name="tie",
    )(value, *after)


def assemble_body(spans, target_ref, *refs):
    out_ref = refs[len(spans)]
    step = pl.program_id(0)
    for piece, (first, size) in zip(refs, spans):

        def put(piece=piece):
            out_ref[...] = piece[...]

        pl.when((step >= first) & (step < first + size))(put)


def assemble(pieces, rows):
    spans, offsets, targets = [], [], []
    for _, source, start, size in pieces:
        spans.append((len(targets), size // rows))
        offsets.append(source // rows)
        targets += [start // rows + at for at in range(size // rows)]
    columns, kind = pieces[0][0].shape[1], pieces[0][0].dtype

    def source_map(offset, first, size):
        return lambda i, target: (offset + jnp.clip(i - first, 0, size - 1), 0)

    return pl.pallas_call(
        partial(assemble_body, spans),
        grid_spec=pltpu.PrefetchScalarGridSpec(
            num_scalar_prefetch=1,
            grid=(len(targets),),
            in_specs=[
                pl.BlockSpec((rows, columns), source_map(offset, first, size))
                for offset, (first, size) in zip(offsets, spans)
            ],
            out_specs=pl.BlockSpec((rows, columns), lambda i, target: (target[i], 0)),
        ),
        out_shape=jax.ShapeDtypeStruct((rows * len(targets), columns), kind),
        compiler_params=pltpu.CompilerParams(
            dimension_semantics=("arbitrary",), vmem_limit_bytes=32 * 1024 * 1024
        ),
        cost_estimate=small_cost,
        name="assemble",
    )(jnp.stack([jnp.asarray(target, jnp.int32) for target in targets]), *[p[0] for p in pieces])


def gather_first(shard, rows):
    part = rows // 4
    w = lax.axis_index("wshard")
    side = lax.axis_index("ctx") % 2
    direct = shard[2 * part :]
    across = exchange(lax.dynamic_slice_in_dim(shard, side * part, part, 0), 0, 2)
    across_direct = exchange(direct, 0, 2)
    beside = exchange(shard, 0, 1)
    across_relayed = exchange(across, 1, 0)
    far, far_direct, far_relayed = (
        exchange(piece, 0, 1) for piece in (across, across_direct, across_relayed)
    )
    pieces = [(shard, 0, w * rows, rows), (beside, 0, (w ^ 1) * rows, rows)]
    for flip, early, late, rest in (
        (2, across, across_relayed, across_direct),
        (3, far, far_relayed, far_direct),
    ):
        start = (w ^ flip) * rows
        pieces.append((early, 0, start + side * part, part))
        pieces.append((late, 0, start + (1 - side) * part, part))
        pieces.append((rest, 0, start + 2 * part, 2 * part))
    tails = [shard[rows:], beside[rows:], across_direct[2 * part :], far_direct[2 * part :]]
    tails = jnp.concatenate([tail[:1] for tail in tails], axis=0)
    small = jnp.concatenate(
        [lax.dynamic_slice_in_dim(tails, w ^ at, 1, 0) for at in range(4)], axis=0
    )
    return assemble(pieces, part), small, across_direct


def start_shards(stacked, after):
    stacked, _ = lax.optimization_barrier((stacked, after))
    return stacked, exchange(stacked, 0, 1), exchange(stacked, 0, 2)


def finish_shards(pieces, sizes, after):
    own, beside, across = pieces
    far = exchange(lax.optimization_barrier((across, after))[0], 0, 1)
    w = lax.axis_index("wshard")
    wholes, source = [], 0
    for size in sizes:
        wholes.append(
            assemble(
                [
                    (part, source, (w ^ flip) * size, size)
                    for flip, part in enumerate((own, beside, across, far))
                ],
                size,
            )
        )
        source += size
    return wholes


def add_low(first, *others):
    total = first.astype(jnp.float32)
    for other in others:
        total = total + other.astype(jnp.float32)
    return total.astype(jnp.bfloat16)


def lay_side_by_side(blocks, rows):
    parts = []
    for block in blocks:
        for start in range(0, block.shape[0], rows):
            part = block[start : start + rows]
            parts.append(jnp.pad(part, ((0, rows - part.shape[0]), (0, 0))))
    return jnp.concatenate(parts, axis=1)


def take_apart(array, shapes):
    rows, start, blocks = array.shape[0], 0, []
    for height, columns in shapes:
        parts = []
        for _ in range(0, height, rows):
            parts.append(array[: min(height, rows), start : start + columns])
            start += columns
        blocks.append(parts[0] if len(parts) == 1 else jnp.concatenate(parts, axis=0))
    return blocks


def ctx_half(blocks, rows):
    side = lax.axis_index("ctx") % 2
    whole = lay_side_by_side(blocks, rows)
    half = rows // 2
    got = exchange(lax.dynamic_slice_in_dim(whole, (1 - side) * half, half, 0), 1, 0)
    return add_low(lax.dynamic_slice_in_dim(whole, side * half, half, 0), got), got


def ctx_lines():
    count = lax.axis_size("ctx")
    return [list(range(start, count, 2)) for start in range(2)]


def ctx_finish(mine, shapes, turn_at):
    side = lax.axis_index("ctx") % 2
    lines = ctx_lines()
    if turn_at % 2:
        lines = lines[::-1]
    if turn_at // 2:
        lines = [line[::-1] for line in lines]
    mine = lax.psum(mine, "ctx", axis_index_groups=lines)
    summed = mine
    got = exchange(mine, 1, 0)
    whole = jnp.where(
        side == 0, jnp.concatenate([mine, got], axis=0), jnp.concatenate([got, mine], axis=0)
    ).astype(jnp.float32)
    return take_apart(whole, shapes), summed


def shard_pieces(array, axis):
    w = lax.axis_index("wshard")
    size = array.shape[axis] // 4

    def piece(flip):
        return lax.dynamic_slice_in_dim(array, (w ^ flip) * size, size, axis)

    return jnp.concatenate([piece(1), piece(3)], axis=axis), piece(2), piece(0)


def shard_sum(beside, across, own):
    rows = own.shape[0]
    got = exchange(beside.astype(jnp.bfloat16), 0, 1)
    got_across = exchange(add_low(across, got[rows:]), 0, 2)
    return add_low(own, got[:rows], got_across), got, got_across


def split_products(left, right, axis=1):
    return [
        lax.dot_general(
            piece, right, (((1 - axis,), (0,)), ((), ())), preferred_element_type=jnp.float32
        )
        for piece in shard_pieces(left, axis)
    ]


def weight_grad(left, right):
    return shard_sum(*split_products(left, right))


def mixed_dot(left, right):
    return jnp.dot(left, right, preferred_element_type=jnp.float32)


def rms_scale(value, gain):
    return value * lax.rsqrt(jnp.mean(value * value, axis=-1, keepdims=True) + eps_norm) * gain


def doc_numbers(lengths, position_index):
    ends = jnp.cumsum(lengths)[:-1]
    tally_count = jnp.sum((position_index[:, None] >= ends[None, :]).astype(jnp.int32), axis=1)
    return jnp.where(position_index >= 0, tally_count, -1)


def turn(value, position_index):
    half = value.shape[-2] // 2
    freq = rope_base ** (-jnp.arange(half, dtype=jnp.float32) / half)
    angle = freq[:, None] * position_index.astype(jnp.float32)[None, :]
    cosine = jnp.cos(angle)
    sine = jnp.sin(angle)
    first = value[..., :half, :]
    second = value[..., half:, :]
    return jnp.concatenate(
        [first * cosine - second * sine, second * cosine + first * sine], axis=-2
    )


def conv_local(taps, extended, weight, bias):
    tally_count = extended.shape[0] - (KW - 1)
    total = bias[None, :]
    for tap in range(KW):
        total = (
            total + weight[tap][None, :] * extended[tap : tap + tally_count] * taps[tap][:, None]
        )
    return jax.nn.silu(total)


def gate_norm(mixed, gate_z, gain):
    return rms_scale(mixed * jax.nn.silu(gate_z), gain)


def swiglu(gate_up_v):
    return jax.nn.silu(gate_up_v[:, :FF]) * gate_up_v[:, FF:]


def split_three(value):
    high = value.astype(jnp.bfloat16)
    rest = value - high.astype(jnp.float32)
    middle = rest.astype(jnp.bfloat16)
    low = (rest - middle.astype(jnp.float32)).astype(jnp.bfloat16)
    return [high, middle, low]


def nt_dot(left, right):
    return lax.dot_general(left, right, (((1,), (1,)), ((), ())), preferred_element_type=jnp.float32)


def causal_tile(scores, group, width):
    rows = lax.broadcasted_iota(jnp.int32, scores.shape, 0)
    columns = lax.broadcasted_iota(jnp.int32, scores.shape, 1)
    return jnp.where(rows <= lax.rem(columns, width) + group * width, scores, mask_fill_value)


def load_extended(extended, group, lower, value_ref, side, extra):
    width = value_ref.shape[2]
    extended[group] = jnp.zeros(extended.shape[1:], extended.dtype)
    for head in range(value_ref.shape[0]):
        here = slice(head * width, (head + 1) * width)
        extended[group, lower : lower + HEAD_SIZE, here] = value_ref[head]
    side = jnp.concatenate([side.astype(jnp.float32)] * value_ref.shape[0], axis=1)
    if extra is not None:
        row = lax.broadcasted_iota(jnp.int32, side.shape, 0)
        for at, part in enumerate(split_three(-extra)):
            side = jnp.where(row == 8 + at, part.astype(jnp.float32), side)
    extended[group, 128:144, :] = side.astype(extended.dtype)


def attend_forward_body(width, blocks, pair_ref, side_ref, query_a, query_b, query_side_ref, *refs):
    heads_refs, (log_ref, query_x, peak, total) = refs[-6:-4], refs[-4:]
    step = pl.program_id(1)

    @pl.when(step == 0)
    def start():
        for group, query_ref in enumerate((query_a, query_b)):
            load_extended(query_x, group, 0, query_ref, query_side_ref[group], None)
        peak[...] = jnp.full(peak.shape, mask_fill_value, jnp.float32)
        total[...] = jnp.zeros(total.shape, jnp.float32)

    @pl.when(step <= jnp.maximum(blocks[0], blocks[1]))
    def work():
        keys = jnp.concatenate([pair_ref[0, 0], side_ref[...]], axis=1)
        values = keys.T[HEAD_SIZE:144]

        def tile(group, masked):
            scores = mixed_dot(keys, query_x[group])
            if masked:
                scores = causal_tile(scores, group, width)
            old = peak[group]
            new = jnp.maximum(old, jnp.max(scores, axis=0, keepdims=True))
            probs = jnp.exp(scores - new)
            total[group] = total[group] * jnp.exp(old - new) + mixed_dot(
                values, probs.astype(jnp.bfloat16)
            )
            peak[group] = new

        for group in range(2):
            pl.when(step < blocks[group])(partial(tile, group, False))
            pl.when(step == blocks[group])(partial(tile, group, True))

    @pl.when(step == pl.num_programs(1) - 1)
    def finish():
        for group in range(2):
            weight = total[group, HEAD_SIZE + 8 : HEAD_SIZE + 9, :]
            heads = total[group, :HEAD_SIZE, :] / weight
            for head in range(heads.shape[1] // width):
                heads_refs[group][head] = heads[:, head * width : (head + 1) * width]
            log_ref[group, 0] = peak[group] + jnp.log(weight)


def attend_backward_body(
    width,
    blocks,
    pair_ref,
    side_ref,
    query_a,
    query_b,
    query_side_ref,
    log_ref,
    heads_a,
    heads_b,
    grad_a,
    grad_b,
    *refs,
):
    query_grad_refs, (pair_grad_ref, query_x, grad_x, pair_acc, query_acc) = refs[-7:-5], refs[-5:]
    step = pl.program_id(1)

    @pl.when(step == 0)
    def start():
        groups = ((query_a, heads_a, grad_a), (query_b, heads_b, grad_b))
        for group, (query_ref, heads_ref, grad_ref) in enumerate(groups):
            load_extended(query_x, group, 0, query_ref, query_side_ref[group], log_ref[group, 0])
            delta = [
                jnp.sum(heads_ref[head] * grad_ref[head].astype(jnp.float32), axis=0, keepdims=True)
                for head in range(heads_ref.shape[0])
            ]
            blank = jnp.zeros(query_side_ref.shape[1:], jnp.float32)
            load_extended(
                grad_x, group, HEAD_SIZE, grad_ref, blank, jnp.concatenate(delta, axis=1)
            )
        query_acc[...] = jnp.zeros(query_acc.shape, jnp.float32)

    pair_acc[...] = jnp.zeros(pair_acc.shape, jnp.float32)

    @pl.when(step <= jnp.maximum(blocks[0], blocks[1]))
    def work():
        pair = pair_ref[0, 0]
        keys = jnp.concatenate([pair, side_ref[...]], axis=1)
        turned = pair.T[:HEAD_SIZE]

        def tile(group, masked):
            scores = mixed_dot(keys, query_x[group])
            if masked:
                scores = causal_tile(scores, group, width)
            probs = jnp.exp(scores)
            low = (probs * mixed_dot(keys, grad_x[group])).astype(jnp.bfloat16)
            pair_acc[...] += nt_dot(low, query_x[group, :128, :]) + nt_dot(
                probs.astype(jnp.bfloat16), grad_x[group, :128, :]
            )
            query_acc[group] += mixed_dot(turned, low)

        for group in range(2):
            pl.when(step < blocks[group])(partial(tile, group, False))
            pl.when(step == blocks[group])(partial(tile, group, True))

    pair_grad_ref[0, 0] = pair_acc[...].astype(jnp.bfloat16)

    @pl.when(step == pl.num_programs(1) - 1)
    def finish():
        for group in range(2):
            for head in range(query_acc.shape[2] // width):
                query_grad_refs[group][head] = query_acc[group, :, head * width : (head + 1) * width]


def attention_calls(rows, count, anchors):
    width = rows // 2
    span = width * (QUERY_HEADS // KEY_VALUE_HEADS)

    def last(blocks):
        return jnp.maximum(blocks[0], blocks[1])

    pair_spec = pl.BlockSpec(
        (1, 1, rows, 128), lambda g, k, blocks: (jnp.minimum(k, last(blocks)), g, 0, 0)
    )
    side_spec = pl.BlockSpec((rows, 128), lambda g, k, blocks: (jnp.minimum(k, last(blocks)), 0))

    heads_per_group = QUERY_HEADS // KEY_VALUE_HEADS
    own = pl.BlockSpec((heads_per_group, HEAD_SIZE, width), lambda g, k, blocks: (g, 0, 0))
    half_spec = own
    log_spec = pl.BlockSpec((2, 1, 1, span), lambda g, k, blocks: (0, g, 0, 0))
    query_side_spec = pl.BlockSpec((2, 16, width), lambda g, k, blocks: (0, 0, 0))
    half_shape = jax.ShapeDtypeStruct((QUERY_HEADS, HEAD_SIZE, width), jnp.float32)

    anywhere = pl.BlockSpec(memory_space=pl.ANY)
    params = pltpu.CompilerParams(
        dimension_semantics=("arbitrary", "arbitrary"), vmem_limit_bytes=48 * 1024 * 1024
    )
    forward = pl.pallas_call(
        partial(attend_forward_body, width),
        grid_spec=pltpu.PrefetchScalarGridSpec(
            num_scalar_prefetch=1,
            grid=(KEY_VALUE_HEADS, count),
            in_specs=[pair_spec, side_spec, own, half_spec, query_side_spec]
            + [anywhere] * anchors[0],
            out_specs=[half_spec, half_spec, log_spec],
            scratch_shapes=[
                pltpu.VMEM((2, 256, span), jnp.bfloat16),
                pltpu.VMEM((2, 1, span), jnp.float32),
                pltpu.VMEM((2, 144 - HEAD_SIZE, span), jnp.float32),
            ],
        ),
        out_shape=[
            half_shape,
            half_shape,
            jax.ShapeDtypeStruct((2, KEY_VALUE_HEADS, 1, span), jnp.float32),
        ],
        compiler_params=params,
        cost_estimate=small_cost,
        name="attend_forward",
    )
    backward = pl.pallas_call(
        partial(attend_backward_body, width),
        grid_spec=pltpu.PrefetchScalarGridSpec(
            num_scalar_prefetch=1,
            grid=(KEY_VALUE_HEADS, count),
            in_specs=[
                pair_spec,
                side_spec,
                own,
                half_spec,
                query_side_spec,
                log_spec,
                half_spec,
                half_spec,
                own,
                half_spec,
            ]
            + [anywhere] * anchors[1],
            out_specs=[
                half_spec,
                half_spec,
                pl.BlockSpec((1, 1, rows, 128), lambda g, k, blocks: (k, g, 0, 0)),
            ],
            scratch_shapes=[
                pltpu.VMEM((2, 256, span), jnp.bfloat16),
                pltpu.VMEM((2, 256, span), jnp.bfloat16),
                pltpu.VMEM((rows, 128), jnp.float32),
                pltpu.VMEM((2, HEAD_SIZE, span), jnp.float32),
            ],
        ),
        out_shape=[
            half_shape,
            half_shape,
            jax.ShapeDtypeStruct((count, KEY_VALUE_HEADS, rows, 128), jnp.bfloat16),
        ],
        compiler_params=params,
        cost_estimate=small_cost,
        name="attend_backward",
    )
    return forward, backward


def pick(pair):
    lane = lax.broadcasted_iota(jnp.int32, (pair.shape[0], 2 * PM), 1)
    return jnp.where(lane < PM, pair[:, 0:1], pair[:, 1:2])


def outer_body(kind, rows_ref, left_ref, right_ref, *refs):
    out_ref = refs[-1]
    for at in range(rows_ref.shape[0]):
        scale = pick(rows_ref[at].T[:, kind : kind + 2])
        left = left_ref[:, at * 128 : (at + 1) * 128].astype(jnp.float32) * scale
        out_ref[at * 128 : (at + 1) * 128, :] = lax.dot_general(
            left.astype(jnp.bfloat16),
            right_ref[...],
            (((0,), (0,)), ((), ())),
            preferred_element_type=jnp.float32,
        ).astype(out_ref.dtype)


def join_body(c_ref, rows_ref, state_ref, local_ref, *refs):
    out_ref = refs[-1]
    for at in range(rows_ref.shape[0]):
        here = slice(at * 2 * PM, (at + 1) * 2 * PM)
        inner = nt_dot(c_ref[...], state_ref[here, :])
        out_ref[:, here] = local_ref[:, here] + inner * pick(rows_ref[at].T[:, 2:4])


def mixed_body(
    skip_ref, x_ref, b_ref, c_ref, row_ref, docs_column, docs_row, out_ref, fill, products
):
    rows = x_ref.shape[0]
    half = rows // 2

    @pl.when(pl.program_id(0) == 0)
    def start():
        at = lax.broadcasted_iota(jnp.int32, (rows, rows), 0)
        source = lax.broadcasted_iota(jnp.int32, (rows, rows), 1)
        same = (at >= source) & (docs_column[...] == docs_row[...])
        fill[...] = jnp.where(same, 0.0, mask_fill_value)
        products[...] = nt_dot(c_ref[...], b_ref[...])

    x = x_ref[...]
    columns = row_ref[0].T
    lane = lax.broadcasted_iota(jnp.int32, (half, 2 * PM), 1)
    for block in range(2):
        here = slice(block * half, (block + 1) * half)
        width = (block + 1) * half
        parts = []
        for head in range(2):
            decay = jnp.exp(
                (columns[here, head : head + 1] - row_ref[0, head : head + 1, :width])
                + fill[here, :width]
            )
            weights = (products[here, :width] * decay).astype(jnp.bfloat16)
            parts.append(mixed_dot(weights, x[:width]))
        local = jnp.where(lane < PM, parts[0], parts[1])
        out_ref[here, :] = local + x[here].astype(jnp.float32) * skip_ref[0]


def mixed_grad_body(
    skip_ref,
    x_ref,
    b_ref,
    c_ref,
    row_ref,
    docs_column,
    docs_row,
    state_ref,
    state_grad_ref,
    grad_ref,
    *refs,
):
    out_ref, skip_grad_ref, fill, products, scores, b_grad, c_grad = refs[-7:]
    rows = x_ref.shape[0]
    half = rows // 2
    step = pl.program_id(0)
    pairs = HM // 2

    @pl.when(step == 0)
    def start():
        source = lax.broadcasted_iota(jnp.int32, (rows, rows), 0)
        at = lax.broadcasted_iota(jnp.int32, (rows, rows), 1)
        same = (at >= source) & (docs_column[...] == docs_row[...])
        fill[...] = jnp.where(same, 0.0, mask_fill_value)
        products[...] = nt_dot(b_ref[...], c_ref[...])
        scores[...] = jnp.zeros(scores.shape, jnp.float32)
        b_grad[...] = jnp.zeros(b_grad.shape, jnp.float32)
        c_grad[...] = jnp.zeros(c_grad.shape, jnp.float32)

    @pl.when(step < pairs)
    def work():
        x = x_ref[...]
        x_f = x.astype(jnp.float32)
        grad = grad_ref[...]
        low = grad.astype(jnp.bfloat16)
        lane = lax.broadcasted_iota(jnp.int32, (half, 2 * PM), 1)
        lane_all = lax.broadcasted_iota(jnp.int32, (rows, 2 * PM), 1)
        skip_grad_ref[0] = jnp.sum(grad * x_f, axis=0, keepdims=True)
        state_grad = state_grad_ref[...]
        columns = row_ref[0].T
        tail = pick(columns[:, 4:6])
        b_grad[...] += mixed_dot((x_f * tail).astype(jnp.bfloat16), state_grad)
        entered = (low.astype(jnp.float32) * pick(columns[:, 2:4])).astype(jnp.bfloat16)
        c_grad[...] += mixed_dot(entered, state_ref[...])
        passed = nt_dot(b_ref[...], state_grad) * tail + grad * skip_ref[0]
        chosen = [
            jnp.where((lane_all < PM) == (head == 0), x_f, 0.0).astype(jnp.bfloat16)
            for head in range(2)
        ]
        for block in range(2):
            here = slice(block * half, (block + 1) * half)
            start_at = block * half
            parts = []
            for head in range(2):
                decay = jnp.exp(
                    (row_ref[0, head : head + 1, start_at:] - columns[here, head : head + 1])
                    + fill[here, start_at:]
                )
                weights = (products[here, start_at:] * decay).astype(jnp.bfloat16)
                parts.append(mixed_dot(weights, low[start_at:]))
                scores[here, start_at:] += nt_dot(chosen[head][here], low[start_at:]) * decay
            out_ref[here, :] = jnp.where(lane < PM, parts[0], parts[1]) + passed[here]

    @pl.when(step == pairs)
    def give_b():
        out_ref[...] = b_grad[...] + mixed_dot(scores[...].astype(jnp.bfloat16), c_ref[...])

    @pl.when(step == pairs + 1)
    def give_c():
        out_ref[...] = c_grad[...] + lax.dot_general(
            scores[...].astype(jnp.bfloat16),
            b_ref[...],
            (((0,), (0,)), ((), ())),
            preferred_element_type=jnp.float32,
        )


def mixer_calls(rows, anchors):
    pairs = HM // 2
    wide = 2 * PM
    params = pltpu.CompilerParams(
        dimension_semantics=("arbitrary",), vmem_limit_bytes=48 * 1024 * 1024
    )

    def capped(p):
        return jnp.minimum(p, pairs - 1)

    anywhere = pl.BlockSpec(memory_space=pl.ANY)

    def join(after):
        each = 4
        wide_spec = pl.BlockSpec((rows, each * wide), lambda p: (0, p))
        return pl.pallas_call(
            join_body,
            grid=(pairs // each,),
            in_specs=[
                pl.BlockSpec((rows, NS), lambda p: (0, DSSM // NS + 1)),
                pl.BlockSpec((each, 8, rows), lambda p: (p, 0, 0)),
                pl.BlockSpec((each * wide, NS), lambda p: (p, 0)),
                wide_spec,
            ]
            + [anywhere] * after,
            out_specs=wide_spec,
            out_shape=jax.ShapeDtypeStruct((rows, DSSM), jnp.float32),
            compiler_params=params,
            cost_estimate=small_cost,
            name="mixer_join",
        )

    def outer(right_at, kind, after):
        each = 2
        return pl.pallas_call(
            partial(outer_body, kind),
            grid=(pairs // each,),
            in_specs=[
                pl.BlockSpec((each, 8, rows), lambda p: (p, 0, 0)),
                pl.BlockSpec((rows, each * wide), lambda p: (0, p)),
                pl.BlockSpec((rows, NS), lambda p: (0, right_at)),
            ]
            + [anywhere] * after,
            out_specs=pl.BlockSpec((each * wide, NS), lambda p: (p, 0)),
            out_shape=jax.ShapeDtypeStruct((DSSM, NS), jnp.bfloat16),
            compiler_params=params,
            cost_estimate=small_cost,
            name="state_outer",
        )

    x_spec = pl.BlockSpec((rows, wide), lambda p: (0, capped(p)))
    b_spec = pl.BlockSpec((rows, NS), lambda p: (0, DSSM // NS))
    c_spec = pl.BlockSpec((rows, NS), lambda p: (0, DSSM // NS + 1))
    row_spec = pl.BlockSpec((1, 8, rows), lambda p: (capped(p), 0, 0))
    skip_spec = pl.BlockSpec((1, 1, wide), lambda p: (capped(p), 0, 0))
    state_spec = pl.BlockSpec((wide, NS), lambda p: (capped(p), 0))
    docs_specs = [pl.BlockSpec((rows, 1), lambda p: (0, 0)), pl.BlockSpec((1, rows), lambda p: (0, 0))]
    square = pltpu.VMEM((rows, rows), jnp.float32)
    narrow = pltpu.VMEM((rows, NS), jnp.float32)
    forward = pl.pallas_call(
        mixed_body,
        grid=(pairs,),
        in_specs=[skip_spec, x_spec, b_spec, c_spec, row_spec] + docs_specs,
        out_specs=pl.BlockSpec((rows, wide), lambda p: (0, p)),
        out_shape=jax.ShapeDtypeStruct((rows, DSSM), jnp.float32),
        scratch_shapes=[square, square],
        compiler_params=params,
        cost_estimate=small_cost,
        name="mixer_forward",
    )
    backward = pl.pallas_call(
        mixed_grad_body,
        grid=(pairs + 2,),
        in_specs=[skip_spec, x_spec, b_spec, c_spec, row_spec]
        + docs_specs
        + [state_spec, state_spec, x_spec]
        + [anywhere] * anchors,
        out_specs=[
            pl.BlockSpec((rows, wide), lambda p: (0, p)),
            pl.BlockSpec((1, 1, wide), lambda p: (capped(p), 0, 0)),
        ],
        out_shape=[
            jax.ShapeDtypeStruct((rows, DSSM + 2 * NS), jnp.float32),
            jax.ShapeDtypeStruct((pairs, 1, wide), jnp.float32),
        ],
        scratch_shapes=[square, square, square, narrow, narrow],
        compiler_params=params,
        cost_estimate=small_cost,
        name="mixer_backward",
    )
    return outer, join, forward, backward


def gain_rows(gain):
    return jnp.pad(jnp.stack(split_three(gain)), ((0, 13), (0, NS - HM)))


def read_gain(rows):
    return jnp.sum(rows[..., :3, :HM].astype(jnp.float32), axis=-2)


def pass_state(part, gain, gains, reverse):
    count, position = lax.axis_size("ctx"), lax.axis_index("ctx")
    side, line_at = position % 2, position // 2
    is_first = (side == 1) if reverse else (side == 0)

    def by_head(array):
        return array.reshape(array.shape[:-2] + (HM, PM, NS)).astype(jnp.float32)

    got = exchange(part if gains else jnp.concatenate([part, gain_rows(gain)], axis=0), 1, 0)
    if gains:
        gain, other, line_gains = gains
    else:
        other = read_gain(got[DSSM:])
    own_f, got_f = by_head(part), by_head(got[:DSSM])
    first = jnp.where(is_first, own_f, got_f)
    second = jnp.where(is_first, got_f, own_f)
    first_gain = jnp.where(is_first, gain, other)[:, None, None]
    second_gain = jnp.where(is_first, other, gain)[:, None, None]
    total = (second_gain * first + second).astype(jnp.bfloat16).reshape(DSSM, NS)
    if not gains:
        total = jnp.concatenate([total, gain_rows(gain * other)], axis=0)
    totals = lax.all_gather(total, "ctx", axis_index_groups=ctx_lines())
    if not gains:
        line_gains = read_gain(totals[:, DSSM:])
    totals = by_head(totals[:, :DSSM])
    factor = jnp.ones((HM,), jnp.float32)
    entering = jnp.zeros((HM, PM, NS), jnp.float32)
    lines = range(count // 2)
    for at in lines if reverse else reversed(lines):
        reached = at > line_at if reverse else at < line_at
        entering = entering + jnp.where(reached, factor, 0.0)[:, None, None] * totals[at]
        factor = factor * jnp.where(reached, line_gains[at], 1.0)
    state = jnp.where(is_first, entering, first_gain * entering + first)
    return state.astype(jnp.bfloat16).reshape(DSSM, NS), (gain, other, line_gains)


def pack_small(norm, conv_weight, conv_bias, skip, mixer, ffn, shards):
    pieces = [
        norm.reshape(shards, -1),
        conv_weight.reshape(KW, shards, -1).transpose(1, 0, 2).reshape(shards, -1),
        conv_bias.reshape(shards, -1),
        mixer.reshape(shards, -1),
        ffn.reshape(shards, -1),
        skip.reshape(shards, -1),
    ]
    packed = jnp.concatenate(pieces, axis=1)
    packed = jnp.pad(packed, ((0, 0), (0, 4096 - packed.shape[1])))
    return packed.reshape(shards * 32, 128)


def unpack_small(packed, model, channels, heads, shards):
    packed = packed.reshape(shards, 4096)
    sizes = [model, KW * channels, channels, DSSM, model, heads]
    parts, start = [], 0
    for size in sizes:
        width = size // 4
        parts.append(packed[:, start : start + width])
        start += width
    norm, conv_weight, conv_bias, mixer, ffn, skip = parts
    conv_weight = conv_weight.reshape(shards, KW, -1).transpose(1, 0, 2).reshape(KW, -1)
    return (
        norm.reshape(-1),
        conv_weight,
        conv_bias.reshape(-1),
        skip.reshape(-1),
        mixer.reshape(-1),
        ffn.reshape(-1),
    )


def per_device(
    tokens,
    cotangent,
    doc_lengths,
    decay,
    norm_gain,
    in_proj,
    conv_weight,
    conv_bias,
    skip_gain,
    mixer_gain,
    mixer_out,
    query_proj,
    key_value_projection,
    attn_out,
    ffn_gain,
    gate_up,
    down_proj,
):
    rows, model = tokens.shape[1:]
    width = rows // 2
    shards = lax.axis_size("wshard")
    channels = conv_bias.shape[0] * shards
    count, block_at = lax.axis_size("ctx"), lax.axis_index("ctx")
    sequence_total = rows * count
    heads_per_group = QUERY_HEADS // KEY_VALUE_HEADS
    scale = HEAD_SIZE ** (-0.5)
    attend_forward, attend_backward = attention_calls(rows, count, (2, 2))
    state_outer, mixer_join, mixer_forward, mixer_backward = mixer_calls(rows, 4)

    packed = pack_small(norm_gain, conv_weight, conv_bias, skip_gain, mixer_gain, ffn_gain, 1)
    first_shard = jnp.concatenate([in_proj, query_proj, key_value_projection], axis=1)
    packed = jnp.pad(packed.reshape(1, -1), ((0, 15), (0, first_shard.shape[1] - 4096)))
    first_w, small, arrived = gather_first(
        jnp.concatenate([first_shard, packed], axis=0), in_proj.shape[0]
    )
    norm_w, conv_w, conv_b, skip_w, mixer_g, ffn_g = (
        part.astype(jnp.float32)
        for part in unpack_small(small[:, :4096], model, channels, HM, shards)
    )
    projected_width = in_proj.shape[1]
    in_w, attn_pair_w = first_w[:, :projected_width], first_w[:, projected_width:]
    out_pieces = start_shards(
        jnp.concatenate([mixer_out, attn_out, down_proj], axis=0), arrived
    )
    gate_up_pieces = start_shards(gate_up, arrived)
    query_w = attn_pair_w[:, : QUERY_HEADS * HEAD_SIZE]
    keyval_w = attn_pair_w[:, QUERY_HEADS * HEAD_SIZE :]

    lengths = doc_lengths[0]
    doc_count = lengths.shape[0]
    position_index = block_at * rows + jnp.arange(rows, dtype=jnp.int32)
    docs = doc_numbers(lengths, position_index)
    doc_prev = doc_numbers(lengths, position_index[:1] - 1)[0]
    log_decay = jnp.log(decay[0])
    source = tokens[0].astype(jnp.float32)
    normed, norm_pull = jax.vjp(rms_scale, source, norm_w)
    normed_b = normed.astype(jnp.bfloat16)

    turned_q = turn(
        lax.dot_general(
            query_w, normed_b, (((0,), (1,)), ((), ())), preferred_element_type=jnp.float32
        ).reshape(QUERY_HEADS, HEAD_SIZE, rows),
        position_index,
    ).astype(jnp.bfloat16)
    key_value_pair = lax.dot_general(
        keyval_w, normed_b, (((0,), (1,)), ((), ())), preferred_element_type=jnp.float32
    ).reshape(2, KEY_VALUE_HEADS, HEAD_SIZE, rows)
    keys_b = turn(key_value_pair[0], position_index).astype(jnp.bfloat16)
    values_b = key_value_pair[1].astype(jnp.bfloat16)
    pairs = lax.all_gather(
        jnp.concatenate([keys_b, values_b], axis=1).transpose(0, 2, 1), "ctx"
    )

    turned_q = turned_q * jnp.asarray(scale, jnp.bfloat16)
    mirrored_q = swap_mirrored(turned_q[:, :, width:])
    mirrored = count - 1 - block_at
    group_blocks = jnp.stack([block_at, mirrored]).astype(jnp.int32)
    group_positions = jnp.stack(
        [
            block_at * rows + jnp.arange(width, dtype=jnp.int32),
            mirrored * rows + width + jnp.arange(width, dtype=jnp.int32),
        ]
    )
    group_docs = jnp.stack([doc_numbers(lengths, group_positions[at]) for at in range(2)])
    key_docs = doc_numbers(lengths, jnp.arange(sequence_total, dtype=jnp.int32))
    lane = jnp.arange(128)[None, :]
    key_side = ((key_docs[:, None] == lane) | ((lane >= 8) & (lane < 11))).astype(jnp.bfloat16)
    side_row = jnp.arange(16)[None, :, None]
    query_side = jnp.where(
        (side_row == group_docs[:, None, :]) | (side_row >= doc_count), 0.0, mask_fill_value
    ).astype(jnp.bfloat16)

    projected = mixed_dot(normed_b, in_w)
    gate_z = projected[:, :DSSM]
    pre_b = projected[:, DSSM:].astype(jnp.bfloat16)
    rim = from_behind(pre_b[rows - (KW - 1) :], "ctx", 1)
    extended = jnp.concatenate([rim, pre_b], axis=0).astype(jnp.float32)
    taps = jnp.stack(
        [
            (doc_numbers(lengths, position_index - (KW - 1) + tap) == docs).astype(jnp.float32)
            for tap in range(KW)
        ]
    )
    conv_f, conv_pull = jax.vjp(partial(conv_local, taps), extended, conv_w, conv_b)
    conv_b16 = conv_f.astype(jnp.bfloat16)
    order = jnp.arange(rows)
    running = jnp.dot(
        log_decay, (order[:, None] <= order[None, :]).astype(jnp.float32), precision=highest
    )
    entry = jnp.where((docs == doc_prev)[None, :], jnp.exp(running), 0.0)
    tail = jnp.where((docs == docs[-1])[None, :], jnp.exp(running[:, -1:] - running), 0.0)
    carry_gain = jnp.where(docs[-1] == doc_prev, jnp.exp(running[:, -1]), 0.0)

    mixer_rows = (
        jnp.stack([running, entry, tail, jnp.zeros_like(tail)])
        .reshape(4, HM // 2, 2, rows)
        .transpose(1, 0, 2, 3)
        .reshape(HM // 2, 8, rows)
    )
    skip_wide = jnp.repeat(skip_w, PM).reshape(HM // 2, 1, 2 * PM)
    docs_column, docs_row = docs[:, None], docs[None, :]
    fresh = state_outer(DSSM // NS, 4, 0)(mixer_rows, conv_b16, conv_b16)
    state_in, gains = pass_state(fresh, carry_gain, None, False)
    local = mixer_forward(
        skip_wide, conv_b16, conv_b16, conv_b16, mixer_rows, docs_column, docs_row
    )

    heads_own, heads_mirrored, log_x = attend_forward(
        group_blocks,
        pairs,
        key_side,
        turned_q,
        mirrored_q,
        query_side,
        out_pieces[1],
        gate_up_pieces[1],
    )
    mixer_w, attn_w, down_w = finish_shards(
        out_pieces,
        [mixer_out.shape[0], attn_out.shape[0], down_proj.shape[0]],
        log_x,
    )
    (gate_up_w,) = finish_shards(gate_up_pieces, [gate_up.shape[0]], log_x)
    heads_back = swap_mirrored(heads_mirrored.astype(jnp.bfloat16))
    heads_t = jnp.concatenate([heads_own.astype(jnp.bfloat16), heads_back], axis=2).reshape(
        QUERY_HEADS * HEAD_SIZE, rows
    )
    mixed = mixer_join(0)(conv_b16, mixer_rows, state_in, local)
    gated, gate_pull = jax.vjp(gate_norm, mixed, gate_z, mixer_g)
    gated_b = gated.astype(jnp.bfloat16)
    mamba = mixed_dot(gated_b, mixer_w)
    attn = lax.dot_general(
        heads_t, attn_w, (((0,), (0,)), ((), ())), preferred_element_type=jnp.float32
    )
    middle = source + attn + mamba
    normed2, ffn_pull = jax.vjp(rms_scale, middle, ffn_g)
    normed2_b = normed2.astype(jnp.bfloat16)
    gate_up_v = mixed_dot(normed2_b, gate_up_w)
    activated, act_pull = jax.vjp(swiglu, gate_up_v)
    activated_b = activated.astype(jnp.bfloat16)
    layer_out = (middle + mixed_dot(activated_b, down_w)).astype(jnp.bfloat16)

    out_low = cotangent[0]
    down_sum, down_beside, down_across = weight_grad(activated_b, out_low)
    down_half, down_got = ctx_half([down_sum], model // shards)
    (gate_up_grad_v,) = act_pull(nt_dot(out_low, down_w))
    gate_up_low = gate_up_grad_v.astype(jnp.bfloat16)
    gate_up_sum, gate_up_beside, gate_up_across = weight_grad(normed2_b, gate_up_low)
    gate_up_half, gate_up_got = ctx_half([gate_up_sum], model // shards)
    middle_norm_grad, ffn_gain_grad = ffn_pull(nt_dot(gate_up_low, gate_up_w))
    middle_grad = out_low.astype(jnp.float32) + middle_norm_grad
    middle_low = middle_grad.astype(jnp.bfloat16)
    heads_low = nt_dot(attn_w, middle_low).astype(jnp.bfloat16)
    heads_low = heads_low.reshape(QUERY_HEADS, HEAD_SIZE, rows)
    mirrored_low = swap_mirrored(heads_low[:, :, width:])
    gated_grad = nt_dot(middle_low, mixer_w)
    mixed_grad, gate_z_grad, mixer_gain_grad = gate_pull(gated_grad)
    upward = state_outer(DSSM // NS + 1, 2, 1)(
        mixer_rows, mixed_grad.astype(jnp.bfloat16), conv_b16, down_beside
    )
    state_out_grad, _ = pass_state(upward, None, gains, True)
    gate_z_low = gate_z_grad.astype(jnp.bfloat16)
    mixer_products = split_products(gated_b, middle_low)
    attn_products = split_products(heads_t, middle_low, 0)
    shard_sizes = [mixer_out.shape[0], attn_out.shape[0]]

    def interleaved(parts):
        return jnp.concatenate(
            [
                part[start * size : (start + 1) * size]
                for start in range(parts[0].shape[0] // shard_sizes[0])
                for part, size in zip(parts, shard_sizes)
            ],
            axis=0,
        ).astype(jnp.bfloat16)

    mixer_attn_sum, mixer_beside, mixer_across = shard_sum(
        *[interleaved(parts) for parts in zip(mixer_products, attn_products)]
    )
    in_sum_z, in_z_beside, in_z_across = weight_grad(normed_b, gate_z_low)
    mixer_half, mixer_got = ctx_half([mixer_attn_sum, in_sum_z], model // shards)

    query_grad_own, query_grad_mirrored, pairs_grad = attend_backward(
        group_blocks,
        pairs,
        key_side,
        turned_q,
        mirrored_q,
        query_side,
        log_x,
        heads_own,
        heads_mirrored,
        heads_low,
        mirrored_low,
        gate_up_beside,
        down_across,
    )
    pair_grad = (
        lax.psum_scatter(pairs_grad, "ctx", scatter_dimension=0)
        .astype(jnp.float32)
        .transpose(0, 2, 1)
    )
    query_low_own, query_low_mirrored = (
        (turn(grad, -group_positions[at]) * scale).astype(jnp.bfloat16)
        for at, grad in enumerate((query_grad_own, query_grad_mirrored))
    )
    query_low = jnp.concatenate(
        [query_low_own, swap_mirrored(query_low_mirrored)], axis=2
    ).reshape(QUERY_HEADS * HEAD_SIZE, rows)

    conv_grad, skip_parts = mixer_backward(
        skip_wide,
        conv_b16,
        conv_b16,
        conv_b16,
        mixer_rows,
        docs_column,
        docs_row,
        state_in,
        state_out_grad,
        mixed_grad,
        gate_up_across,
        in_z_beside,
        down_got,
        mixer_beside,
    )
    skip_grad = jnp.sum(skip_parts.reshape(HM, PM), axis=1)
    extended_grad, conv_weight_grad, conv_bias_grad = conv_pull(conv_grad)
    from_above = from_behind(extended_grad[: KW - 1], "ctx", -1)
    pre_grad = extended_grad[KW - 1 :] + jnp.pad(from_above, ((rows - (KW - 1), 0), (0, 0)))
    pre_low = tie(pre_grad.astype(jnp.bfloat16), gate_up_got, in_z_across, mixer_across)
    in_sum_pre, _, _ = weight_grad(normed_b, pre_low)
    projected_low = jnp.concatenate([gate_z_low, pre_low], axis=1)
    normed_grad = nt_dot(projected_low, in_w)

    keys_low = turn(pair_grad[:, :HEAD_SIZE], -position_index)
    keyval_low = jnp.concatenate(
        [
            keys_low.reshape(KEY_VALUE_HEADS * HEAD_SIZE, rows),
            pair_grad[:, HEAD_SIZE:].reshape(KEY_VALUE_HEADS * HEAD_SIZE, rows),
        ],
        axis=0,
    ).astype(jnp.bfloat16)
    attn_pair_low = jnp.concatenate([query_low, keyval_low], axis=0).T
    attn_pair_sum, _, _ = weight_grad(normed_b, attn_pair_low)
    normed_grad = normed_grad + nt_dot(attn_pair_low, attn_pair_w)
    source_grad, norm_grad = norm_pull(normed_grad)
    tokens_grad = (middle_grad + source_grad)[None]

    small_grad = pack_small(
        norm_grad, conv_weight_grad, conv_bias_grad, skip_grad, mixer_gain_grad, ffn_gain_grad, shards
    )
    small_sum, _, _ = shard_sum(*shard_pieces(small_grad, 0))
    last_half, _ = ctx_half([in_sum_pre, attn_pair_sum, small_sum], model // shards)
    (down_share,), summed = ctx_finish(down_half, [down_sum.shape], 0)
    (gate_up_share,), summed = ctx_finish(tie(gate_up_half, summed), [gate_up_sum.shape], 1)
    (mixer_attn_share, in_share_z), summed = ctx_finish(
        tie(mixer_half, summed), [mixer_attn_sum.shape, in_sum_z.shape], 2
    )
    mixer_share = mixer_attn_share[: mixer_out.shape[0]]
    attn_share = mixer_attn_share[mixer_out.shape[0] :]
    (in_share_pre, attn_pair_share, small_share), _ = ctx_finish(
        tie(last_half, summed),
        [in_sum_pre.shape, attn_pair_sum.shape, small_sum.shape],
        3,
    )
    norm_share, conv_w_share, conv_b_share, skip_share, mixer_g_share, ffn_share = unpack_small(
        small_share, model, channels, HM, 1
    )
    return (
        layer_out[None],
        tokens_grad,
        norm_share,
        jnp.concatenate([in_share_z, in_share_pre], axis=1),
        conv_w_share,
        conv_b_share,
        skip_share,
        mixer_g_share,
        mixer_share,
        attn_pair_share[:, : QUERY_HEADS * HEAD_SIZE],
        attn_pair_share[:, QUERY_HEADS * HEAD_SIZE :],
        attn_share,
        ffn_share,
        gate_up_share,
        down_share,
    )


def solution(mesh):
    in_specs = (
        P("wshard", "ctx", None),
        P("wshard", "ctx", None),
        P("wshard", None),
        P("wshard", None, "ctx"),
        P("wshard"),
        P("wshard", None),
        P(None, "wshard"),
        P("wshard"),
        P("wshard"),
        P("wshard"),
        P("wshard", None),
        P("wshard", None),
        P("wshard", None),
        P("wshard", None),
        P("wshard"),
        P("wshard", None),
        P("wshard", None),
    )
    out_specs = (
        P("wshard", "ctx", None),
        P("wshard", "ctx", None),
        P("wshard"),
        P("wshard", None),
        P(None, "wshard"),
        P("wshard"),
        P("wshard"),
        P("wshard"),
        P("wshard", None),
        P("wshard", None),
        P("wshard", None),
        P("wshard", None),
        P("wshard"),
        P("wshard", None),
        P("wshard", None),
    )
    return jax.shard_map(
        per_device, mesh=mesh, in_specs=in_specs, out_specs=out_specs, check_vma=False
    )
```

```python
from functools import partial

import jax
import jax.numpy as jnp
from jax import lax
from jax.experimental import pallas as pl
from jax.experimental.pallas import tpu as pltpu
from jax.sharding import PartitionSpec as P

FF = 2048
QUERY_HEADS = 8
KEY_VALUE_HEADS = 2
HEAD_SIZE = 64
HM = 24
PM = 64
NS = 128
KW = 4
DSSM = 1536

eps_norm = 1e-05
rope_base = 100000000000.0
mask_fill_value = -1e30
highest = lax.Precision.HIGHEST
MESH_AXES = ("ctx", "wshard")
small_cost = pl.CostEstimate(flops=1024, bytes_accessed=1024, transcendentals=0)


def exchange(block, ctx_flip, shard_flip):
    blocks, shards = lax.axis_size("ctx"), lax.axis_size("wshard")
    route = [
        (c * shards + w, (c ^ ctx_flip) * shards + (w ^ shard_flip))
        for c in range(blocks)
        for w in range(shards)
    ]
    return lax.ppermute(block, MESH_AXES, route)


def from_behind(block, axis, distance):
    devices = range(lax.axis_size(axis))
    route = [(i - distance, i) for i in devices if i - distance in devices]
    return lax.ppermute(block, axis, route)


def swap_mirrored(block):
    count = lax.axis_size("ctx")
    return lax.ppermute(block, "ctx", [(i, count - 1 - i) for i in range(count)])


def tie_body(*refs):
    pass


def tie(value, *after):
    anywhere = pl.BlockSpec(memory_space=pl.ANY)
    return pl.pallas_call(
        tie_body,
        in_specs=[anywhere] * (1 + len(after)),
        out_specs=anywhere,
        out_shape=jax.ShapeDtypeStruct(value.shape, value.dtype),
        input_output_aliases={0: 0},
        cost_estimate=pl.CostEstimate(flops=0, bytes_accessed=0, transcendentals=0),
        name="tie",
    )(value, *after)


def assemble_body(spans, target_ref, *refs):
    out_ref = refs[-1]
    step = pl.program_id(0)
    for piece, (first, size) in zip(refs, spans):

        def put(piece=piece):
            out_ref[...] = piece[...]

        pl.when((step >= first) & (step < first + size))(put)


def assemble(pieces, rows, anchors=()):
    spans, offsets, targets = [], [], []
    for _, source, start, size in pieces:
        spans.append((len(targets), size // rows))
        offsets.append(source // rows)
        targets += [start // rows + at for at in range(size // rows)]
    columns, kind = pieces[0][0].shape[1], pieces[0][0].dtype

    def source_map(offset, first, size):
        return lambda i, target: (offset + jnp.clip(i - first, 0, size - 1), 0)

    return pl.pallas_call(
        partial(assemble_body, spans),
        grid_spec=pltpu.PrefetchScalarGridSpec(
            num_scalar_prefetch=1,
            grid=(len(targets),),
            in_specs=[
                pl.BlockSpec((rows, columns), source_map(offset, first, size))
                for offset, (first, size) in zip(offsets, spans)
            ]
            + [pl.BlockSpec(memory_space=pl.ANY)] * len(anchors),
            out_specs=pl.BlockSpec((rows, columns), lambda i, target: (target[i], 0)),
        ),
        out_shape=jax.ShapeDtypeStruct((rows * len(targets), columns), kind),
        compiler_params=pltpu.CompilerParams(
            dimension_semantics=("arbitrary",), vmem_limit_bytes=32 * 1024 * 1024
        ),
        cost_estimate=small_cost,
        name="assemble",
    )(jnp.stack([jnp.asarray(target, jnp.int32) for target in targets]), *[p[0] for p in pieces], *anchors)


def gather_first(shard, rows, anchors):
    part = rows // 4
    w = lax.axis_index("wshard")
    side = lax.axis_index("ctx") % 2
    direct = shard[2 * part :]
    across = exchange(lax.dynamic_slice_in_dim(shard, side * part, part, 0), 0, 2)
    across_direct = exchange(direct, 0, 2)
    beside = exchange(shard, 0, 1)
    across_relayed = exchange(across, 1, 0)
    far, far_direct, far_relayed = (
        exchange(piece, 0, 1) for piece in (across, across_direct, across_relayed)
    )
    pieces = [(shard, 0, w * rows, rows), (beside, 0, (w ^ 1) * rows, rows)]
    for flip, early, late, rest in (
        (2, across, across_relayed, across_direct),
        (3, far, far_relayed, far_direct),
    ):
        start = (w ^ flip) * rows
        pieces.append((early, 0, start + side * part, part))
        pieces.append((late, 0, start + (1 - side) * part, part))
        pieces.append((rest, 0, start + 2 * part, 2 * part))
    tails = [shard[rows:], beside[rows:], across_direct[2 * part :], far_direct[2 * part :]]
    tails = jnp.concatenate([tail[:1] for tail in tails], axis=0)
    small = jnp.concatenate(
        [lax.dynamic_slice_in_dim(tails, w ^ at, 1, 0) for at in range(4)], axis=0
    )
    return assemble(pieces, part, anchors), small, across_direct


def start_shards(stacked, after):
    stacked, _ = lax.optimization_barrier((stacked, after))
    return stacked, exchange(stacked, 0, 1), exchange(stacked, 0, 2)


def finish_shards(pieces, sizes, after):
    own, beside, across = pieces
    far = exchange(lax.optimization_barrier((across, after))[0], 0, 1)
    w = lax.axis_index("wshard")
    wholes, source = [], 0
    for size in sizes:
        wholes.append(
            assemble(
                [
                    (part, source, (w ^ flip) * size, size)
                    for flip, part in enumerate((own, beside, across, far))
                ],
                size,
            )
        )
        source += size
    return wholes


def add_low(first, *others):
    total = first.astype(jnp.float32)
    for other in others:
        total = total + other.astype(jnp.float32)
    return total.astype(jnp.bfloat16)


def lay_side_by_side(blocks, rows):
    parts = []
    for block in blocks:
        for start in range(0, block.shape[0], rows):
            part = block[start : start + rows]
            parts.append(jnp.pad(part, ((0, rows - part.shape[0]), (0, 0))))
    return jnp.concatenate(parts, axis=1)


def take_apart(array, shapes):
    rows, start, blocks = array.shape[0], 0, []
    for height, columns in shapes:
        parts = []
        for _ in range(0, height, rows):
            parts.append(array[: min(height, rows), start : start + columns])
            start += columns
        blocks.append(parts[0] if len(parts) == 1 else jnp.concatenate(parts, axis=0))
    return blocks


def ctx_half(blocks, rows):
    side = lax.axis_index("ctx") % 2
    whole = lay_side_by_side(blocks, rows)
    half = rows // 2
    got = exchange(lax.dynamic_slice_in_dim(whole, (1 - side) * half, half, 0), 1, 0)
    return add_low(lax.dynamic_slice_in_dim(whole, side * half, half, 0), got), got


def ctx_lines():
    count = lax.axis_size("ctx")
    return [list(range(start, count, 2)) for start in range(2)]


def ctx_finish(mine, shapes, turn_at):
    side = lax.axis_index("ctx") % 2
    lines = ctx_lines()
    if turn_at % 2:
        lines = lines[::-1]
    if turn_at // 2:
        lines = [line[::-1] for line in lines]
    mine = lax.psum(mine, "ctx", axis_index_groups=lines)
    summed = mine
    got = exchange(mine, 1, 0)
    whole = jnp.where(
        side == 0, jnp.concatenate([mine, got], axis=0), jnp.concatenate([got, mine], axis=0)
    ).astype(jnp.float32)
    return take_apart(whole, shapes), summed


def shard_pieces(array, axis):
    w = lax.axis_index("wshard")
    size = array.shape[axis] // 4

    def piece(flip):
        return lax.dynamic_slice_in_dim(array, (w ^ flip) * size, size, axis)

    return jnp.concatenate([piece(1), piece(3)], axis=axis), piece(2), piece(0)


def shard_sum(beside, across, own, after=None):
    rows = own.shape[0]
    got = exchange(beside.astype(jnp.bfloat16), 0, 1)
    across = add_low(across, got[rows:])
    got_across = exchange(across if after is None else tie(across, after), 0, 2)
    return add_low(own, got[:rows], got_across), got, got_across


def split_products(left, right, axis=1):
    return [
        lax.dot_general(
            piece, right, (((1 - axis,), (0,)), ((), ())), preferred_element_type=jnp.float32
        )
        for piece in shard_pieces(left, axis)
    ]


def weight_grad(left, right, after=None):
    return shard_sum(*split_products(left, right), after)


def sum_small(value):
    rows = value.shape[0] // 4
    for flip in (1, 2):
        value = value + exchange(value, 0, flip)
    value = lax.dynamic_slice_in_dim(value, lax.axis_index("wshard") * rows, rows, 0)
    bit = 1
    while bit < lax.axis_size("ctx"):
        value = value + exchange(value, bit, 0)
        bit *= 2
    return value


def scatter_blocks(blocks):
    position, bit = lax.axis_index("ctx"), 1
    while blocks.shape[0] > 1:
        up = (position // bit) % 2
        halves = blocks.reshape((blocks.shape[0] // 2, 2) + blocks.shape[1:])
        keep = lax.dynamic_index_in_dim(halves, up, 1, keepdims=False)
        give = lax.dynamic_index_in_dim(halves, 1 - up, 1, keepdims=False)
        blocks = add_low(keep, exchange(give, bit, 0))
        bit *= 2
    return blocks[0]


def mixed_dot(left, right):
    return jnp.dot(left, right, preferred_element_type=jnp.float32)


def rms_scale(value, gain):
    return value * lax.rsqrt(jnp.mean(value * value, axis=-1, keepdims=True) + eps_norm) * gain


def doc_numbers(lengths, position_index):
    ends = jnp.cumsum(lengths)[:-1]
    tally_count = jnp.sum((position_index[:, None] >= ends[None, :]).astype(jnp.int32), axis=1)
    return jnp.where(position_index >= 0, tally_count, -1)


def turn_tables(position_index):
    half = HEAD_SIZE // 2
    freq = rope_base ** (-jnp.arange(half, dtype=jnp.float32) / half)
    angle = freq[:, None] * position_index.astype(jnp.float32)[None, :]
    return jnp.cos(angle), jnp.sin(angle)


def turn(value, cosine, sine):
    half = value.shape[-2] // 2
    first = value[..., :half, :]
    second = value[..., half:, :]
    return jnp.concatenate(
        [first * cosine - second * sine, second * cosine + first * sine], axis=-2
    )


def conv_local(taps, extended, weight, bias):
    tally_count = extended.shape[0] - (KW - 1)
    total = bias[None, :]
    for tap in range(KW):
        total = (
            total + weight[tap][None, :] * extended[tap : tap + tally_count] * taps[tap][:, None]
        )
    return jax.nn.silu(total)


def gate_norm(mixed, gate_z, gain):
    return rms_scale(mixed * jax.nn.silu(gate_z), gain)


def swiglu(gate_up_v):
    return jax.nn.silu(gate_up_v[:, :FF]) * gate_up_v[:, FF:]


def split_three(value):
    high = value.astype(jnp.bfloat16)
    rest = value - high.astype(jnp.float32)
    middle = rest.astype(jnp.bfloat16)
    low = (rest - middle.astype(jnp.float32)).astype(jnp.bfloat16)
    return [high, middle, low]


def nt_dot(left, right):
    return lax.dot_general(left, right, (((1,), (1,)), ((), ())), preferred_element_type=jnp.float32)


def causal_tile(scores, group, width):
    rows = lax.broadcasted_iota(jnp.int32, scores.shape, 0)
    columns = lax.broadcasted_iota(jnp.int32, scores.shape, 1)
    return jnp.where(rows <= lax.rem(columns, width) + group * width, scores, mask_fill_value)


def load_extended(extended, group, lower, value_ref, side, extra):
    width = value_ref.shape[2]
    extended[group] = jnp.zeros(extended.shape[1:], extended.dtype)
    for head in range(value_ref.shape[0]):
        here = slice(head * width, (head + 1) * width)
        extended[group, lower : lower + HEAD_SIZE, here] = value_ref[head]
    side = jnp.concatenate([side.astype(jnp.float32)] * value_ref.shape[0], axis=1)
    if extra is not None:
        row = lax.broadcasted_iota(jnp.int32, side.shape, 0)
        for at, part in enumerate(split_three(-extra)):
            side = jnp.where(row == 8 + at, part.astype(jnp.float32), side)
    extended[group, 128:144, :] = side.astype(extended.dtype)


def attend_forward_body(width, blocks, pair_ref, side_ref, query_a, query_b, query_side_ref, *refs):
    heads_refs, (log_ref, query_x, peak, total) = refs[-6:-4], refs[-4:]
    step = pl.program_id(1)

    @pl.when(step == 0)
    def start():
        for group, query_ref in enumerate((query_a, query_b)):
            load_extended(query_x, group, 0, query_ref, query_side_ref[group], None)
        peak[...] = jnp.full(peak.shape, mask_fill_value, jnp.float32)
        total[...] = jnp.zeros(total.shape, jnp.float32)

    @pl.when(step <= jnp.maximum(blocks[0], blocks[1]))
    def work():
        keys = jnp.concatenate([pair_ref[0, 0], side_ref[...]], axis=1)
        values = keys.T[HEAD_SIZE:144]

        def tile(group, masked):
            scores = mixed_dot(keys, query_x[group])
            if masked:
                scores = causal_tile(scores, group, width)
            old = peak[group]
            new = jnp.maximum(old, jnp.max(scores, axis=0, keepdims=True))
            probs = jnp.exp(scores - new)
            total[group] = total[group] * jnp.exp(old - new) + mixed_dot(
                values, probs.astype(jnp.bfloat16)
            )
            peak[group] = new

        for group in range(2):
            pl.when(step < blocks[group])(partial(tile, group, False))
            pl.when(step == blocks[group])(partial(tile, group, True))

    @pl.when(step == pl.num_programs(1) - 1)
    def finish():
        for group in range(2):
            weight = total[group, HEAD_SIZE + 8 : HEAD_SIZE + 9, :]
            heads = total[group, :HEAD_SIZE, :] / weight
            for head in range(heads.shape[1] // width):
                heads_refs[group][head] = heads[:, head * width : (head + 1) * width]
            log_ref[group, 0] = peak[group] + jnp.log(weight)


def attend_backward_body(
    width,
    blocks,
    pair_ref,
    side_ref,
    query_a,
    query_b,
    query_side_ref,
    log_ref,
    heads_a,
    heads_b,
    grad_a,
    grad_b,
    *refs,
):
    query_grad_refs, (pair_grad_ref, query_x, grad_x, pair_acc, query_acc) = refs[-7:-5], refs[-5:]
    step = pl.program_id(1)

    @pl.when(step == 0)
    def start():
        groups = ((query_a, heads_a, grad_a), (query_b, heads_b, grad_b))
        for group, (query_ref, heads_ref, grad_ref) in enumerate(groups):
            load_extended(query_x, group, 0, query_ref, query_side_ref[group], log_ref[group, 0])
            delta = [
                jnp.sum(heads_ref[head] * grad_ref[head].astype(jnp.float32), axis=0, keepdims=True)
                for head in range(heads_ref.shape[0])
            ]
            blank = jnp.zeros(query_side_ref.shape[1:], jnp.float32)
            load_extended(
                grad_x, group, HEAD_SIZE, grad_ref, blank, jnp.concatenate(delta, axis=1)
            )
        query_acc[...] = jnp.zeros(query_acc.shape, jnp.float32)

    pair_acc[...] = jnp.zeros(pair_acc.shape, jnp.float32)

    @pl.when(step <= jnp.maximum(blocks[0], blocks[1]))
    def work():
        pair = pair_ref[0, 0]
        keys = jnp.concatenate([pair, side_ref[...]], axis=1)
        turned = pair.T[:HEAD_SIZE]

        def tile(group, masked):
            scores = mixed_dot(keys, query_x[group])
            if masked:
                scores = causal_tile(scores, group, width)
            probs = jnp.exp(scores)
            low = (probs * mixed_dot(keys, grad_x[group])).astype(jnp.bfloat16)
            pair_acc[...] += nt_dot(low, query_x[group, :128, :]) + nt_dot(
                probs.astype(jnp.bfloat16), grad_x[group, :128, :]
            )
            query_acc[group] += mixed_dot(turned, low)

        for group in range(2):
            pl.when(step < blocks[group])(partial(tile, group, False))
            pl.when(step == blocks[group])(partial(tile, group, True))

    pair_grad_ref[0, 0] = pair_acc[...].astype(jnp.bfloat16)

    @pl.when(step == pl.num_programs(1) - 1)
    def finish():
        for group in range(2):
            for head in range(query_acc.shape[2] // width):
                query_grad_refs[group][head] = query_acc[group, :, head * width : (head + 1) * width]


def attention_calls(rows, count, anchors):
    width = rows // 2
    span = width * (QUERY_HEADS // KEY_VALUE_HEADS)

    def last(blocks):
        return jnp.maximum(blocks[0], blocks[1])

    pair_spec = pl.BlockSpec(
        (1, 1, rows, 128), lambda g, k, blocks: (jnp.minimum(k, last(blocks)), g, 0, 0)
    )
    side_spec = pl.BlockSpec((rows, 128), lambda g, k, blocks: (jnp.minimum(k, last(blocks)), 0))

    heads_per_group = QUERY_HEADS // KEY_VALUE_HEADS
    own = pl.BlockSpec((heads_per_group, HEAD_SIZE, width), lambda g, k, blocks: (g, 0, 0))
    half_spec = own
    log_spec = pl.BlockSpec((2, 1, 1, span), lambda g, k, blocks: (0, g, 0, 0))
    query_side_spec = pl.BlockSpec((2, 16, width), lambda g, k, blocks: (0, 0, 0))
    half_shape = jax.ShapeDtypeStruct((QUERY_HEADS, HEAD_SIZE, width), jnp.float32)

    anywhere = pl.BlockSpec(memory_space=pl.ANY)
    params = pltpu.CompilerParams(
        dimension_semantics=("arbitrary", "arbitrary"), vmem_limit_bytes=48 * 1024 * 1024
    )
    forward = pl.pallas_call(
        partial(attend_forward_body, width),
        grid_spec=pltpu.PrefetchScalarGridSpec(
            num_scalar_prefetch=1,
            grid=(KEY_VALUE_HEADS, count),
            in_specs=[pair_spec, side_spec, own, half_spec, query_side_spec]
            + [anywhere] * anchors[0],
            out_specs=[half_spec, half_spec, log_spec],
            scratch_shapes=[
                pltpu.VMEM((2, 256, span), jnp.bfloat16),
                pltpu.VMEM((2, 1, span), jnp.float32),
                pltpu.VMEM((2, 144 - HEAD_SIZE, span), jnp.float32),
            ],
        ),
        out_shape=[
            half_shape,
            half_shape,
            jax.ShapeDtypeStruct((2, KEY_VALUE_HEADS, 1, span), jnp.float32),
        ],
        compiler_params=params,
        cost_estimate=small_cost,
        name="attend_forward",
    )
    backward = pl.pallas_call(
        partial(attend_backward_body, width),
        grid_spec=pltpu.PrefetchScalarGridSpec(
            num_scalar_prefetch=1,
            grid=(KEY_VALUE_HEADS, count),
            in_specs=[
                pair_spec,
                side_spec,
                own,
                half_spec,
                query_side_spec,
                log_spec,
                half_spec,
                half_spec,
                own,
                half_spec,
            ]
            + [anywhere] * anchors[1],
            out_specs=[
                half_spec,
                half_spec,
                pl.BlockSpec((1, 1, rows, 128), lambda g, k, blocks: (k, g, 0, 0)),
            ],
            scratch_shapes=[
                pltpu.VMEM((2, 256, span), jnp.bfloat16),
                pltpu.VMEM((2, 256, span), jnp.bfloat16),
                pltpu.VMEM((rows, 128), jnp.float32),
                pltpu.VMEM((2, HEAD_SIZE, span), jnp.float32),
            ],
        ),
        out_shape=[
            half_shape,
            half_shape,
            jax.ShapeDtypeStruct((count, KEY_VALUE_HEADS, rows, 128), jnp.bfloat16),
        ],
        compiler_params=params,
        cost_estimate=small_cost,
        name="attend_backward",
    )
    return forward, backward


def pick(pair):
    lane = lax.broadcasted_iota(jnp.int32, (pair.shape[0], 2 * PM), 1)
    return jnp.where(lane < PM, pair[:, 0:1], pair[:, 1:2])


def outer_body(kind, rows_ref, left_ref, right_ref, *refs):
    out_ref = refs[-1]
    for at in range(rows_ref.shape[0]):
        scale = pick(rows_ref[at].T[:, kind : kind + 2])
        left = left_ref[:, at * 128 : (at + 1) * 128].astype(jnp.float32) * scale
        out_ref[at * 128 : (at + 1) * 128, :] = lax.dot_general(
            left.astype(jnp.bfloat16),
            right_ref[...],
            (((0,), (0,)), ((), ())),
            preferred_element_type=jnp.float32,
        ).astype(out_ref.dtype)


def join_body(c_ref, rows_ref, state_ref, local_ref, *refs):
    out_ref = refs[-1]
    for at in range(rows_ref.shape[0]):
        here = slice(at * 2 * PM, (at + 1) * 2 * PM)
        inner = nt_dot(c_ref[...], state_ref[here, :])
        out_ref[:, here] = local_ref[:, here] + inner * pick(rows_ref[at].T[:, 2:4])


def mixed_body(
    skip_ref, x_ref, b_ref, c_ref, row_ref, docs_column, docs_row, out_ref, fill, products
):
    rows = x_ref.shape[0]
    half = rows // 2

    @pl.when(pl.program_id(0) == 0)
    def start():
        at = lax.broadcasted_iota(jnp.int32, (rows, rows), 0)
        source = lax.broadcasted_iota(jnp.int32, (rows, rows), 1)
        same = (at >= source) & (docs_column[...] == docs_row[...])
        fill[...] = jnp.where(same, 0.0, mask_fill_value)
        products[...] = nt_dot(c_ref[...], b_ref[...])

    x = x_ref[...]
    columns = row_ref[0].T
    lane = lax.broadcasted_iota(jnp.int32, (half, 2 * PM), 1)
    for block in range(2):
        here = slice(block * half, (block + 1) * half)
        width = (block + 1) * half
        parts = []
        for head in range(2):
            decay = jnp.exp(
                (columns[here, head : head + 1] - row_ref[0, head : head + 1, :width])
                + fill[here, :width]
            )
            weights = (products[here, :width] * decay).astype(jnp.bfloat16)
            parts.append(mixed_dot(weights, x[:width]))
        local = jnp.where(lane < PM, parts[0], parts[1])
        out_ref[here, :] = local + x[here].astype(jnp.float32) * skip_ref[0]


def mixed_grad_body(
    skip_ref,
    x_ref,
    b_ref,
    c_ref,
    row_ref,
    docs_column,
    docs_row,
    state_ref,
    state_grad_ref,
    grad_ref,
    *refs,
):
    out_ref, skip_grad_ref, fill, products, scores, b_grad, c_grad = refs[-7:]
    rows = x_ref.shape[0]
    half = rows // 2
    step = pl.program_id(0)
    pairs = HM // 2

    @pl.when(step == 0)
    def start():
        source = lax.broadcasted_iota(jnp.int32, (rows, rows), 0)
        at = lax.broadcasted_iota(jnp.int32, (rows, rows), 1)
        same = (at >= source) & (docs_column[...] == docs_row[...])
        fill[...] = jnp.where(same, 0.0, mask_fill_value)
        products[...] = nt_dot(b_ref[...], c_ref[...])
        scores[...] = jnp.zeros(scores.shape, jnp.float32)
        b_grad[...] = jnp.zeros(b_grad.shape, jnp.float32)
        c_grad[...] = jnp.zeros(c_grad.shape, jnp.float32)

    @pl.when(step < pairs)
    def work():
        x = x_ref[...]
        x_f = x.astype(jnp.float32)
        grad = grad_ref[...]
        low = grad.astype(jnp.bfloat16)
        lane = lax.broadcasted_iota(jnp.int32, (half, 2 * PM), 1)
        lane_all = lax.broadcasted_iota(jnp.int32, (rows, 2 * PM), 1)
        skip_grad_ref[0] = jnp.sum(grad * x_f, axis=0, keepdims=True)
        state_grad = state_grad_ref[...]
        columns = row_ref[0].T
        tail = pick(columns[:, 4:6])
        b_grad[...] += mixed_dot((x_f * tail).astype(jnp.bfloat16), state_grad)
        entered = (low.astype(jnp.float32) * pick(columns[:, 2:4])).astype(jnp.bfloat16)
        c_grad[...] += mixed_dot(entered, state_ref[...])
        passed = nt_dot(b_ref[...], state_grad) * tail + grad * skip_ref[0]
        chosen = [
            jnp.where((lane_all < PM) == (head == 0), x_f, 0.0).astype(jnp.bfloat16)
            for head in range(2)
        ]
        for block in range(2):
            here = slice(block * half, (block + 1) * half)
            start_at = block * half
            parts = []
            for head in range(2):
                decay = jnp.exp(
                    (row_ref[0, head : head + 1, start_at:] - columns[here, head : head + 1])
                    + fill[here, start_at:]
                )
                weights = (products[here, start_at:] * decay).astype(jnp.bfloat16)
                parts.append(mixed_dot(weights, low[start_at:]))
                scores[here, start_at:] += nt_dot(chosen[head][here], low[start_at:]) * decay
            out_ref[here, :] = jnp.where(lane < PM, parts[0], parts[1]) + passed[here]

    @pl.when(step == pairs)
    def give_b():
        out_ref[...] = b_grad[...] + mixed_dot(scores[...].astype(jnp.bfloat16), c_ref[...])

    @pl.when(step == pairs + 1)
    def give_c():
        out_ref[...] = c_grad[...] + lax.dot_general(
            scores[...].astype(jnp.bfloat16),
            b_ref[...],
            (((0,), (0,)), ((), ())),
            preferred_element_type=jnp.float32,
        )


def mixer_calls(rows, anchors):
    pairs = HM // 2
    wide = 2 * PM
    params = pltpu.CompilerParams(
        dimension_semantics=("arbitrary",), vmem_limit_bytes=48 * 1024 * 1024
    )

    def capped(p):
        return jnp.minimum(p, pairs - 1)

    anywhere = pl.BlockSpec(memory_space=pl.ANY)

    def join(after):
        each = 4
        wide_spec = pl.BlockSpec((rows, each * wide), lambda p: (0, p))
        return pl.pallas_call(
            join_body,
            grid=(pairs // each,),
            in_specs=[
                pl.BlockSpec((rows, NS), lambda p: (0, DSSM // NS + 1)),
                pl.BlockSpec((each, 8, rows), lambda p: (p, 0, 0)),
                pl.BlockSpec((each * wide, NS), lambda p: (p, 0)),
                wide_spec,
            ]
            + [anywhere] * after,
            out_specs=wide_spec,
            out_shape=jax.ShapeDtypeStruct((rows, DSSM), jnp.float32),
            compiler_params=params,
            cost_estimate=small_cost,
            name="mixer_join",
        )

    def outer(right_at, kind, after):
        each = 2
        return pl.pallas_call(
            partial(outer_body, kind),
            grid=(pairs // each,),
            in_specs=[
                pl.BlockSpec((each, 8, rows), lambda p: (p, 0, 0)),
                pl.BlockSpec((rows, each * wide), lambda p: (0, p)),
                pl.BlockSpec((rows, NS), lambda p: (0, right_at)),
            ]
            + [anywhere] * after,
            out_specs=pl.BlockSpec((each * wide, NS), lambda p: (p, 0)),
            out_shape=jax.ShapeDtypeStruct((DSSM, NS), jnp.bfloat16),
            compiler_params=params,
            cost_estimate=small_cost,
            name="state_outer",
        )

    x_spec = pl.BlockSpec((rows, wide), lambda p: (0, capped(p)))
    b_spec = pl.BlockSpec((rows, NS), lambda p: (0, DSSM // NS))
    c_spec = pl.BlockSpec((rows, NS), lambda p: (0, DSSM // NS + 1))
    row_spec = pl.BlockSpec((1, 8, rows), lambda p: (capped(p), 0, 0))
    skip_spec = pl.BlockSpec((1, 1, wide), lambda p: (capped(p), 0, 0))
    state_spec = pl.BlockSpec((wide, NS), lambda p: (capped(p), 0))
    docs_specs = [pl.BlockSpec((rows, 1), lambda p: (0, 0)), pl.BlockSpec((1, rows), lambda p: (0, 0))]
    square = pltpu.VMEM((rows, rows), jnp.float32)
    narrow = pltpu.VMEM((rows, NS), jnp.float32)
    forward = pl.pallas_call(
        mixed_body,
        grid=(pairs,),
        in_specs=[skip_spec, x_spec, b_spec, c_spec, row_spec] + docs_specs,
        out_specs=pl.BlockSpec((rows, wide), lambda p: (0, p)),
        out_shape=jax.ShapeDtypeStruct((rows, DSSM), jnp.float32),
        scratch_shapes=[square, square],
        compiler_params=params,
        cost_estimate=small_cost,
        name="mixer_forward",
    )
    backward = pl.pallas_call(
        mixed_grad_body,
        grid=(pairs + 2,),
        in_specs=[skip_spec, x_spec, b_spec, c_spec, row_spec]
        + docs_specs
        + [state_spec, state_spec, x_spec]
        + [anywhere] * anchors,
        out_specs=[
            pl.BlockSpec((rows, wide), lambda p: (0, p)),
            pl.BlockSpec((1, 1, wide), lambda p: (capped(p), 0, 0)),
        ],
        out_shape=[
            jax.ShapeDtypeStruct((rows, DSSM + 2 * NS), jnp.float32),
            jax.ShapeDtypeStruct((pairs, 1, wide), jnp.float32),
        ],
        scratch_shapes=[square, square, square, narrow, narrow],
        compiler_params=params,
        cost_estimate=small_cost,
        name="mixer_backward",
    )
    return outer, join, forward, backward


def gain_rows(gain):
    return jnp.pad(jnp.stack(split_three(gain)), ((0, 13), (0, NS - HM)))


def read_gain(rows):
    return jnp.sum(rows[..., :3, :HM].astype(jnp.float32), axis=-2)


def pass_state(part, gain, gains, reverse, after=None):
    count, position = lax.axis_size("ctx"), lax.axis_index("ctx")
    side, line_at = position % 2, position // 2
    is_first = (side == 1) if reverse else (side == 0)

    def by_head(array):
        return array.reshape(array.shape[:-2] + (HM, PM, NS)).astype(jnp.float32)

    got = exchange(part if gains else jnp.concatenate([part, gain_rows(gain)], axis=0), 1, 0)
    if gains:
        gain, other, line_gains = gains
    else:
        other = read_gain(got[DSSM:])
    own_f, got_f = by_head(part), by_head(got[:DSSM])
    first = jnp.where(is_first, own_f, got_f)
    second = jnp.where(is_first, got_f, own_f)
    first_gain = jnp.where(is_first, gain, other)[:, None, None]
    second_gain = jnp.where(is_first, other, gain)[:, None, None]
    total = (second_gain * first + second).astype(jnp.bfloat16).reshape(DSSM, NS)
    if not gains:
        total = jnp.concatenate([total, gain_rows(gain * other)], axis=0)
    if after is not None:
        total = tie(total, after)
    totals = lax.all_gather(total, "ctx", axis_index_groups=ctx_lines())
    if not gains:
        line_gains = read_gain(totals[:, DSSM:])
    totals = by_head(totals[:, :DSSM])
    factor = jnp.ones((HM,), jnp.float32)
    entering = jnp.zeros((HM, PM, NS), jnp.float32)
    lines = range(count // 2)
    for at in lines if reverse else reversed(lines):
        reached = at > line_at if reverse else at < line_at
        entering = entering + jnp.where(reached, factor, 0.0)[:, None, None] * totals[at]
        factor = factor * jnp.where(reached, line_gains[at], 1.0)
    state = jnp.where(is_first, entering, first_gain * entering + first)
    return state.astype(jnp.bfloat16).reshape(DSSM, NS), (gain, other, line_gains)


def pack_small(norm, conv_weight, conv_bias, skip, mixer, ffn, shards):
    pieces = [
        norm.reshape(shards, -1),
        conv_weight.reshape(KW, shards, -1).transpose(1, 0, 2).reshape(shards, -1),
        conv_bias.reshape(shards, -1),
        mixer.reshape(shards, -1),
        ffn.reshape(shards, -1),
        skip.reshape(shards, -1),
    ]
    packed = jnp.concatenate(pieces, axis=1)
    packed = jnp.pad(packed, ((0, 0), (0, 4096 - packed.shape[1])))
    return packed.reshape(shards * 32, 128)


def unpack_small(packed, model, channels, heads, shards):
    packed = packed.reshape(shards, 4096)
    sizes = [model, KW * channels, channels, DSSM, model, heads]
    parts, start = [], 0
    for size in sizes:
        width = size // 4
        parts.append(packed[:, start : start + width])
        start += width
    norm, conv_weight, conv_bias, mixer, ffn, skip = parts
    conv_weight = conv_weight.reshape(shards, KW, -1).transpose(1, 0, 2).reshape(KW, -1)
    return (
        norm.reshape(-1),
        conv_weight,
        conv_bias.reshape(-1),
        skip.reshape(-1),
        mixer.reshape(-1),
        ffn.reshape(-1),
    )


def per_device(
    tokens,
    cotangent,
    doc_lengths,
    decay,
    norm_gain,
    in_proj,
    conv_weight,
    conv_bias,
    skip_gain,
    mixer_gain,
    mixer_out,
    query_proj,
    key_value_projection,
    attn_out,
    ffn_gain,
    gate_up,
    down_proj,
):
    rows, model = tokens.shape[1:]
    width = rows // 2
    shards = lax.axis_size("wshard")
    channels = conv_bias.shape[0] * shards
    count, block_at = lax.axis_size("ctx"), lax.axis_index("ctx")
    sequence_total = rows * count
    heads_per_group = QUERY_HEADS // KEY_VALUE_HEADS
    scale = HEAD_SIZE ** (-0.5)
    attend_forward, attend_backward = attention_calls(rows, count, (2, 2))
    state_outer, mixer_join, mixer_forward, mixer_backward = mixer_calls(rows, 4)

    lengths = doc_lengths[0]
    doc_count = lengths.shape[0]
    position_index = block_at * rows + jnp.arange(rows, dtype=jnp.int32)
    docs = doc_numbers(lengths, position_index)
    doc_prev = doc_numbers(lengths, position_index[:1] - 1)[0]
    log_decay = jnp.log(decay[0])
    mirrored = count - 1 - block_at
    group_blocks = jnp.stack([block_at, mirrored]).astype(jnp.int32)
    group_positions = jnp.stack(
        [
            block_at * rows + jnp.arange(width, dtype=jnp.int32),
            mirrored * rows + width + jnp.arange(width, dtype=jnp.int32),
        ]
    )
    group_docs = jnp.stack([doc_numbers(lengths, group_positions[at]) for at in range(2)])
    key_docs = doc_numbers(lengths, jnp.arange(sequence_total, dtype=jnp.int32))
    lane = jnp.arange(128)[None, :]
    key_side = ((key_docs[:, None] == lane) | ((lane >= 8) & (lane < 11))).astype(jnp.bfloat16)
    side_row = jnp.arange(16)[None, :, None]
    query_side = jnp.where(
        (side_row == group_docs[:, None, :]) | (side_row >= doc_count), 0.0, mask_fill_value
    ).astype(jnp.bfloat16)

    order = jnp.arange(rows)
    running = jnp.dot(
        log_decay, (order[:, None] <= order[None, :]).astype(jnp.float32), precision=highest
    )
    entry = jnp.where((docs == doc_prev)[None, :], jnp.exp(running), 0.0)
    tail = jnp.where((docs == docs[-1])[None, :], jnp.exp(running[:, -1:] - running), 0.0)
    carry_gain = jnp.where(docs[-1] == doc_prev, jnp.exp(running[:, -1]), 0.0)

    mixer_rows = (
        jnp.stack([running, entry, tail, jnp.zeros_like(tail)])
        .reshape(4, HM // 2, 2, rows)
        .transpose(1, 0, 2, 3)
        .reshape(HM // 2, 8, rows)
    )
    taps = jnp.stack(
        [
            (doc_numbers(lengths, position_index - (KW - 1) + tap) == docs).astype(jnp.float32)
            for tap in range(KW)
        ]
    )
    docs_column, docs_row = docs[:, None], docs[None, :]
    cosine, sine = turn_tables(position_index)
    mirrored_cosine, mirrored_sine = turn_tables(group_positions[1])
    prepared = lax.optimization_barrier(
        (
            key_side,
            query_side,
            mixer_rows,
            taps,
            docs_column,
            docs_row,
            cosine,
            sine,
            mirrored_cosine,
            mirrored_sine,
            group_blocks,
        )
    )
    (
        key_side,
        query_side,
        mixer_rows,
        taps,
        docs_column,
        docs_row,
        cosine,
        sine,
        mirrored_cosine,
        mirrored_sine,
        group_blocks,
    ) = prepared
    packed = pack_small(norm_gain, conv_weight, conv_bias, skip_gain, mixer_gain, ffn_gain, 1)
    first_shard = jnp.concatenate([in_proj, query_proj, key_value_projection], axis=1)
    packed = jnp.pad(packed.reshape(1, -1), ((0, 15), (0, first_shard.shape[1] - 4096)))
    first_w, small, arrived = gather_first(
        jnp.concatenate([first_shard, packed], axis=0), in_proj.shape[0], prepared
    )
    norm_w, conv_w, conv_b, skip_w, mixer_g, ffn_g = (
        part.astype(jnp.float32)
        for part in unpack_small(small[:, :4096], model, channels, HM, shards)
    )
    projected_width = in_proj.shape[1]
    in_w, attn_pair_w = first_w[:, :projected_width], first_w[:, projected_width:]
    out_pieces = start_shards(
        jnp.concatenate([mixer_out, attn_out, down_proj], axis=0), arrived
    )
    gate_up_pieces = start_shards(gate_up, arrived)
    source = tokens[0].astype(jnp.float32)
    normed, norm_pull = jax.vjp(rms_scale, source, norm_w)
    normed_b = normed.astype(jnp.bfloat16)
    projected = mixed_dot(normed_b, first_w)

    query_width = QUERY_HEADS * HEAD_SIZE
    attn_inputs = projected[:, projected_width:].T
    turned_q = turn(
        attn_inputs[:query_width].reshape(QUERY_HEADS, HEAD_SIZE, rows), cosine, sine
    ).astype(jnp.bfloat16)
    key_value_pair = attn_inputs[query_width:].reshape(2, KEY_VALUE_HEADS, HEAD_SIZE, rows)
    keys_b = turn(key_value_pair[0], cosine, sine).astype(jnp.bfloat16)
    values_b = key_value_pair[1].astype(jnp.bfloat16)
    pairs = lax.all_gather(
        jnp.concatenate([keys_b, values_b], axis=1).transpose(0, 2, 1), "ctx"
    )
    turned_q = turned_q * jnp.asarray(scale, jnp.bfloat16)
    mirrored_q = swap_mirrored(turned_q[:, :, width:])

    gate_z = projected[:, :DSSM]
    pre_b = projected[:, DSSM:projected_width].astype(jnp.bfloat16)
    rim = from_behind(pre_b[rows - (KW - 1) :], "ctx", 1)
    extended = jnp.concatenate([rim, pre_b], axis=0).astype(jnp.float32)
    conv_f, conv_pull = jax.vjp(partial(conv_local, taps), extended, conv_w, conv_b)
    conv_b16 = conv_f.astype(jnp.bfloat16)
    skip_wide = jnp.repeat(skip_w, PM).reshape(HM // 2, 1, 2 * PM)
    fresh = state_outer(DSSM // NS, 4, 0)(mixer_rows, conv_b16, conv_b16)
    state_in, gains = pass_state(fresh, carry_gain, None, False, pairs)
    local = mixer_forward(
        skip_wide, conv_b16, conv_b16, conv_b16, mixer_rows, docs_column, docs_row
    )

    heads_own, heads_mirrored, log_x = attend_forward(
        group_blocks,
        pairs,
        key_side,
        turned_q,
        mirrored_q,
        query_side,
        out_pieces[1],
        gate_up_pieces[1],
    )
    mixer_w, attn_w, down_w = finish_shards(
        out_pieces,
        [mixer_out.shape[0], attn_out.shape[0], down_proj.shape[0]],
        log_x,
    )
    (gate_up_w,) = finish_shards(gate_up_pieces, [gate_up.shape[0]], log_x)
    heads_back = swap_mirrored(heads_mirrored.astype(jnp.bfloat16))
    heads_t = jnp.concatenate([heads_own.astype(jnp.bfloat16), heads_back], axis=2).reshape(
        QUERY_HEADS * HEAD_SIZE, rows
    )
    mixed = mixer_join(0)(conv_b16, mixer_rows, state_in, local)
    gated, gate_pull = jax.vjp(gate_norm, mixed, gate_z, mixer_g)
    gated_b = gated.astype(jnp.bfloat16)
    mamba = mixed_dot(gated_b, mixer_w)
    attn = lax.dot_general(
        heads_t, attn_w, (((0,), (0,)), ((), ())), preferred_element_type=jnp.float32
    )
    middle = source + attn + mamba
    normed2, ffn_pull = jax.vjp(rms_scale, middle, ffn_g)
    normed2_b = normed2.astype(jnp.bfloat16)
    gate_up_v = mixed_dot(normed2_b, gate_up_w)
    activated, act_pull = jax.vjp(swiglu, gate_up_v)
    activated_b = activated.astype(jnp.bfloat16)
    layer_out = (middle + mixed_dot(activated_b, down_w)).astype(jnp.bfloat16)

    out_low = cotangent[0]
    down_sum, down_beside, down_across = weight_grad(activated_b, out_low)
    (gate_up_grad_v,) = act_pull(nt_dot(out_low, down_w))
    gate_up_low = gate_up_grad_v.astype(jnp.bfloat16)
    gate_up_sum, gate_up_beside, gate_up_across = weight_grad(normed2_b, gate_up_low)
    gate_up_half, gate_up_got = ctx_half([gate_up_sum], model // shards)
    middle_norm_grad, ffn_gain_grad = ffn_pull(nt_dot(gate_up_low, gate_up_w))
    middle_grad = out_low.astype(jnp.float32) + middle_norm_grad
    middle_low = middle_grad.astype(jnp.bfloat16)
    heads_low = nt_dot(attn_w, middle_low).astype(jnp.bfloat16)
    heads_low = heads_low.reshape(QUERY_HEADS, HEAD_SIZE, rows)
    mirrored_low = swap_mirrored(heads_low[:, :, width:])
    gated_grad = nt_dot(middle_low, mixer_w)
    mixed_grad, gate_z_grad, mixer_gain_grad = gate_pull(gated_grad)
    upward = state_outer(DSSM // NS + 1, 2, 1)(
        mixer_rows, mixed_grad.astype(jnp.bfloat16), conv_b16, down_beside
    )
    state_out_grad, _ = pass_state(upward, None, gains, True)
    down_half, down_got = ctx_half([tie(down_sum, upward)], model // shards)
    gate_z_low = gate_z_grad.astype(jnp.bfloat16)
    query_grad_own, query_grad_mirrored, pairs_grad = attend_backward(
        group_blocks,
        pairs,
        key_side,
        turned_q,
        mirrored_q,
        query_side,
        log_x,
        heads_own,
        heads_mirrored,
        heads_low,
        mirrored_low,
        gate_up_beside,
        down_across,
    )
    mixer_products = split_products(gated_b, middle_low)
    attn_products = split_products(heads_t, middle_low, 0)
    shard_sizes = [mixer_out.shape[0], attn_out.shape[0]]

    def interleaved(parts):
        return jnp.concatenate(
            [
                part[start * size : (start + 1) * size]
                for start in range(parts[0].shape[0] // shard_sizes[0])
                for part, size in zip(parts, shard_sizes)
            ],
            axis=0,
        ).astype(jnp.bfloat16)

    mixer_attn_sum, mixer_beside, mixer_across = shard_sum(
        *[interleaved(parts) for parts in zip(mixer_products, attn_products)], pairs_grad
    )
    in_sum_z, in_z_beside, in_z_across = weight_grad(normed_b, gate_z_low, pairs_grad)
    pair_grad = (
        scatter_blocks(pairs_grad).astype(jnp.float32).transpose(0, 2, 1)
    )
    query_low_own, query_low_mirrored = (
        (turn(grad, *tables) * scale).astype(jnp.bfloat16)
        for grad, tables in (
            (query_grad_own, (cosine[:, :width], -sine[:, :width])),
            (query_grad_mirrored, (mirrored_cosine, -mirrored_sine)),
        )
    )
    query_low = jnp.concatenate(
        [query_low_own, swap_mirrored(query_low_mirrored)], axis=2
    ).reshape(QUERY_HEADS * HEAD_SIZE, rows)

    conv_grad, skip_parts = mixer_backward(
        skip_wide,
        conv_b16,
        conv_b16,
        conv_b16,
        mixer_rows,
        docs_column,
        docs_row,
        state_in,
        state_out_grad,
        mixed_grad,
        gate_up_across,
        in_z_beside,
        down_got,
        mixer_beside,
    )
    mixer_half, mixer_got = ctx_half(
        [tie(mixer_attn_sum, conv_grad), tie(in_sum_z, conv_grad)], model // shards
    )
    skip_grad = jnp.sum(skip_parts.reshape(HM, PM), axis=1)
    extended_grad, conv_weight_grad, conv_bias_grad = conv_pull(conv_grad)
    from_above = from_behind(extended_grad[: KW - 1], "ctx", -1)
    pre_grad = extended_grad[KW - 1 :] + jnp.pad(from_above, ((rows - (KW - 1), 0), (0, 0)))
    pre_low = tie(pre_grad.astype(jnp.bfloat16), gate_up_got, in_z_across, mixer_across)
    in_sum_pre, _, _ = weight_grad(normed_b, pre_low)
    projected_low = jnp.concatenate([gate_z_low, pre_low], axis=1)
    normed_grad = nt_dot(projected_low, in_w)

    keys_low = turn(pair_grad[:, :HEAD_SIZE], cosine, -sine)
    keyval_low = jnp.concatenate(
        [
            keys_low.reshape(KEY_VALUE_HEADS * HEAD_SIZE, rows),
            pair_grad[:, HEAD_SIZE:].reshape(KEY_VALUE_HEADS * HEAD_SIZE, rows),
        ],
        axis=0,
    ).astype(jnp.bfloat16)
    attn_pair_low = jnp.concatenate([query_low, keyval_low], axis=0).T
    attn_pair_sum, _, _ = weight_grad(normed_b, attn_pair_low)
    normed_grad = normed_grad + nt_dot(attn_pair_low, attn_pair_w)
    source_grad, norm_grad = norm_pull(normed_grad)
    tokens_grad = (middle_grad + source_grad)[None]

    small_grad = pack_small(
        norm_grad, conv_weight_grad, conv_bias_grad, skip_grad, mixer_gain_grad, ffn_gain_grad, shards
    )
    small_share = sum_small(small_grad)
    last_half, _ = ctx_half([in_sum_pre, attn_pair_sum], model // shards)
    (down_share,), summed = ctx_finish(down_half, [down_sum.shape], 0)
    (gate_up_share,), summed = ctx_finish(tie(gate_up_half, summed), [gate_up_sum.shape], 1)
    (mixer_attn_share, in_share_z), summed = ctx_finish(
        tie(mixer_half, summed), [mixer_attn_sum.shape, in_sum_z.shape], 2
    )
    mixer_share = mixer_attn_share[: mixer_out.shape[0]]
    attn_share = mixer_attn_share[mixer_out.shape[0] :]
    (in_share_pre, attn_pair_share), _ = ctx_finish(
        tie(last_half, summed),
        [in_sum_pre.shape, attn_pair_sum.shape],
        3,
    )
    norm_share, conv_w_share, conv_b_share, skip_share, mixer_g_share, ffn_share = unpack_small(
        small_share, model, channels, HM, 1
    )
    return (
        layer_out[None],
        tokens_grad,
        norm_share,
        jnp.concatenate([in_share_z, in_share_pre], axis=1),
        conv_w_share,
        conv_b_share,
        skip_share,
        mixer_g_share,
        mixer_share,
        attn_pair_share[:, : QUERY_HEADS * HEAD_SIZE],
        attn_pair_share[:, QUERY_HEADS * HEAD_SIZE :],
        attn_share,
        ffn_share,
        gate_up_share,
        down_share,
    )


def solution(mesh):
    in_specs = (
        P("wshard", "ctx", None),
        P("wshard", "ctx", None),
        P("wshard", None),
        P("wshard", None, "ctx"),
        P("wshard"),
        P("wshard", None),
        P(None, "wshard"),
        P("wshard"),
        P("wshard"),
        P("wshard"),
        P("wshard", None),
        P("wshard", None),
        P("wshard", None),
        P("wshard", None),
        P("wshard"),
        P("wshard", None),
        P("wshard", None),
    )
    out_specs = (
        P("wshard", "ctx", None),
        P("wshard", "ctx", None),
        P("wshard"),
        P("wshard", None),
        P(None, "wshard"),
        P("wshard"),
        P("wshard"),
        P("wshard"),
        P("wshard", None),
        P("wshard", None),
        P("wshard", None),
        P("wshard", None),
        P("wshard"),
        P("wshard", None),
        P("wshard", None),
    )
    return jax.shard_map(
        per_device, mesh=mesh, in_specs=in_specs, out_specs=out_specs, check_vma=False
    )
```

```python
from functools import partial

import jax
import jax.numpy as jnp
from jax import lax
from jax.experimental import pallas as pl
from jax.experimental.pallas import tpu as pltpu
from jax.sharding import PartitionSpec as P

FF = 2048
QUERY_HEADS = 8
KEY_VALUE_HEADS = 2
HEAD_SIZE = 64
HM = 24
PM = 64
NS = 128
KW = 4
DSSM = 1536

eps_norm = 1e-05
rope_base = 100000000000.0
mask_fill_value = -1e30
highest = lax.Precision.HIGHEST
MESH_AXES = ("ctx", "wshard")
small_cost = pl.CostEstimate(flops=1024, bytes_accessed=1024, transcendentals=0)


def exchange(block, ctx_flip, shard_flip):
    blocks, shards = lax.axis_size("ctx"), lax.axis_size("wshard")
    route = [
        (c * shards + w, (c ^ ctx_flip) * shards + (w ^ shard_flip))
        for c in range(blocks)
        for w in range(shards)
    ]
    return lax.ppermute(block, MESH_AXES, route)


def from_behind(block, axis, distance):
    devices = range(lax.axis_size(axis))
    route = [(i - distance, i) for i in devices if i - distance in devices]
    return lax.ppermute(block, axis, route)


def swap_mirrored(block):
    count = lax.axis_size("ctx")
    return lax.ppermute(block, "ctx", [(i, count - 1 - i) for i in range(count)])


def tie_body(*refs):
    pass


def tie(value, *after):
    anywhere = pl.BlockSpec(memory_space=pl.ANY)
    return pl.pallas_call(
        tie_body,
        in_specs=[anywhere] * (1 + len(after)),
        out_specs=anywhere,
        out_shape=jax.ShapeDtypeStruct(value.shape, value.dtype),
        input_output_aliases={0: 0},
        cost_estimate=pl.CostEstimate(flops=0, bytes_accessed=0, transcendentals=0),
        name="tie",
    )(value, *after)


def assemble_body(spans, target_ref, *refs):
    out_ref = refs[-1]
    step = pl.program_id(0)
    for piece, (first, size) in zip(refs, spans):

        def put(piece=piece):
            out_ref[...] = piece[...]

        pl.when((step >= first) & (step < first + size))(put)


def assemble(pieces, rows, anchors=()):
    spans, offsets, targets = [], [], []
    for _, source, start, size in pieces:
        spans.append((len(targets), size // rows))
        offsets.append(source // rows)
        targets += [start // rows + at for at in range(size // rows)]
    columns, kind = pieces[0][0].shape[1], pieces[0][0].dtype

    def source_map(offset, first, size):
        return lambda i, target: (offset + jnp.clip(i - first, 0, size - 1), 0)

    return pl.pallas_call(
        partial(assemble_body, spans),
        grid_spec=pltpu.PrefetchScalarGridSpec(
            num_scalar_prefetch=1,
            grid=(len(targets),),
            in_specs=[
                pl.BlockSpec((rows, columns), source_map(offset, first, size))
                for offset, (first, size) in zip(offsets, spans)
            ]
            + [pl.BlockSpec(memory_space=pl.ANY)] * len(anchors),
            out_specs=pl.BlockSpec((rows, columns), lambda i, target: (target[i], 0)),
        ),
        out_shape=jax.ShapeDtypeStruct((rows * len(targets), columns), kind),
        compiler_params=pltpu.CompilerParams(
            dimension_semantics=("arbitrary",), vmem_limit_bytes=32 * 1024 * 1024
        ),
        cost_estimate=small_cost,
        name="assemble",
    )(jnp.stack([jnp.asarray(target, jnp.int32) for target in targets]), *[p[0] for p in pieces], *anchors)


def gather_first(shard, rows, anchors):
    part = rows // 4
    w = lax.axis_index("wshard")
    side = lax.axis_index("ctx") % 2
    direct = shard[2 * part :]
    across = exchange(lax.dynamic_slice_in_dim(shard, side * part, part, 0), 0, 2)
    across_direct = exchange(direct, 0, 2)
    beside = exchange(shard, 0, 1)
    across_relayed = exchange(across, 1, 0)
    far, far_direct, far_relayed = (
        exchange(piece, 0, 1) for piece in (across, across_direct, across_relayed)
    )
    pieces = [(shard, 0, w * rows, rows), (beside, 0, (w ^ 1) * rows, rows)]
    for flip, early, late, rest in (
        (2, across, across_relayed, across_direct),
        (3, far, far_relayed, far_direct),
    ):
        start = (w ^ flip) * rows
        pieces.append((early, 0, start + side * part, part))
        pieces.append((late, 0, start + (1 - side) * part, part))
        pieces.append((rest, 0, start + 2 * part, 2 * part))
    tails = [shard[rows:], beside[rows:], across_direct[2 * part :], far_direct[2 * part :]]
    tails = jnp.concatenate([tail[:1] for tail in tails], axis=0)
    small = jnp.concatenate(
        [lax.dynamic_slice_in_dim(tails, w ^ at, 1, 0) for at in range(4)], axis=0
    )
    return assemble(pieces, part, anchors), small, across_direct


def start_shards(stacked, after):
    stacked, _ = lax.optimization_barrier((stacked, after))
    return stacked, exchange(stacked, 0, 1), exchange(stacked, 0, 2)


def finish_shards(pieces, sizes, after):
    own, beside, across = pieces
    far = exchange(lax.optimization_barrier((across, after))[0], 0, 1)
    w = lax.axis_index("wshard")
    wholes, source = [], 0
    for size in sizes:
        wholes.append(
            assemble(
                [
                    (part, source, (w ^ flip) * size, size)
                    for flip, part in enumerate((own, beside, across, far))
                ],
                size,
            )
        )
        source += size
    return wholes


def add_low(first, *others):
    total = first.astype(jnp.float32)
    for other in others:
        total = total + other.astype(jnp.float32)
    return total.astype(jnp.bfloat16)


def lay_side_by_side(blocks, rows):
    parts = []
    for block in blocks:
        for start in range(0, block.shape[0], rows):
            part = block[start : start + rows]
            parts.append(jnp.pad(part, ((0, rows - part.shape[0]), (0, 0))))
    return jnp.concatenate(parts, axis=1)


def take_apart(array, shapes):
    rows, start, blocks = array.shape[0], 0, []
    for height, columns in shapes:
        parts = []
        for _ in range(0, height, rows):
            parts.append(array[: min(height, rows), start : start + columns])
            start += columns
        blocks.append(parts[0] if len(parts) == 1 else jnp.concatenate(parts, axis=0))
    return blocks


def ctx_half(blocks, rows):
    side = lax.axis_index("ctx") % 2
    whole = lay_side_by_side(blocks, rows)
    half = rows // 2
    give = lax.dynamic_slice_in_dim(whole, (1 - side) * half, half, 0)
    got = exchange(give, 1, 0)
    return add_low(lax.dynamic_slice_in_dim(whole, side * half, half, 0), got), got, give


def ctx_lines():
    count = lax.axis_size("ctx")
    return [list(range(start, count, 2)) for start in range(2)]


def ctx_finish(mine, shapes, turn_at):
    side = lax.axis_index("ctx") % 2
    lines = ctx_lines()
    if turn_at % 2:
        lines = lines[::-1]
    if turn_at // 2:
        lines = [line[::-1] for line in lines]
    mine = lax.psum(mine, "ctx", axis_index_groups=lines)
    summed = mine
    got = exchange(mine, 1, 0)
    whole = jnp.where(
        side == 0, jnp.concatenate([mine, got], axis=0), jnp.concatenate([got, mine], axis=0)
    ).astype(jnp.float32)
    return take_apart(whole, shapes), summed


def shard_pieces(array, axis):
    w = lax.axis_index("wshard")
    size = array.shape[axis] // 4

    def piece(flip):
        return lax.dynamic_slice_in_dim(array, (w ^ flip) * size, size, axis)

    return jnp.concatenate([piece(1), piece(3)], axis=axis), piece(2), piece(0)


def shard_sum(beside, across, own):
    rows = own.shape[0]
    got = exchange(beside.astype(jnp.bfloat16), 0, 1)
    sent = add_low(across, got[rows:])
    got_across = exchange(sent, 0, 2)
    return add_low(own, got[:rows], got_across), got, got_across, sent


def split_products(left, right, axis=1):
    return [
        lax.dot_general(
            piece, right, (((1 - axis,), (0,)), ((), ())), preferred_element_type=jnp.float32
        )
        for piece in shard_pieces(left, axis)
    ]


def weight_grad(left, right):
    return shard_sum(*split_products(left, right))


def start_sum(beside, across, own, after):
    rows = own.shape[0]
    got = exchange(beside.astype(jnp.bfloat16), 0, 1)
    got_across = exchange(tie(add_low(across, got[rows:]), after), 0, 2)
    return own, got, got_across


def finish_sum(started, after):
    own, got, got_across = started
    return add_low(own, got[: own.shape[0]], tie(got_across, after))


def sum_small(value):
    rows = value.shape[0] // 4
    for flip in (1, 2):
        value = value + exchange(value, 0, flip)
    value = lax.dynamic_slice_in_dim(value, lax.axis_index("wshard") * rows, rows, 0)
    bit = 1
    while bit < lax.axis_size("ctx"):
        value = value + exchange(value, bit, 0)
        bit *= 2
    return value


def scatter_blocks(blocks, after):
    position, bit = lax.axis_index("ctx"), 1
    while blocks.shape[0] > 1:
        up = (position // bit) % 2
        halves = blocks.reshape((blocks.shape[0] // 2, 2) + blocks.shape[1:])
        keep = lax.dynamic_index_in_dim(halves, up, 1, keepdims=False)
        give = lax.dynamic_index_in_dim(halves, 1 - up, 1, keepdims=False)
        got = exchange(give, bit, 0)
        if bit == 1:
            got = tie(got, after)
        blocks = add_low(keep, got)
        bit *= 2
    return blocks[0]


def mixed_dot(left, right):
    return jnp.dot(left, right, preferred_element_type=jnp.float32)


def rms_scale(value, gain):
    return value * lax.rsqrt(jnp.mean(value * value, axis=-1, keepdims=True) + eps_norm) * gain


def doc_numbers(lengths, position_index):
    ends = jnp.cumsum(lengths)[:-1]
    tally_count = jnp.sum((position_index[:, None] >= ends[None, :]).astype(jnp.int32), axis=1)
    return jnp.where(position_index >= 0, tally_count, -1)


def turn_tables(position_index):
    half = HEAD_SIZE // 2
    freq = rope_base ** (-jnp.arange(half, dtype=jnp.float32) / half)
    angle = freq[:, None] * position_index.astype(jnp.float32)[None, :]
    return jnp.cos(angle), jnp.sin(angle)


def turn(value, cosine, sine):
    half = value.shape[-2] // 2
    first = value[..., :half, :]
    second = value[..., half:, :]
    return jnp.concatenate(
        [first * cosine - second * sine, second * cosine + first * sine], axis=-2
    )


def conv_local(taps, extended, weight, bias):
    tally_count = extended.shape[0] - (KW - 1)
    total = bias[None, :]
    for tap in range(KW):
        total = (
            total + weight[tap][None, :] * extended[tap : tap + tally_count] * taps[tap][:, None]
        )
    return jax.nn.silu(total)


def gate_norm(mixed, gate_z, gain):
    return rms_scale(mixed * jax.nn.silu(gate_z), gain)


def swiglu(gate_up_v):
    return jax.nn.silu(gate_up_v[:, :FF]) * gate_up_v[:, FF:]


def split_three(value):
    high = value.astype(jnp.bfloat16)
    rest = value - high.astype(jnp.float32)
    middle = rest.astype(jnp.bfloat16)
    low = (rest - middle.astype(jnp.float32)).astype(jnp.bfloat16)
    return [high, middle, low]


def nt_dot(left, right):
    return lax.dot_general(left, right, (((1,), (1,)), ((), ())), preferred_element_type=jnp.float32)


def causal_tile(scores, group, width):
    rows = lax.broadcasted_iota(jnp.int32, scores.shape, 0)
    columns = lax.broadcasted_iota(jnp.int32, scores.shape, 1)
    return jnp.where(rows <= lax.rem(columns, width) + group * width, scores, mask_fill_value)


def load_extended(extended, group, lower, value_ref, side, extra):
    width = value_ref.shape[2]
    extended[group] = jnp.zeros(extended.shape[1:], extended.dtype)
    for head in range(value_ref.shape[0]):
        here = slice(head * width, (head + 1) * width)
        extended[group, lower : lower + HEAD_SIZE, here] = value_ref[head]
    side = jnp.concatenate([side.astype(jnp.float32)] * value_ref.shape[0], axis=1)
    if extra is not None:
        row = lax.broadcasted_iota(jnp.int32, side.shape, 0)
        for at, part in enumerate(split_three(-extra)):
            side = jnp.where(row == 8 + at, part.astype(jnp.float32), side)
    extended[group, 128:144, :] = side.astype(extended.dtype)


def attend_forward_body(width, blocks, pair_ref, side_ref, query_a, query_b, query_side_ref, *refs):
    heads_refs, (log_ref, query_x, peak, total) = refs[-6:-4], refs[-4:]
    step = pl.program_id(1)

    @pl.when(step == 0)
    def start():
        for group, query_ref in enumerate((query_a, query_b)):
            load_extended(query_x, group, 0, query_ref, query_side_ref[group], None)
        peak[...] = jnp.full(peak.shape, mask_fill_value, jnp.float32)
        total[...] = jnp.zeros(total.shape, jnp.float32)

    @pl.when(step <= jnp.maximum(blocks[0], blocks[1]))
    def work():
        keys = jnp.concatenate([pair_ref[0, 0], side_ref[...]], axis=1)
        values = keys.T[HEAD_SIZE:144]

        def tile(group, masked):
            scores = mixed_dot(keys, query_x[group])
            if masked:
                scores = causal_tile(scores, group, width)
            old = peak[group]
            new = jnp.maximum(old, jnp.max(scores, axis=0, keepdims=True))
            probs = jnp.exp(scores - new)
            total[group] = total[group] * jnp.exp(old - new) + mixed_dot(
                values, probs.astype(jnp.bfloat16)
            )
            peak[group] = new

        for group in range(2):
            pl.when(step < blocks[group])(partial(tile, group, False))
            pl.when(step == blocks[group])(partial(tile, group, True))

    @pl.when(step == pl.num_programs(1) - 1)
    def finish():
        for group in range(2):
            weight = total[group, HEAD_SIZE + 8 : HEAD_SIZE + 9, :]
            heads = total[group, :HEAD_SIZE, :] / weight
            for head in range(heads.shape[1] // width):
                heads_refs[group][head] = heads[:, head * width : (head + 1) * width]
            log_ref[group, 0] = peak[group] + jnp.log(weight)


def attend_backward_body(
    width,
    blocks,
    pair_ref,
    side_ref,
    query_a,
    query_b,
    query_side_ref,
    log_ref,
    heads_a,
    heads_b,
    grad_a,
    grad_b,
    *refs,
):
    query_grad_refs, (pair_grad_ref, query_x, grad_x, pair_acc, query_acc) = refs[-7:-5], refs[-5:]
    step = pl.program_id(1)

    @pl.when(step == 0)
    def start():
        groups = ((query_a, heads_a, grad_a), (query_b, heads_b, grad_b))
        for group, (query_ref, heads_ref, grad_ref) in enumerate(groups):
            load_extended(query_x, group, 0, query_ref, query_side_ref[group], log_ref[group, 0])
            delta = [
                jnp.sum(heads_ref[head] * grad_ref[head].astype(jnp.float32), axis=0, keepdims=True)
                for head in range(heads_ref.shape[0])
            ]
            blank = jnp.zeros(query_side_ref.shape[1:], jnp.float32)
            load_extended(
                grad_x, group, HEAD_SIZE, grad_ref, blank, jnp.concatenate(delta, axis=1)
            )
        query_acc[...] = jnp.zeros(query_acc.shape, jnp.float32)

    pair_acc[...] = jnp.zeros(pair_acc.shape, jnp.float32)

    @pl.when(step <= jnp.maximum(blocks[0], blocks[1]))
    def work():
        pair = pair_ref[0, 0]
        keys = jnp.concatenate([pair, side_ref[...]], axis=1)
        turned = pair.T[:HEAD_SIZE]

        def tile(group, masked):
            scores = mixed_dot(keys, query_x[group])
            if masked:
                scores = causal_tile(scores, group, width)
            probs = jnp.exp(scores)
            low = (probs * mixed_dot(keys, grad_x[group])).astype(jnp.bfloat16)
            pair_acc[...] += nt_dot(low, query_x[group, :128, :]) + nt_dot(
                probs.astype(jnp.bfloat16), grad_x[group, :128, :]
            )
            query_acc[group] += mixed_dot(turned, low)

        for group in range(2):
            pl.when(step < blocks[group])(partial(tile, group, False))
            pl.when(step == blocks[group])(partial(tile, group, True))

    pair_grad_ref[0, 0] = pair_acc[...].astype(jnp.bfloat16)

    @pl.when(step == pl.num_programs(1) - 1)
    def finish():
        for group in range(2):
            for head in range(query_acc.shape[2] // width):
                query_grad_refs[group][head] = query_acc[group, :, head * width : (head + 1) * width]


def attention_calls(rows, count, anchors):
    width = rows // 2
    span = width * (QUERY_HEADS // KEY_VALUE_HEADS)

    def last(blocks):
        return jnp.maximum(blocks[0], blocks[1])

    pair_spec = pl.BlockSpec(
        (1, 1, rows, 128), lambda g, k, blocks: (jnp.minimum(k, last(blocks)), g, 0, 0)
    )
    side_spec = pl.BlockSpec((rows, 128), lambda g, k, blocks: (jnp.minimum(k, last(blocks)), 0))

    heads_per_group = QUERY_HEADS // KEY_VALUE_HEADS
    own = pl.BlockSpec((heads_per_group, HEAD_SIZE, width), lambda g, k, blocks: (g, 0, 0))
    half_spec = own
    log_spec = pl.BlockSpec((2, 1, 1, span), lambda g, k, blocks: (0, g, 0, 0))
    query_side_spec = pl.BlockSpec((2, 16, width), lambda g, k, blocks: (0, 0, 0))
    half_shape = jax.ShapeDtypeStruct((QUERY_HEADS, HEAD_SIZE, width), jnp.float32)

    anywhere = pl.BlockSpec(memory_space=pl.ANY)
    params = pltpu.CompilerParams(
        dimension_semantics=("arbitrary", "arbitrary"), vmem_limit_bytes=48 * 1024 * 1024
    )
    forward = pl.pallas_call(
        partial(attend_forward_body, width),
        grid_spec=pltpu.PrefetchScalarGridSpec(
            num_scalar_prefetch=1,
            grid=(KEY_VALUE_HEADS, count),
            in_specs=[pair_spec, side_spec, own, half_spec, query_side_spec]
            + [anywhere] * anchors[0],
            out_specs=[half_spec, half_spec, log_spec],
            scratch_shapes=[
                pltpu.VMEM((2, 256, span), jnp.bfloat16),
                pltpu.VMEM((2, 1, span), jnp.float32),
                pltpu.VMEM((2, 144 - HEAD_SIZE, span), jnp.float32),
            ],
        ),
        out_shape=[
            half_shape,
            half_shape,
            jax.ShapeDtypeStruct((2, KEY_VALUE_HEADS, 1, span), jnp.float32),
        ],
        compiler_params=params,
        cost_estimate=small_cost,
        name="attend_forward",
    )
    backward = pl.pallas_call(
        partial(attend_backward_body, width),
        grid_spec=pltpu.PrefetchScalarGridSpec(
            num_scalar_prefetch=1,
            grid=(KEY_VALUE_HEADS, count),
            in_specs=[
                pair_spec,
                side_spec,
                own,
                half_spec,
                query_side_spec,
                log_spec,
                half_spec,
                half_spec,
                own,
                half_spec,
            ]
            + [anywhere] * anchors[1],
            out_specs=[
                half_spec,
                half_spec,
                pl.BlockSpec((1, 1, rows, 128), lambda g, k, blocks: (k, g, 0, 0)),
            ],
            scratch_shapes=[
                pltpu.VMEM((2, 256, span), jnp.bfloat16),
                pltpu.VMEM((2, 256, span), jnp.bfloat16),
                pltpu.VMEM((rows, 128), jnp.float32),
                pltpu.VMEM((2, HEAD_SIZE, span), jnp.float32),
            ],
        ),
        out_shape=[
            half_shape,
            half_shape,
            jax.ShapeDtypeStruct((count, KEY_VALUE_HEADS, rows, 128), jnp.bfloat16),
        ],
        compiler_params=params,
        cost_estimate=small_cost,
        name="attend_backward",
    )
    return forward, backward


def pick(pair):
    lane = lax.broadcasted_iota(jnp.int32, (pair.shape[0], 2 * PM), 1)
    return jnp.where(lane < PM, pair[:, 0:1], pair[:, 1:2])


def outer_body(kind, rows_ref, left_ref, right_ref, *refs):
    out_ref = refs[-1]
    for at in range(rows_ref.shape[0]):
        scale = pick(rows_ref[at].T[:, kind : kind + 2])
        left = left_ref[:, at * 128 : (at + 1) * 128].astype(jnp.float32) * scale
        out_ref[at * 128 : (at + 1) * 128, :] = lax.dot_general(
            left.astype(jnp.bfloat16),
            right_ref[...],
            (((0,), (0,)), ((), ())),
            preferred_element_type=jnp.float32,
        ).astype(out_ref.dtype)


def join_body(c_ref, rows_ref, state_ref, local_ref, *refs):
    out_ref = refs[-1]
    for at in range(rows_ref.shape[0]):
        here = slice(at * 2 * PM, (at + 1) * 2 * PM)
        inner = nt_dot(c_ref[...], state_ref[here, :])
        out_ref[:, here] = local_ref[:, here] + inner * pick(rows_ref[at].T[:, 2:4])


def mixed_body(
    skip_ref, x_ref, b_ref, c_ref, row_ref, docs_column, docs_row, out_ref, fill, products
):
    rows = x_ref.shape[0]
    half = rows // 2

    @pl.when(pl.program_id(0) == 0)
    def start():
        at = lax.broadcasted_iota(jnp.int32, (rows, rows), 0)
        source = lax.broadcasted_iota(jnp.int32, (rows, rows), 1)
        same = (at >= source) & (docs_column[...] == docs_row[...])
        fill[...] = jnp.where(same, 0.0, mask_fill_value)
        products[...] = nt_dot(c_ref[...], b_ref[...])

    x = x_ref[...]
    columns = row_ref[0].T
    lane = lax.broadcasted_iota(jnp.int32, (half, 2 * PM), 1)
    for block in range(2):
        here = slice(block * half, (block + 1) * half)
        width = (block + 1) * half
        parts = []
        for head in range(2):
            decay = jnp.exp(
                (columns[here, head : head + 1] - row_ref[0, head : head + 1, :width])
                + fill[here, :width]
            )
            weights = (products[here, :width] * decay).astype(jnp.bfloat16)
            parts.append(mixed_dot(weights, x[:width]))
        local = jnp.where(lane < PM, parts[0], parts[1])
        out_ref[here, :] = local + x[here].astype(jnp.float32) * skip_ref[0]


def mixed_grad_body(
    skip_ref,
    x_ref,
    b_ref,
    c_ref,
    row_ref,
    docs_column,
    docs_row,
    state_ref,
    state_grad_ref,
    grad_ref,
    *refs,
):
    out_ref, skip_grad_ref, fill, products, scores, b_grad, c_grad = refs[-7:]
    rows = x_ref.shape[0]
    half = rows // 2
    step = pl.program_id(0)
    pairs = HM // 2

    @pl.when(step == 0)
    def start():
        source = lax.broadcasted_iota(jnp.int32, (rows, rows), 0)
        at = lax.broadcasted_iota(jnp.int32, (rows, rows), 1)
        same = (at >= source) & (docs_column[...] == docs_row[...])
        fill[...] = jnp.where(same, 0.0, mask_fill_value)
        products[...] = nt_dot(b_ref[...], c_ref[...])
        scores[...] = jnp.zeros(scores.shape, jnp.float32)
        b_grad[...] = jnp.zeros(b_grad.shape, jnp.float32)
        c_grad[...] = jnp.zeros(c_grad.shape, jnp.float32)

    @pl.when(step < pairs)
    def work():
        x = x_ref[...]
        x_f = x.astype(jnp.float32)
        grad = grad_ref[...]
        low = grad.astype(jnp.bfloat16)
        lane = lax.broadcasted_iota(jnp.int32, (half, 2 * PM), 1)
        lane_all = lax.broadcasted_iota(jnp.int32, (rows, 2 * PM), 1)
        skip_grad_ref[0] = jnp.sum(grad * x_f, axis=0, keepdims=True)
        state_grad = state_grad_ref[...]
        columns = row_ref[0].T
        tail = pick(columns[:, 4:6])
        b_grad[...] += mixed_dot((x_f * tail).astype(jnp.bfloat16), state_grad)
        entered = (low.astype(jnp.float32) * pick(columns[:, 2:4])).astype(jnp.bfloat16)
        c_grad[...] += mixed_dot(entered, state_ref[...])
        passed = nt_dot(b_ref[...], state_grad) * tail + grad * skip_ref[0]
        chosen = [
            jnp.where((lane_all < PM) == (head == 0), x_f, 0.0).astype(jnp.bfloat16)
            for head in range(2)
        ]
        for block in range(2):
            here = slice(block * half, (block + 1) * half)
            start_at = block * half
            parts = []
            for head in range(2):
                decay = jnp.exp(
                    (row_ref[0, head : head + 1, start_at:] - columns[here, head : head + 1])
                    + fill[here, start_at:]
                )
                weights = (products[here, start_at:] * decay).astype(jnp.bfloat16)
                parts.append(mixed_dot(weights, low[start_at:]))
                scores[here, start_at:] += nt_dot(chosen[head][here], low[start_at:]) * decay
            out_ref[here, :] = jnp.where(lane < PM, parts[0], parts[1]) + passed[here]

    @pl.when(step == pairs)
    def give_b():
        out_ref[...] = b_grad[...] + mixed_dot(scores[...].astype(jnp.bfloat16), c_ref[...])

    @pl.when(step == pairs + 1)
    def give_c():
        out_ref[...] = c_grad[...] + lax.dot_general(
            scores[...].astype(jnp.bfloat16),
            b_ref[...],
            (((0,), (0,)), ((), ())),
            preferred_element_type=jnp.float32,
        )


def mixer_calls(rows, anchors):
    pairs = HM // 2
    wide = 2 * PM
    params = pltpu.CompilerParams(
        dimension_semantics=("arbitrary",), vmem_limit_bytes=48 * 1024 * 1024
    )

    def capped(p):
        return jnp.minimum(p, pairs - 1)

    anywhere = pl.BlockSpec(memory_space=pl.ANY)

    def join(after):
        each = 4
        wide_spec = pl.BlockSpec((rows, each * wide), lambda p: (0, p))
        return pl.pallas_call(
            join_body,
            grid=(pairs // each,),
            in_specs=[
                pl.BlockSpec((rows, NS), lambda p: (0, DSSM // NS + 1)),
                pl.BlockSpec((each, 8, rows), lambda p: (p, 0, 0)),
                pl.BlockSpec((each * wide, NS), lambda p: (p, 0)),
                wide_spec,
            ]
            + [anywhere] * after,
            out_specs=wide_spec,
            out_shape=jax.ShapeDtypeStruct((rows, DSSM), jnp.float32),
            compiler_params=params,
            cost_estimate=small_cost,
            name="mixer_join",
        )

    def outer(right_at, kind, after):
        each = 2
        return pl.pallas_call(
            partial(outer_body, kind),
            grid=(pairs // each,),
            in_specs=[
                pl.BlockSpec((each, 8, rows), lambda p: (p, 0, 0)),
                pl.BlockSpec((rows, each * wide), lambda p: (0, p)),
                pl.BlockSpec((rows, NS), lambda p: (0, right_at)),
            ]
            + [anywhere] * after,
            out_specs=pl.BlockSpec((each * wide, NS), lambda p: (p, 0)),
            out_shape=jax.ShapeDtypeStruct((DSSM, NS), jnp.bfloat16),
            compiler_params=params,
            cost_estimate=small_cost,
            name="state_outer",
        )

    x_spec = pl.BlockSpec((rows, wide), lambda p: (0, capped(p)))
    b_spec = pl.BlockSpec((rows, NS), lambda p: (0, DSSM // NS))
    c_spec = pl.BlockSpec((rows, NS), lambda p: (0, DSSM // NS + 1))
    row_spec = pl.BlockSpec((1, 8, rows), lambda p: (capped(p), 0, 0))
    skip_spec = pl.BlockSpec((1, 1, wide), lambda p: (capped(p), 0, 0))
    state_spec = pl.BlockSpec((wide, NS), lambda p: (capped(p), 0))
    docs_specs = [pl.BlockSpec((rows, 1), lambda p: (0, 0)), pl.BlockSpec((1, rows), lambda p: (0, 0))]
    square = pltpu.VMEM((rows, rows), jnp.float32)
    narrow = pltpu.VMEM((rows, NS), jnp.float32)
    forward = pl.pallas_call(
        mixed_body,
        grid=(pairs,),
        in_specs=[skip_spec, x_spec, b_spec, c_spec, row_spec] + docs_specs,
        out_specs=pl.BlockSpec((rows, wide), lambda p: (0, p)),
        out_shape=jax.ShapeDtypeStruct((rows, DSSM), jnp.float32),
        scratch_shapes=[square, square],
        compiler_params=params,
        cost_estimate=small_cost,
        name="mixer_forward",
    )
    backward = pl.pallas_call(
        mixed_grad_body,
        grid=(pairs + 2,),
        in_specs=[skip_spec, x_spec, b_spec, c_spec, row_spec]
        + docs_specs
        + [state_spec, state_spec, x_spec]
        + [anywhere] * anchors,
        out_specs=[
            pl.BlockSpec((rows, wide), lambda p: (0, p)),
            pl.BlockSpec((1, 1, wide), lambda p: (capped(p), 0, 0)),
        ],
        out_shape=[
            jax.ShapeDtypeStruct((rows, DSSM + 2 * NS), jnp.float32),
            jax.ShapeDtypeStruct((pairs, 1, wide), jnp.float32),
        ],
        scratch_shapes=[square, square, square, narrow, narrow],
        compiler_params=params,
        cost_estimate=small_cost,
        name="mixer_backward",
    )
    return outer, join, forward, backward


def gain_rows(gain):
    return jnp.pad(jnp.stack(split_three(gain)), ((0, 13), (0, NS - HM)))


def read_gain(rows):
    return jnp.sum(rows[..., :3, :HM].astype(jnp.float32), axis=-2)


def pass_state(part, gain, gains, reverse, after=None):
    count, position = lax.axis_size("ctx"), lax.axis_index("ctx")
    side, line_at = position % 2, position // 2
    is_first = (side == 1) if reverse else (side == 0)

    def by_head(array):
        return array.reshape(array.shape[:-2] + (HM, PM, NS)).astype(jnp.float32)

    got = exchange(part if gains else jnp.concatenate([part, gain_rows(gain)], axis=0), 1, 0)
    if gains:
        gain, other, line_gains = gains
    else:
        other = read_gain(got[DSSM:])
    own_f, got_f = by_head(part), by_head(got[:DSSM])
    first = jnp.where(is_first, own_f, got_f)
    second = jnp.where(is_first, got_f, own_f)
    first_gain = jnp.where(is_first, gain, other)[:, None, None]
    second_gain = jnp.where(is_first, other, gain)[:, None, None]
    total = (second_gain * first + second).astype(jnp.bfloat16).reshape(DSSM, NS)
    if not gains:
        total = jnp.concatenate([total, gain_rows(gain * other)], axis=0)
    if after is not None:
        total = tie(total, after)
    totals = lax.all_gather(total, "ctx", axis_index_groups=ctx_lines())
    if not gains:
        line_gains = read_gain(totals[:, DSSM:])
    totals = by_head(totals[:, :DSSM])
    factor = jnp.ones((HM,), jnp.float32)
    entering = jnp.zeros((HM, PM, NS), jnp.float32)
    lines = range(count // 2)
    for at in lines if reverse else reversed(lines):
        reached = at > line_at if reverse else at < line_at
        entering = entering + jnp.where(reached, factor, 0.0)[:, None, None] * totals[at]
        factor = factor * jnp.where(reached, line_gains[at], 1.0)
    state = jnp.where(is_first, entering, first_gain * entering + first)
    return state.astype(jnp.bfloat16).reshape(DSSM, NS), (gain, other, line_gains), total


def pack_small(norm, conv_weight, conv_bias, skip, mixer, ffn, shards):
    pieces = [
        norm.reshape(shards, -1),
        conv_weight.reshape(KW, shards, -1).transpose(1, 0, 2).reshape(shards, -1),
        conv_bias.reshape(shards, -1),
        mixer.reshape(shards, -1),
        ffn.reshape(shards, -1),
        skip.reshape(shards, -1),
    ]
    packed = jnp.concatenate(pieces, axis=1)
    packed = jnp.pad(packed, ((0, 0), (0, 4096 - packed.shape[1])))
    return packed.reshape(shards * 32, 128)


def unpack_small(packed, model, channels, heads, shards):
    packed = packed.reshape(shards, 4096)
    sizes = [model, KW * channels, channels, DSSM, model, heads]
    parts, start = [], 0
    for size in sizes:
        width = size // 4
        parts.append(packed[:, start : start + width])
        start += width
    norm, conv_weight, conv_bias, mixer, ffn, skip = parts
    conv_weight = conv_weight.reshape(shards, KW, -1).transpose(1, 0, 2).reshape(KW, -1)
    return (
        norm.reshape(-1),
        conv_weight,
        conv_bias.reshape(-1),
        skip.reshape(-1),
        mixer.reshape(-1),
        ffn.reshape(-1),
    )


def per_device(
    tokens,
    cotangent,
    doc_lengths,
    decay,
    norm_gain,
    in_proj,
    conv_weight,
    conv_bias,
    skip_gain,
    mixer_gain,
    mixer_out,
    query_proj,
    key_value_projection,
    attn_out,
    ffn_gain,
    gate_up,
    down_proj,
):
    rows, model = tokens.shape[1:]
    width = rows // 2
    shards = lax.axis_size("wshard")
    channels = conv_bias.shape[0] * shards
    count, block_at = lax.axis_size("ctx"), lax.axis_index("ctx")
    sequence_total = rows * count
    heads_per_group = QUERY_HEADS // KEY_VALUE_HEADS
    scale = HEAD_SIZE ** (-0.5)
    attend_forward, attend_backward = attention_calls(rows, count, (3, 3))
    state_outer, mixer_join, mixer_forward, mixer_backward = mixer_calls(rows, 4)

    lengths = doc_lengths[0]
    doc_count = lengths.shape[0]
    position_index = block_at * rows + jnp.arange(rows, dtype=jnp.int32)
    docs = doc_numbers(lengths, position_index)
    doc_prev = doc_numbers(lengths, position_index[:1] - 1)[0]
    log_decay = jnp.log(decay[0])
    mirrored = count - 1 - block_at
    group_blocks = jnp.stack([block_at, mirrored]).astype(jnp.int32)
    group_positions = jnp.stack(
        [
            block_at * rows + jnp.arange(width, dtype=jnp.int32),
            mirrored * rows + width + jnp.arange(width, dtype=jnp.int32),
        ]
    )
    group_docs = jnp.stack([doc_numbers(lengths, group_positions[at]) for at in range(2)])
    key_docs = doc_numbers(lengths, jnp.arange(sequence_total, dtype=jnp.int32))
    lane = jnp.arange(128)[None, :]
    key_side = ((key_docs[:, None] == lane) | ((lane >= 8) & (lane < 11))).astype(jnp.bfloat16)
    side_row = jnp.arange(16)[None, :, None]
    query_side = jnp.where(
        (side_row == group_docs[:, None, :]) | (side_row >= doc_count), 0.0, mask_fill_value
    ).astype(jnp.bfloat16)

    order = jnp.arange(rows)
    running = jnp.dot(
        log_decay, (order[:, None] <= order[None, :]).astype(jnp.float32), precision=highest
    )
    entry = jnp.where((docs == doc_prev)[None, :], jnp.exp(running), 0.0)
    tail = jnp.where((docs == docs[-1])[None, :], jnp.exp(running[:, -1:] - running), 0.0)
    carry_gain = jnp.where(docs[-1] == doc_prev, jnp.exp(running[:, -1]), 0.0)

    mixer_rows = (
        jnp.stack([running, entry, tail, jnp.zeros_like(tail)])
        .reshape(4, HM // 2, 2, rows)
        .transpose(1, 0, 2, 3)
        .reshape(HM // 2, 8, rows)
    )
    taps = jnp.stack(
        [
            (doc_numbers(lengths, position_index - (KW - 1) + tap) == docs).astype(jnp.float32)
            for tap in range(KW)
        ]
    )
    docs_column, docs_row = docs[:, None], docs[None, :]
    cosine, sine = turn_tables(position_index)
    mirrored_cosine, mirrored_sine = turn_tables(group_positions[1])
    prepared = lax.optimization_barrier(
        (
            key_side,
            query_side,
            mixer_rows,
            taps,
            docs_column,
            docs_row,
            cosine,
            sine,
            mirrored_cosine,
            mirrored_sine,
            group_blocks,
        )
    )
    (
        key_side,
        query_side,
        mixer_rows,
        taps,
        docs_column,
        docs_row,
        cosine,
        sine,
        mirrored_cosine,
        mirrored_sine,
        group_blocks,
    ) = prepared
    packed = pack_small(norm_gain, conv_weight, conv_bias, skip_gain, mixer_gain, ffn_gain, 1)
    first_shard = jnp.concatenate([in_proj, query_proj, key_value_projection], axis=1)
    packed = jnp.pad(packed.reshape(1, -1), ((0, 15), (0, first_shard.shape[1] - 4096)))
    first_w, small, arrived = gather_first(
        jnp.concatenate([first_shard, packed], axis=0), in_proj.shape[0], prepared
    )
    norm_w, conv_w, conv_b, skip_w, mixer_g, ffn_g = (
        part.astype(jnp.float32)
        for part in unpack_small(small[:, :4096], model, channels, HM, shards)
    )
    projected_width = in_proj.shape[1]
    in_w, attn_pair_w = first_w[:, :projected_width], first_w[:, projected_width:]
    out_pieces = start_shards(
        jnp.concatenate([mixer_out, attn_out, down_proj], axis=0), arrived
    )
    gate_up_pieces = start_shards(gate_up, arrived)
    source = tokens[0].astype(jnp.float32)
    normed, norm_pull = jax.vjp(rms_scale, source, norm_w)
    normed_b = normed.astype(jnp.bfloat16)
    projected = mixed_dot(normed_b, first_w)

    query_width = QUERY_HEADS * HEAD_SIZE
    attn_inputs = projected[:, projected_width:].T
    turned_q = turn(
        attn_inputs[:query_width].reshape(QUERY_HEADS, HEAD_SIZE, rows), cosine, sine
    ).astype(jnp.bfloat16)
    key_value_pair = attn_inputs[query_width:].reshape(2, KEY_VALUE_HEADS, HEAD_SIZE, rows)
    keys_b = turn(key_value_pair[0], cosine, sine).astype(jnp.bfloat16)
    values_b = key_value_pair[1].astype(jnp.bfloat16)
    pairs = lax.all_gather(
        jnp.concatenate([keys_b, values_b], axis=1).transpose(0, 2, 1), "ctx"
    )
    turned_q = turned_q * jnp.asarray(scale, jnp.bfloat16)
    mirrored_q = swap_mirrored(turned_q[:, :, width:])

    gate_z = projected[:, :DSSM]
    pre_b = projected[:, DSSM:projected_width].astype(jnp.bfloat16)
    rim = from_behind(pre_b[rows - (KW - 1) :], "ctx", 1)
    extended = jnp.concatenate([rim, pre_b], axis=0).astype(jnp.float32)
    conv_f, conv_pull = jax.vjp(partial(conv_local, taps), extended, conv_w, conv_b)
    conv_b16 = conv_f.astype(jnp.bfloat16)
    skip_wide = jnp.repeat(skip_w, PM).reshape(HM // 2, 1, 2 * PM)
    fresh = state_outer(DSSM // NS, 4, 0)(mixer_rows, conv_b16, conv_b16)
    state_in, gains, _ = pass_state(fresh, carry_gain, None, False, pairs)
    local = mixer_forward(
        skip_wide, conv_b16, conv_b16, conv_b16, mixer_rows, docs_column, docs_row
    )

    heads_own, heads_mirrored, log_x = attend_forward(
        group_blocks,
        pairs,
        key_side,
        turned_q,
        mirrored_q,
        query_side,
        out_pieces[1],
        gate_up_pieces[1],
        local,
    )
    mixer_w, attn_w, down_w = finish_shards(
        out_pieces,
        [mixer_out.shape[0], attn_out.shape[0], down_proj.shape[0]],
        log_x,
    )
    (gate_up_w,) = finish_shards(gate_up_pieces, [gate_up.shape[0]], log_x)
    heads_back = swap_mirrored(heads_mirrored.astype(jnp.bfloat16))
    heads_t = jnp.concatenate([heads_own.astype(jnp.bfloat16), heads_back], axis=2).reshape(
        QUERY_HEADS * HEAD_SIZE, rows
    )
    mixed = mixer_join(0)(conv_b16, mixer_rows, state_in, local)
    gated, gate_pull = jax.vjp(gate_norm, mixed, gate_z, mixer_g)
    gated_b = gated.astype(jnp.bfloat16)
    mamba = mixed_dot(gated_b, mixer_w)
    attn = lax.dot_general(
        heads_t, attn_w, (((0,), (0,)), ((), ())), preferred_element_type=jnp.float32
    )
    middle = source + attn + mamba
    normed2, ffn_pull = jax.vjp(rms_scale, middle, ffn_g)
    normed2_b = normed2.astype(jnp.bfloat16)
    gate_up_v = mixed_dot(normed2_b, gate_up_w)
    activated, act_pull = jax.vjp(swiglu, gate_up_v)
    activated_b = activated.astype(jnp.bfloat16)
    layer_out = (middle + mixed_dot(activated_b, down_w)).astype(jnp.bfloat16)

    out_low = cotangent[0]
    down_sum, down_beside, down_across, _ = weight_grad(activated_b, out_low)
    (gate_up_grad_v,) = act_pull(nt_dot(out_low, down_w))
    gate_up_low = gate_up_grad_v.astype(jnp.bfloat16)
    gate_up_sum, gate_up_beside, _, gate_up_sent = weight_grad(normed2_b, gate_up_low)
    gate_up_half, gate_up_got, gate_up_give = ctx_half([gate_up_sum], model // shards)
    middle_norm_grad, ffn_gain_grad = ffn_pull(nt_dot(gate_up_low, gate_up_w))
    middle_grad = out_low.astype(jnp.float32) + middle_norm_grad
    middle_low = middle_grad.astype(jnp.bfloat16)
    heads_low = nt_dot(attn_w, middle_low).astype(jnp.bfloat16)
    heads_low = heads_low.reshape(QUERY_HEADS, HEAD_SIZE, rows)
    mirrored_low = swap_mirrored(heads_low[:, :, width:])
    gated_grad = nt_dot(middle_low, mixer_w)
    mixed_grad, gate_z_grad, mixer_gain_grad = gate_pull(gated_grad)
    upward = state_outer(DSSM // NS + 1, 2, 2)(
        mixer_rows, mixed_grad.astype(jnp.bfloat16), conv_b16, down_beside, gate_up_sent
    )
    state_out_grad, _, pair_total = pass_state(upward, None, gains, True)
    down_half, down_got, _ = ctx_half([tie(down_sum, upward)], model // shards)
    gate_z_low = gate_z_grad.astype(jnp.bfloat16)
    query_grad_own, query_grad_mirrored, pairs_grad = attend_backward(
        group_blocks,
        pairs,
        key_side,
        turned_q,
        mirrored_q,
        query_side,
        log_x,
        heads_own,
        heads_mirrored,
        heads_low,
        mirrored_low,
        gate_up_beside,
        down_across,
        pair_total,
    )
    mixer_products = split_products(gated_b, middle_low)
    attn_products = split_products(heads_t, middle_low, 0)
    shard_sizes = [mixer_out.shape[0], attn_out.shape[0]]

    def interleaved(parts):
        return jnp.concatenate(
            [
                part[start * size : (start + 1) * size]
                for start in range(parts[0].shape[0] // shard_sizes[0])
                for part, size in zip(parts, shard_sizes)
            ],
            axis=0,
        ).astype(jnp.bfloat16)

    mixer_attn_started = start_sum(
        *[interleaved(parts) for parts in zip(mixer_products, attn_products)], pairs_grad
    )
    in_z_started = start_sum(*split_products(normed_b, gate_z_low), pairs_grad)
    query_low_own, query_low_mirrored = (
        (turn(grad, *tables) * scale).astype(jnp.bfloat16)
        for grad, tables in (
            (query_grad_own, (cosine[:, :width], -sine[:, :width])),
            (query_grad_mirrored, (mirrored_cosine, -mirrored_sine)),
        )
    )
    query_low = jnp.concatenate(
        [query_low_own, swap_mirrored(query_low_mirrored)], axis=2
    ).reshape(QUERY_HEADS * HEAD_SIZE, rows)

    conv_grad, skip_parts = mixer_backward(
        skip_wide,
        conv_b16,
        conv_b16,
        conv_b16,
        mixer_rows,
        docs_column,
        docs_row,
        state_in,
        state_out_grad,
        mixed_grad,
        gate_up_give,
        in_z_started[1],
        down_got,
        mixer_attn_started[1],
    )
    pair_grad = scatter_blocks(pairs_grad, conv_grad).astype(jnp.float32).transpose(0, 2, 1)
    skip_grad = jnp.sum(skip_parts.reshape(HM, PM), axis=1)
    extended_grad, conv_weight_grad, conv_bias_grad = conv_pull(conv_grad)
    from_above = from_behind(extended_grad[: KW - 1], "ctx", -1)
    pre_grad = extended_grad[KW - 1 :] + jnp.pad(from_above, ((rows - (KW - 1), 0), (0, 0)))
    pre_low = tie(pre_grad.astype(jnp.bfloat16), gate_up_got)
    mixer_attn_sum = finish_sum(mixer_attn_started, pre_low)
    in_sum_z = finish_sum(in_z_started, pre_low)
    mixer_half, _, _ = ctx_half([mixer_attn_sum, in_sum_z], model // shards)
    in_sum_pre = weight_grad(normed_b, pre_low)[0]
    projected_low = jnp.concatenate([gate_z_low, pre_low], axis=1)
    normed_grad = nt_dot(projected_low, in_w)

    keys_low = turn(pair_grad[:, :HEAD_SIZE], cosine, -sine)
    keyval_low = jnp.concatenate(
        [
            keys_low.reshape(KEY_VALUE_HEADS * HEAD_SIZE, rows),
            pair_grad[:, HEAD_SIZE:].reshape(KEY_VALUE_HEADS * HEAD_SIZE, rows),
        ],
        axis=0,
    ).astype(jnp.bfloat16)
    attn_pair_low = jnp.concatenate([query_low, keyval_low], axis=0).T
    attn_pair_sum = weight_grad(normed_b, attn_pair_low)[0]
    normed_grad = normed_grad + nt_dot(attn_pair_low, attn_pair_w)
    source_grad, norm_grad = norm_pull(normed_grad)
    tokens_grad = (middle_grad + source_grad)[None]

    small_grad = pack_small(
        norm_grad, conv_weight_grad, conv_bias_grad, skip_grad, mixer_gain_grad, ffn_gain_grad, shards
    )
    small_share = sum_small(small_grad)
    last_half, _, _ = ctx_half([in_sum_pre, attn_pair_sum], model // shards)
    (gate_up_share,), summed = ctx_finish(
        tie(gate_up_half, state_out_grad), [gate_up_sum.shape], 1
    )
    (down_share,), summed = ctx_finish(tie(down_half, summed), [down_sum.shape], 0)
    (mixer_attn_share, in_share_z), summed = ctx_finish(
        tie(mixer_half, summed), [mixer_attn_sum.shape, in_sum_z.shape], 2
    )
    mixer_share = mixer_attn_share[: mixer_out.shape[0]]
    attn_share = mixer_attn_share[mixer_out.shape[0] :]
    (in_share_pre, attn_pair_share), _ = ctx_finish(
        tie(last_half, summed),
        [in_sum_pre.shape, attn_pair_sum.shape],
        3,
    )
    norm_share, conv_w_share, conv_b_share, skip_share, mixer_g_share, ffn_share = unpack_small(
        small_share, model, channels, HM, 1
    )
    return (
        layer_out[None],
        tokens_grad,
        norm_share,
        jnp.concatenate([in_share_z, in_share_pre], axis=1),
        conv_w_share,
        conv_b_share,
        skip_share,
        mixer_g_share,
        mixer_share,
        attn_pair_share[:, : QUERY_HEADS * HEAD_SIZE],
        attn_pair_share[:, QUERY_HEADS * HEAD_SIZE :],
        attn_share,
        ffn_share,
        gate_up_share,
        down_share,
    )


def solution(mesh):
    in_specs = (
        P("wshard", "ctx", None),
        P("wshard", "ctx", None),
        P("wshard", None),
        P("wshard", None, "ctx"),
        P("wshard"),
        P("wshard", None),
        P(None, "wshard"),
        P("wshard"),
        P("wshard"),
        P("wshard"),
        P("wshard", None),
        P("wshard", None),
        P("wshard", None),
        P("wshard", None),
        P("wshard"),
        P("wshard", None),
        P("wshard", None),
    )
    out_specs = (
        P("wshard", "ctx", None),
        P("wshard", "ctx", None),
        P("wshard"),
        P("wshard", None),
        P(None, "wshard"),
        P("wshard"),
        P("wshard"),
        P("wshard"),
        P("wshard", None),
        P("wshard", None),
        P("wshard", None),
        P("wshard", None),
        P("wshard"),
        P("wshard", None),
        P("wshard", None),
    )
    return jax.shard_map(
        per_device, mesh=mesh, in_specs=in_specs, out_specs=out_specs, check_vma=False
    )
```

```python
from functools import partial

import jax
import jax.numpy as jnp
from jax import lax
from jax.experimental import pallas as pl
from jax.experimental.pallas import tpu as pltpu
from jax.sharding import PartitionSpec as P

FF = 2048
QUERY_HEADS = 8
KEY_VALUE_HEADS = 2
HEAD_SIZE = 64
HM = 24
PM = 64
NS = 128
KW = 4
DSSM = 1536

eps_norm = 1e-05
rope_base = 100000000000.0
mask_fill_value = -1e30
highest = lax.Precision.HIGHEST
MESH_AXES = ("ctx", "wshard")
small_cost = pl.CostEstimate(flops=1024, bytes_accessed=1024, transcendentals=0)


def exchange(block, ctx_flip, shard_flip):
    blocks, shards = lax.axis_size("ctx"), lax.axis_size("wshard")
    route = [
        (c * shards + w, (c ^ ctx_flip) * shards + (w ^ shard_flip))
        for c in range(blocks)
        for w in range(shards)
    ]
    return lax.ppermute(block, MESH_AXES, route)


def from_behind(block, axis, distance):
    devices = range(lax.axis_size(axis))
    route = [(i - distance, i) for i in devices if i - distance in devices]
    return lax.ppermute(block, axis, route)


def swap_mirrored(block):
    count = lax.axis_size("ctx")
    return lax.ppermute(block, "ctx", [(i, count - 1 - i) for i in range(count)])


def tie_body(*refs):
    pass


def tie(value, *after):
    anywhere = pl.BlockSpec(memory_space=pl.ANY)
    return pl.pallas_call(
        tie_body,
        in_specs=[anywhere] * (1 + len(after)),
        out_specs=anywhere,
        out_shape=jax.ShapeDtypeStruct(value.shape, value.dtype),
        input_output_aliases={0: 0},
        cost_estimate=pl.CostEstimate(flops=0, bytes_accessed=0, transcendentals=0),
        name="tie",
    )(value, *after)


def assemble_body(spans, target_ref, *refs):
    out_ref = refs[-1]
    step = pl.program_id(0)
    for piece, (first, size) in zip(refs, spans):

        def put(piece=piece):
            out_ref[...] = piece[...]

        pl.when((step >= first) & (step < first + size))(put)


def assemble(pieces, rows, anchors=()):
    spans, offsets, targets = [], [], []
    for _, source, start, size in pieces:
        spans.append((len(targets), size // rows))
        offsets.append(source // rows)
        targets += [start // rows + at for at in range(size // rows)]
    columns, kind = pieces[0][0].shape[1], pieces[0][0].dtype

    def source_map(offset, first, size):
        return lambda i, target: (offset + jnp.clip(i - first, 0, size - 1), 0)

    return pl.pallas_call(
        partial(assemble_body, spans),
        grid_spec=pltpu.PrefetchScalarGridSpec(
            num_scalar_prefetch=1,
            grid=(len(targets),),
            in_specs=[
                pl.BlockSpec((rows, columns), source_map(offset, first, size))
                for offset, (first, size) in zip(offsets, spans)
            ]
            + [pl.BlockSpec(memory_space=pl.ANY)] * len(anchors),
            out_specs=pl.BlockSpec((rows, columns), lambda i, target: (target[i], 0)),
        ),
        out_shape=jax.ShapeDtypeStruct((rows * len(targets), columns), kind),
        compiler_params=pltpu.CompilerParams(
            dimension_semantics=("arbitrary",), vmem_limit_bytes=32 * 1024 * 1024
        ),
        cost_estimate=small_cost,
        name="assemble",
    )(jnp.stack([jnp.asarray(target, jnp.int32) for target in targets]), *[p[0] for p in pieces], *anchors)


def gather_first(shard, rows, anchors):
    part = rows // 4
    w = lax.axis_index("wshard")
    side = lax.axis_index("ctx") % 2
    direct = shard[2 * part :]
    across = exchange(lax.dynamic_slice_in_dim(shard, side * part, part, 0), 0, 2)
    across_direct = exchange(direct, 0, 2)
    beside = exchange(shard, 0, 1)
    across_relayed = exchange(across, 1, 0)
    far, far_direct, far_relayed = (
        exchange(piece, 0, 1) for piece in (across, across_direct, across_relayed)
    )
    pieces = [(shard, 0, w * rows, rows), (beside, 0, (w ^ 1) * rows, rows)]
    for flip, early, late, rest in (
        (2, across, across_relayed, across_direct),
        (3, far, far_relayed, far_direct),
    ):
        start = (w ^ flip) * rows
        pieces.append((early, 0, start + side * part, part))
        pieces.append((late, 0, start + (1 - side) * part, part))
        pieces.append((rest, 0, start + 2 * part, 2 * part))
    tails = [shard[rows:], beside[rows:], across_direct[2 * part :], far_direct[2 * part :]]
    tails = jnp.concatenate([tail[:1] for tail in tails], axis=0)
    small = jnp.concatenate(
        [lax.dynamic_slice_in_dim(tails, w ^ at, 1, 0) for at in range(4)], axis=0
    )
    return assemble(pieces, part, anchors), small, across_direct


def start_shards(stacked, after):
    stacked, _ = lax.optimization_barrier((stacked, after))
    return stacked, exchange(stacked, 0, 1), exchange(stacked, 0, 2)


def finish_shards(pieces, sizes, after):
    own, beside, across = pieces
    far = exchange(lax.optimization_barrier((across, after))[0], 0, 1)
    w = lax.axis_index("wshard")
    wholes, source = [], 0
    for size in sizes:
        wholes.append(
            assemble(
                [
                    (part, source, (w ^ flip) * size, size)
                    for flip, part in enumerate((own, beside, across, far))
                ],
                size,
            )
        )
        source += size
    return wholes


def add_low(first, *others):
    total = first.astype(jnp.float32)
    for other in others:
        total = total + other.astype(jnp.float32)
    return total.astype(jnp.bfloat16)


def lay_side_by_side(blocks, rows):
    parts = []
    for block in blocks:
        for start in range(0, block.shape[0], rows):
            part = block[start : start + rows]
            parts.append(jnp.pad(part, ((0, rows - part.shape[0]), (0, 0))))
    return jnp.concatenate(parts, axis=1)


def take_apart(array, shapes):
    rows, start, blocks = array.shape[0], 0, []
    for height, columns in shapes:
        parts = []
        for _ in range(0, height, rows):
            parts.append(array[: min(height, rows), start : start + columns])
            start += columns
        blocks.append(parts[0] if len(parts) == 1 else jnp.concatenate(parts, axis=0))
    return blocks


def ctx_half(blocks, rows):
    side = lax.axis_index("ctx") % 2
    whole = lay_side_by_side(blocks, rows)
    half = rows // 2
    give = lax.dynamic_slice_in_dim(whole, (1 - side) * half, half, 0)
    got = exchange(give, 1, 0)
    return add_low(lax.dynamic_slice_in_dim(whole, side * half, half, 0), got), got, give


def ctx_lines():
    count = lax.axis_size("ctx")
    return [list(range(start, count, 2)) for start in range(2)]


def line_sum(mine, turn_at):
    lines = ctx_lines()
    if turn_at % 2:
        lines = lines[::-1]
    if turn_at // 2:
        lines = [line[::-1] for line in lines]
    return lax.psum(mine, "ctx", axis_index_groups=lines)


def ctx_finish(mine, shapes):
    side = lax.axis_index("ctx") % 2
    got = exchange(mine, 1, 0)
    whole = jnp.where(
        side == 0, jnp.concatenate([mine, got], axis=0), jnp.concatenate([got, mine], axis=0)
    ).astype(jnp.float32)
    return take_apart(whole, shapes)


def shard_pieces(array, axis):
    w = lax.axis_index("wshard")
    size = array.shape[axis] // 4

    def piece(flip):
        return lax.dynamic_slice_in_dim(array, (w ^ flip) * size, size, axis)

    return jnp.concatenate([piece(1), piece(3)], axis=axis), piece(2), piece(0)


def shard_sum(beside, across, own):
    rows = own.shape[0]
    got = exchange(beside.astype(jnp.bfloat16), 0, 1)
    sent = add_low(across, got[rows:])
    got_across = exchange(sent, 0, 2)
    return add_low(own, got[:rows], got_across), got, got_across, sent


def split_products(left, right, axis=1):
    return [
        lax.dot_general(
            piece, right, (((1 - axis,), (0,)), ((), ())), preferred_element_type=jnp.float32
        )
        for piece in shard_pieces(left, axis)
    ]


def weight_grad(left, right):
    return shard_sum(*split_products(left, right))


def start_sum(beside, across, own, after):
    rows = own.shape[0]
    got = exchange(beside.astype(jnp.bfloat16), 0, 1)
    got_across = exchange(tie(add_low(across, got[rows:]), after), 0, 2)
    return own, got, got_across


def finish_sum(started, after):
    own, got, got_across = started
    if after is not None:
        got_across = tie(got_across, after)
    return add_low(own, got[: own.shape[0]], got_across)


def sum_small(value):
    rows = value.shape[0] // 4
    for flip in (1, 2):
        value = value + exchange(value, 0, flip)
    value = lax.dynamic_slice_in_dim(value, lax.axis_index("wshard") * rows, rows, 0)
    bit = 1
    while bit < lax.axis_size("ctx"):
        value = value + exchange(value, bit, 0)
        bit *= 2
    return value


def scatter_blocks(blocks, after):
    position, bit = lax.axis_index("ctx"), 1
    while blocks.shape[0] > 1:
        up = (position // bit) % 2
        halves = blocks.reshape((blocks.shape[0] // 2, 2) + blocks.shape[1:])
        keep = lax.dynamic_index_in_dim(halves, up, 1, keepdims=False)
        give = lax.dynamic_index_in_dim(halves, 1 - up, 1, keepdims=False)
        got = exchange(give, bit, 0)
        if bit == 1:
            got = tie(got, after)
        blocks = add_low(keep, got)
        bit *= 2
    return blocks[0]


def mixed_dot(left, right):
    return jnp.dot(left, right, preferred_element_type=jnp.float32)


def rms_scale(value, gain):
    return value * lax.rsqrt(jnp.mean(value * value, axis=-1, keepdims=True) + eps_norm) * gain


def doc_numbers(lengths, position_index):
    ends = jnp.cumsum(lengths)[:-1]
    tally_count = jnp.sum((position_index[:, None] >= ends[None, :]).astype(jnp.int32), axis=1)
    return jnp.where(position_index >= 0, tally_count, -1)


def turn_tables(position_index):
    half = HEAD_SIZE // 2
    freq = rope_base ** (-jnp.arange(half, dtype=jnp.float32) / half)
    angle = freq[:, None] * position_index.astype(jnp.float32)[None, :]
    return jnp.cos(angle), jnp.sin(angle)


def turn(value, cosine, sine):
    half = value.shape[-2] // 2
    first = value[..., :half, :]
    second = value[..., half:, :]
    return jnp.concatenate(
        [first * cosine - second * sine, second * cosine + first * sine], axis=-2
    )


def conv_local(taps, extended, weight, bias):
    tally_count = extended.shape[0] - (KW - 1)
    total = bias[None, :]
    for tap in range(KW):
        total = (
            total + weight[tap][None, :] * extended[tap : tap + tally_count] * taps[tap][:, None]
        )
    return jax.nn.silu(total)


def gate_norm(mixed, gate_z, gain):
    return rms_scale(mixed * jax.nn.silu(gate_z), gain)


def swiglu(gate_up_v):
    return jax.nn.silu(gate_up_v[:, :FF]) * gate_up_v[:, FF:]


def split_three(value):
    high = value.astype(jnp.bfloat16)
    rest = value - high.astype(jnp.float32)
    middle = rest.astype(jnp.bfloat16)
    low = (rest - middle.astype(jnp.float32)).astype(jnp.bfloat16)
    return [high, middle, low]


def nt_dot(left, right):
    return lax.dot_general(left, right, (((1,), (1,)), ((), ())), preferred_element_type=jnp.float32)


def causal_tile(scores, group, width):
    rows = lax.broadcasted_iota(jnp.int32, scores.shape, 0)
    columns = lax.broadcasted_iota(jnp.int32, scores.shape, 1)
    return jnp.where(rows <= lax.rem(columns, width) + group * width, scores, mask_fill_value)


def load_extended(extended, group, lower, value_ref, side, extra):
    width = value_ref.shape[2]
    extended[group] = jnp.zeros(extended.shape[1:], extended.dtype)
    for head in range(value_ref.shape[0]):
        here = slice(head * width, (head + 1) * width)
        extended[group, lower : lower + HEAD_SIZE, here] = value_ref[head]
    side = jnp.concatenate([side.astype(jnp.float32)] * value_ref.shape[0], axis=1)
    if extra is not None:
        row = lax.broadcasted_iota(jnp.int32, side.shape, 0)
        for at, part in enumerate(split_three(-extra)):
            side = jnp.where(row == 8 + at, part.astype(jnp.float32), side)
    extended[group, 128:144, :] = side.astype(extended.dtype)


def attend_forward_body(width, blocks, pair_ref, side_ref, query_a, query_b, query_side_ref, *refs):
    heads_refs, (log_ref, query_x, peak, total) = refs[-6:-4], refs[-4:]
    step = pl.program_id(1)

    @pl.when(step == 0)
    def start():
        for group, query_ref in enumerate((query_a, query_b)):
            load_extended(query_x, group, 0, query_ref, query_side_ref[group], None)
        peak[...] = jnp.full(peak.shape, mask_fill_value, jnp.float32)
        total[...] = jnp.zeros(total.shape, jnp.float32)

    @pl.when(step <= jnp.maximum(blocks[0], blocks[1]))
    def work():
        keys = jnp.concatenate([pair_ref[0, 0], side_ref[...]], axis=1)
        values = keys.T[HEAD_SIZE:144]

        def tile(group, masked):
            scores = mixed_dot(keys, query_x[group])
            if masked:
                scores = causal_tile(scores, group, width)
            old = peak[group]
            new = jnp.maximum(old, jnp.max(scores, axis=0, keepdims=True))
            probs = jnp.exp(scores - new)
            total[group] = total[group] * jnp.exp(old - new) + mixed_dot(
                values, probs.astype(jnp.bfloat16)
            )
            peak[group] = new

        for group in range(2):
            pl.when(step < blocks[group])(partial(tile, group, False))
            pl.when(step == blocks[group])(partial(tile, group, True))

    @pl.when(step == pl.num_programs(1) - 1)
    def finish():
        for group in range(2):
            weight = total[group, HEAD_SIZE + 8 : HEAD_SIZE + 9, :]
            heads = total[group, :HEAD_SIZE, :] / weight
            for head in range(heads.shape[1] // width):
                heads_refs[group][head] = heads[:, head * width : (head + 1) * width]
            log_ref[group, 0] = peak[group] + jnp.log(weight)


def attend_backward_body(
    width,
    blocks,
    pair_ref,
    side_ref,
    query_a,
    query_b,
    query_side_ref,
    log_ref,
    heads_a,
    heads_b,
    grad_a,
    grad_b,
    *refs,
):
    query_grad_refs, (pair_grad_ref, query_x, grad_x, pair_acc, query_acc) = refs[-7:-5], refs[-5:]
    step = pl.program_id(1)

    @pl.when(step == 0)
    def start():
        groups = ((query_a, heads_a, grad_a), (query_b, heads_b, grad_b))
        for group, (query_ref, heads_ref, grad_ref) in enumerate(groups):
            load_extended(query_x, group, 0, query_ref, query_side_ref[group], log_ref[group, 0])
            delta = [
                jnp.sum(heads_ref[head] * grad_ref[head].astype(jnp.float32), axis=0, keepdims=True)
                for head in range(heads_ref.shape[0])
            ]
            blank = jnp.zeros(query_side_ref.shape[1:], jnp.float32)
            load_extended(
                grad_x, group, HEAD_SIZE, grad_ref, blank, jnp.concatenate(delta, axis=1)
            )
        query_acc[...] = jnp.zeros(query_acc.shape, jnp.float32)

    pair_acc[...] = jnp.zeros(pair_acc.shape, jnp.float32)

    @pl.when(step <= jnp.maximum(blocks[0], blocks[1]))
    def work():
        pair = pair_ref[0, 0]
        keys = jnp.concatenate([pair, side_ref[...]], axis=1)
        turned = pair.T[:HEAD_SIZE]

        def tile(group, masked):
            scores = mixed_dot(keys, query_x[group])
            if masked:
                scores = causal_tile(scores, group, width)
            probs = jnp.exp(scores)
            low = (probs * mixed_dot(keys, grad_x[group])).astype(jnp.bfloat16)
            pair_acc[...] += nt_dot(low, query_x[group, :128, :]) + nt_dot(
                probs.astype(jnp.bfloat16), grad_x[group, :128, :]
            )
            query_acc[group] += mixed_dot(turned, low)

        for group in range(2):
            pl.when(step < blocks[group])(partial(tile, group, False))
            pl.when(step == blocks[group])(partial(tile, group, True))

    pair_grad_ref[0, 0] = pair_acc[...].astype(jnp.bfloat16)

    @pl.when(step == pl.num_programs(1) - 1)
    def finish():
        for group in range(2):
            for head in range(query_acc.shape[2] // width):
                query_grad_refs[group][head] = query_acc[group, :, head * width : (head + 1) * width]


def attention_calls(rows, count, anchors):
    width = rows // 2
    span = width * (QUERY_HEADS // KEY_VALUE_HEADS)

    def last(blocks):
        return jnp.maximum(blocks[0], blocks[1])

    pair_spec = pl.BlockSpec(
        (1, 1, rows, 128), lambda g, k, blocks: (jnp.minimum(k, last(blocks)), g, 0, 0)
    )
    side_spec = pl.BlockSpec((rows, 128), lambda g, k, blocks: (jnp.minimum(k, last(blocks)), 0))

    heads_per_group = QUERY_HEADS // KEY_VALUE_HEADS
    own = pl.BlockSpec((heads_per_group, HEAD_SIZE, width), lambda g, k, blocks: (g, 0, 0))
    half_spec = own
    log_spec = pl.BlockSpec((2, 1, 1, span), lambda g, k, blocks: (0, g, 0, 0))
    query_side_spec = pl.BlockSpec((2, 16, width), lambda g, k, blocks: (0, 0, 0))
    half_shape = jax.ShapeDtypeStruct((QUERY_HEADS, HEAD_SIZE, width), jnp.float32)

    anywhere = pl.BlockSpec(memory_space=pl.ANY)
    params = pltpu.CompilerParams(
        dimension_semantics=("arbitrary", "arbitrary"), vmem_limit_bytes=48 * 1024 * 1024
    )
    forward = pl.pallas_call(
        partial(attend_forward_body, width),
        grid_spec=pltpu.PrefetchScalarGridSpec(
            num_scalar_prefetch=1,
            grid=(KEY_VALUE_HEADS, count),
            in_specs=[pair_spec, side_spec, own, half_spec, query_side_spec]
            + [anywhere] * anchors[0],
            out_specs=[half_spec, half_spec, log_spec],
            scratch_shapes=[
                pltpu.VMEM((2, 256, span), jnp.bfloat16),
                pltpu.VMEM((2, 1, span), jnp.float32),
                pltpu.VMEM((2, 144 - HEAD_SIZE, span), jnp.float32),
            ],
        ),
        out_shape=[
            half_shape,
            half_shape,
            jax.ShapeDtypeStruct((2, KEY_VALUE_HEADS, 1, span), jnp.float32),
        ],
        compiler_params=params,
        cost_estimate=small_cost,
        name="attend_forward",
    )
    backward = pl.pallas_call(
        partial(attend_backward_body, width),
        grid_spec=pltpu.PrefetchScalarGridSpec(
            num_scalar_prefetch=1,
            grid=(KEY_VALUE_HEADS, count),
            in_specs=[
                pair_spec,
                side_spec,
                own,
                half_spec,
                query_side_spec,
                log_spec,
                half_spec,
                half_spec,
                own,
                half_spec,
            ]
            + [anywhere] * anchors[1],
            out_specs=[
                half_spec,
                half_spec,
                pl.BlockSpec((1, 1, rows, 128), lambda g, k, blocks: (k, g, 0, 0)),
            ],
            scratch_shapes=[
                pltpu.VMEM((2, 256, span), jnp.bfloat16),
                pltpu.VMEM((2, 256, span), jnp.bfloat16),
                pltpu.VMEM((rows, 128), jnp.float32),
                pltpu.VMEM((2, HEAD_SIZE, span), jnp.float32),
            ],
        ),
        out_shape=[
            half_shape,
            half_shape,
            jax.ShapeDtypeStruct((count, KEY_VALUE_HEADS, rows, 128), jnp.bfloat16),
        ],
        compiler_params=params,
        cost_estimate=small_cost,
        name="attend_backward",
    )
    return forward, backward


def pick(pair):
    lane = lax.broadcasted_iota(jnp.int32, (pair.shape[0], 2 * PM), 1)
    return jnp.where(lane < PM, pair[:, 0:1], pair[:, 1:2])


def outer_body(kind, rows_ref, left_ref, right_ref, *refs):
    out_ref = refs[-1]
    for at in range(rows_ref.shape[0]):
        scale = pick(rows_ref[at].T[:, kind : kind + 2])
        left = left_ref[:, at * 128 : (at + 1) * 128].astype(jnp.float32) * scale
        out_ref[at * 128 : (at + 1) * 128, :] = lax.dot_general(
            left.astype(jnp.bfloat16),
            right_ref[...],
            (((0,), (0,)), ((), ())),
            preferred_element_type=jnp.float32,
        ).astype(out_ref.dtype)


def join_body(c_ref, rows_ref, state_ref, local_ref, *refs):
    out_ref = refs[-1]
    for at in range(rows_ref.shape[0]):
        here = slice(at * 2 * PM, (at + 1) * 2 * PM)
        inner = nt_dot(c_ref[...], state_ref[here, :])
        out_ref[:, here] = local_ref[:, here] + inner * pick(rows_ref[at].T[:, 2:4])


def mixed_body(
    skip_ref, x_ref, b_ref, c_ref, row_ref, docs_column, docs_row, out_ref, fill, products
):
    rows = x_ref.shape[0]
    half = rows // 2

    @pl.when(pl.program_id(0) == 0)
    def start():
        at = lax.broadcasted_iota(jnp.int32, (rows, rows), 0)
        source = lax.broadcasted_iota(jnp.int32, (rows, rows), 1)
        same = (at >= source) & (docs_column[...] == docs_row[...])
        fill[...] = jnp.where(same, 0.0, mask_fill_value)
        products[...] = nt_dot(c_ref[...], b_ref[...])

    x = x_ref[...]
    columns = row_ref[0].T
    lane = lax.broadcasted_iota(jnp.int32, (half, 2 * PM), 1)
    for block in range(2):
        here = slice(block * half, (block + 1) * half)
        width = (block + 1) * half
        parts = []
        for head in range(2):
            decay = jnp.exp(
                (columns[here, head : head + 1] - row_ref[0, head : head + 1, :width])
                + fill[here, :width]
            )
            weights = (products[here, :width] * decay).astype(jnp.bfloat16)
            parts.append(mixed_dot(weights, x[:width]))
        local = jnp.where(lane < PM, parts[0], parts[1])
        out_ref[here, :] = local + x[here].astype(jnp.float32) * skip_ref[0]


def mixed_grad_body(
    skip_ref,
    x_ref,
    b_ref,
    c_ref,
    row_ref,
    docs_column,
    docs_row,
    state_ref,
    state_grad_ref,
    grad_ref,
    *refs,
):
    out_ref, skip_grad_ref, fill, products, scores, b_grad, c_grad = refs[-7:]
    rows = x_ref.shape[0]
    half = rows // 2
    step = pl.program_id(0)
    pairs = HM // 2

    @pl.when(step == 0)
    def start():
        source = lax.broadcasted_iota(jnp.int32, (rows, rows), 0)
        at = lax.broadcasted_iota(jnp.int32, (rows, rows), 1)
        same = (at >= source) & (docs_column[...] == docs_row[...])
        fill[...] = jnp.where(same, 0.0, mask_fill_value)
        products[...] = nt_dot(b_ref[...], c_ref[...])
        scores[...] = jnp.zeros(scores.shape, jnp.float32)
        b_grad[...] = jnp.zeros(b_grad.shape, jnp.float32)
        c_grad[...] = jnp.zeros(c_grad.shape, jnp.float32)

    @pl.when(step < pairs)
    def work():
        x = x_ref[...]
        x_f = x.astype(jnp.float32)
        grad = grad_ref[...]
        low = grad.astype(jnp.bfloat16)
        lane = lax.broadcasted_iota(jnp.int32, (half, 2 * PM), 1)
        lane_all = lax.broadcasted_iota(jnp.int32, (rows, 2 * PM), 1)
        skip_grad_ref[0] = jnp.sum(grad * x_f, axis=0, keepdims=True)
        state_grad = state_grad_ref[...]
        columns = row_ref[0].T
        tail = pick(columns[:, 4:6])
        b_grad[...] += mixed_dot((x_f * tail).astype(jnp.bfloat16), state_grad)
        entered = (low.astype(jnp.float32) * pick(columns[:, 2:4])).astype(jnp.bfloat16)
        c_grad[...] += mixed_dot(entered, state_ref[...])
        passed = nt_dot(b_ref[...], state_grad) * tail + grad * skip_ref[0]
        chosen = [
            jnp.where((lane_all < PM) == (head == 0), x_f, 0.0).astype(jnp.bfloat16)
            for head in range(2)
        ]
        for block in range(2):
            here = slice(block * half, (block + 1) * half)
            start_at = block * half
            parts = []
            for head in range(2):
                decay = jnp.exp(
                    (row_ref[0, head : head + 1, start_at:] - columns[here, head : head + 1])
                    + fill[here, start_at:]
                )
                weights = (products[here, start_at:] * decay).astype(jnp.bfloat16)
                parts.append(mixed_dot(weights, low[start_at:]))
                scores[here, start_at:] += nt_dot(chosen[head][here], low[start_at:]) * decay
            out_ref[here, :] = jnp.where(lane < PM, parts[0], parts[1]) + passed[here]

    @pl.when(step == pairs)
    def give_b():
        out_ref[...] = b_grad[...] + mixed_dot(scores[...].astype(jnp.bfloat16), c_ref[...])

    @pl.when(step == pairs + 1)
    def give_c():
        out_ref[...] = c_grad[...] + lax.dot_general(
            scores[...].astype(jnp.bfloat16),
            b_ref[...],
            (((0,), (0,)), ((), ())),
            preferred_element_type=jnp.float32,
        )


def mixer_calls(rows, anchors):
    pairs = HM // 2
    wide = 2 * PM
    params = pltpu.CompilerParams(
        dimension_semantics=("arbitrary",), vmem_limit_bytes=48 * 1024 * 1024
    )

    def capped(p):
        return jnp.minimum(p, pairs - 1)

    anywhere = pl.BlockSpec(memory_space=pl.ANY)

    def join(after):
        each = 4
        wide_spec = pl.BlockSpec((rows, each * wide), lambda p: (0, p))
        return pl.pallas_call(
            join_body,
            grid=(pairs // each,),
            in_specs=[
                pl.BlockSpec((rows, NS), lambda p: (0, DSSM // NS + 1)),
                pl.BlockSpec((each, 8, rows), lambda p: (p, 0, 0)),
                pl.BlockSpec((each * wide, NS), lambda p: (p, 0)),
                wide_spec,
            ]
            + [anywhere] * after,
            out_specs=wide_spec,
            out_shape=jax.ShapeDtypeStruct((rows, DSSM), jnp.float32),
            compiler_params=params,
            cost_estimate=small_cost,
            name="mixer_join",
        )

    def outer(right_at, kind, after):
        each = 2
        return pl.pallas_call(
            partial(outer_body, kind),
            grid=(pairs // each,),
            in_specs=[
                pl.BlockSpec((each, 8, rows), lambda p: (p, 0, 0)),
                pl.BlockSpec((rows, each * wide), lambda p: (0, p)),
                pl.BlockSpec((rows, NS), lambda p: (0, right_at)),
            ]
            + [anywhere] * after,
            out_specs=pl.BlockSpec((each * wide, NS), lambda p: (p, 0)),
            out_shape=jax.ShapeDtypeStruct((DSSM, NS), jnp.bfloat16),
            compiler_params=params,
            cost_estimate=small_cost,
            name="state_outer",
        )

    x_spec = pl.BlockSpec((rows, wide), lambda p: (0, capped(p)))
    b_spec = pl.BlockSpec((rows, NS), lambda p: (0, DSSM // NS))
    c_spec = pl.BlockSpec((rows, NS), lambda p: (0, DSSM // NS + 1))
    row_spec = pl.BlockSpec((1, 8, rows), lambda p: (capped(p), 0, 0))
    skip_spec = pl.BlockSpec((1, 1, wide), lambda p: (capped(p), 0, 0))
    state_spec = pl.BlockSpec((wide, NS), lambda p: (capped(p), 0))
    docs_specs = [pl.BlockSpec((rows, 1), lambda p: (0, 0)), pl.BlockSpec((1, rows), lambda p: (0, 0))]
    square = pltpu.VMEM((rows, rows), jnp.float32)
    narrow = pltpu.VMEM((rows, NS), jnp.float32)
    forward = pl.pallas_call(
        mixed_body,
        grid=(pairs,),
        in_specs=[skip_spec, x_spec, b_spec, c_spec, row_spec] + docs_specs,
        out_specs=pl.BlockSpec((rows, wide), lambda p: (0, p)),
        out_shape=jax.ShapeDtypeStruct((rows, DSSM), jnp.float32),
        scratch_shapes=[square, square],
        compiler_params=params,
        cost_estimate=small_cost,
        name="mixer_forward",
    )
    backward = pl.pallas_call(
        mixed_grad_body,
        grid=(pairs + 2,),
        in_specs=[skip_spec, x_spec, b_spec, c_spec, row_spec]
        + docs_specs
        + [state_spec, state_spec, x_spec]
        + [anywhere] * anchors,
        out_specs=[
            pl.BlockSpec((rows, wide), lambda p: (0, p)),
            pl.BlockSpec((1, 1, wide), lambda p: (capped(p), 0, 0)),
        ],
        out_shape=[
            jax.ShapeDtypeStruct((rows, DSSM + 2 * NS), jnp.float32),
            jax.ShapeDtypeStruct((pairs, 1, wide), jnp.float32),
        ],
        scratch_shapes=[square, square, square, narrow, narrow],
        compiler_params=params,
        cost_estimate=small_cost,
        name="mixer_backward",
    )
    return outer, join, forward, backward


def gain_rows(gain):
    return jnp.pad(jnp.stack(split_three(gain)), ((0, 13), (0, NS - HM)))


def read_gain(rows):
    return jnp.sum(rows[..., :3, :HM].astype(jnp.float32), axis=-2)


def pass_state(part, gain, gains, reverse, after=None):
    count, position = lax.axis_size("ctx"), lax.axis_index("ctx")
    side, line_at = position % 2, position // 2
    is_first = (side == 1) if reverse else (side == 0)

    def by_head(array):
        return array.reshape(array.shape[:-2] + (HM, PM, NS)).astype(jnp.float32)

    got = exchange(part if gains else jnp.concatenate([part, gain_rows(gain)], axis=0), 1, 0)
    if gains:
        gain, other, line_gains = gains
    else:
        other = read_gain(got[DSSM:])
    own_f, got_f = by_head(part), by_head(got[:DSSM])
    first = jnp.where(is_first, own_f, got_f)
    second = jnp.where(is_first, got_f, own_f)
    first_gain = jnp.where(is_first, gain, other)[:, None, None]
    second_gain = jnp.where(is_first, other, gain)[:, None, None]
    total = (second_gain * first + second).astype(jnp.bfloat16).reshape(DSSM, NS)
    if not gains:
        total = jnp.concatenate([total, gain_rows(gain * other)], axis=0)
    if after is not None:
        total = tie(total, after)
    totals = lax.all_gather(total, "ctx", axis_index_groups=ctx_lines())
    if not gains:
        line_gains = read_gain(totals[:, DSSM:])
    totals = by_head(totals[:, :DSSM])
    factor = jnp.ones((HM,), jnp.float32)
    entering = jnp.zeros((HM, PM, NS), jnp.float32)
    lines = range(count // 2)
    for at in lines if reverse else reversed(lines):
        reached = at > line_at if reverse else at < line_at
        entering = entering + jnp.where(reached, factor, 0.0)[:, None, None] * totals[at]
        factor = factor * jnp.where(reached, line_gains[at], 1.0)
    state = jnp.where(is_first, entering, first_gain * entering + first)
    return state.astype(jnp.bfloat16).reshape(DSSM, NS), (gain, other, line_gains), total


def pack_small(norm, conv_weight, conv_bias, skip, mixer, ffn, shards):
    pieces = [
        norm.reshape(shards, -1),
        conv_weight.reshape(KW, shards, -1).transpose(1, 0, 2).reshape(shards, -1),
        conv_bias.reshape(shards, -1),
        mixer.reshape(shards, -1),
        ffn.reshape(shards, -1),
        skip.reshape(shards, -1),
    ]
    packed = jnp.concatenate(pieces, axis=1)
    packed = jnp.pad(packed, ((0, 0), (0, 4096 - packed.shape[1])))
    return packed.reshape(shards * 32, 128)


def unpack_small(packed, model, channels, heads, shards):
    packed = packed.reshape(shards, 4096)
    sizes = [model, KW * channels, channels, DSSM, model, heads]
    parts, start = [], 0
    for size in sizes:
        width = size // 4
        parts.append(packed[:, start : start + width])
        start += width
    norm, conv_weight, conv_bias, mixer, ffn, skip = parts
    conv_weight = conv_weight.reshape(shards, KW, -1).transpose(1, 0, 2).reshape(KW, -1)
    return (
        norm.reshape(-1),
        conv_weight,
        conv_bias.reshape(-1),
        skip.reshape(-1),
        mixer.reshape(-1),
        ffn.reshape(-1),
    )


def per_device(
    tokens,
    cotangent,
    doc_lengths,
    decay,
    norm_gain,
    in_proj,
    conv_weight,
    conv_bias,
    skip_gain,
    mixer_gain,
    mixer_out,
    query_proj,
    key_value_projection,
    attn_out,
    ffn_gain,
    gate_up,
    down_proj,
):
    rows, model = tokens.shape[1:]
    width = rows // 2
    shards = lax.axis_size("wshard")
    channels = conv_bias.shape[0] * shards
    count, block_at = lax.axis_size("ctx"), lax.axis_index("ctx")
    sequence_total = rows * count
    heads_per_group = QUERY_HEADS // KEY_VALUE_HEADS
    scale = HEAD_SIZE ** (-0.5)
    attend_forward, attend_backward = attention_calls(rows, count, (3, 3))
    state_outer, mixer_join, mixer_forward, mixer_backward = mixer_calls(rows, 4)

    lengths = doc_lengths[0]
    doc_count = lengths.shape[0]
    position_index = block_at * rows + jnp.arange(rows, dtype=jnp.int32)
    docs = doc_numbers(lengths, position_index)
    doc_prev = doc_numbers(lengths, position_index[:1] - 1)[0]
    log_decay = jnp.log(decay[0])
    mirrored = count - 1 - block_at
    group_blocks = jnp.stack([block_at, mirrored]).astype(jnp.int32)
    group_positions = jnp.stack(
        [
            block_at * rows + jnp.arange(width, dtype=jnp.int32),
            mirrored * rows + width + jnp.arange(width, dtype=jnp.int32),
        ]
    )
    group_docs = jnp.stack([doc_numbers(lengths, group_positions[at]) for at in range(2)])
    key_docs = doc_numbers(lengths, jnp.arange(sequence_total, dtype=jnp.int32))
    lane = jnp.arange(128)[None, :]
    key_side = ((key_docs[:, None] == lane) | ((lane >= 8) & (lane < 11))).astype(jnp.bfloat16)
    side_row = jnp.arange(16)[None, :, None]
    query_side = jnp.where(
        (side_row == group_docs[:, None, :]) | (side_row >= doc_count), 0.0, mask_fill_value
    ).astype(jnp.bfloat16)

    order = jnp.arange(rows)
    running = jnp.dot(
        log_decay, (order[:, None] <= order[None, :]).astype(jnp.float32), precision=highest
    )
    entry = jnp.where((docs == doc_prev)[None, :], jnp.exp(running), 0.0)
    tail = jnp.where((docs == docs[-1])[None, :], jnp.exp(running[:, -1:] - running), 0.0)
    carry_gain = jnp.where(docs[-1] == doc_prev, jnp.exp(running[:, -1]), 0.0)

    mixer_rows = (
        jnp.stack([running, entry, tail, jnp.zeros_like(tail)])
        .reshape(4, HM // 2, 2, rows)
        .transpose(1, 0, 2, 3)
        .reshape(HM // 2, 8, rows)
    )
    taps = jnp.stack(
        [
            (doc_numbers(lengths, position_index - (KW - 1) + tap) == docs).astype(jnp.float32)
            for tap in range(KW)
        ]
    )
    docs_column, docs_row = docs[:, None], docs[None, :]
    cosine, sine = turn_tables(position_index)
    mirrored_cosine, mirrored_sine = turn_tables(group_positions[1])
    prepared = lax.optimization_barrier(
        (
            key_side,
            query_side,
            mixer_rows,
            taps,
            docs_column,
            docs_row,
            cosine,
            sine,
            mirrored_cosine,
            mirrored_sine,
            group_blocks,
        )
    )
    (
        key_side,
        query_side,
        mixer_rows,
        taps,
        docs_column,
        docs_row,
        cosine,
        sine,
        mirrored_cosine,
        mirrored_sine,
        group_blocks,
    ) = prepared
    packed = pack_small(norm_gain, conv_weight, conv_bias, skip_gain, mixer_gain, ffn_gain, 1)
    first_shard = jnp.concatenate([in_proj, query_proj, key_value_projection], axis=1)
    packed = jnp.pad(packed.reshape(1, -1), ((0, 15), (0, first_shard.shape[1] - 4096)))
    first_w, small, arrived = gather_first(
        jnp.concatenate([first_shard, packed], axis=0), in_proj.shape[0], prepared
    )
    norm_w, conv_w, conv_b, skip_w, mixer_g, ffn_g = (
        part.astype(jnp.float32)
        for part in unpack_small(small[:, :4096], model, channels, HM, shards)
    )
    projected_width = in_proj.shape[1]
    in_w, attn_pair_w = first_w[:, :projected_width], first_w[:, projected_width:]
    out_pieces = start_shards(
        jnp.concatenate([mixer_out, attn_out, down_proj], axis=0), arrived
    )
    gate_up_pieces = start_shards(gate_up, arrived)
    source = tokens[0].astype(jnp.float32)
    normed, norm_pull = jax.vjp(rms_scale, source, norm_w)
    normed_b = normed.astype(jnp.bfloat16)
    projected = mixed_dot(normed_b, first_w)

    query_width = QUERY_HEADS * HEAD_SIZE
    attn_inputs = projected[:, projected_width:].T
    turned_q = turn(
        attn_inputs[:query_width].reshape(QUERY_HEADS, HEAD_SIZE, rows), cosine, sine
    ).astype(jnp.bfloat16)
    key_value_pair = attn_inputs[query_width:].reshape(2, KEY_VALUE_HEADS, HEAD_SIZE, rows)
    keys_b = turn(key_value_pair[0], cosine, sine).astype(jnp.bfloat16)
    values_b = key_value_pair[1].astype(jnp.bfloat16)
    pairs = lax.all_gather(
        jnp.concatenate([keys_b, values_b], axis=1).transpose(0, 2, 1), "ctx"
    )
    turned_q = turned_q * jnp.asarray(scale, jnp.bfloat16)
    mirrored_q = swap_mirrored(turned_q[:, :, width:])

    gate_z = projected[:, :DSSM]
    pre_b = projected[:, DSSM:projected_width].astype(jnp.bfloat16)
    rim = from_behind(pre_b[rows - (KW - 1) :], "ctx", 1)
    extended = jnp.concatenate([rim, pre_b], axis=0).astype(jnp.float32)
    conv_f, conv_pull = jax.vjp(partial(conv_local, taps), extended, conv_w, conv_b)
    conv_b16 = conv_f.astype(jnp.bfloat16)
    skip_wide = jnp.repeat(skip_w, PM).reshape(HM // 2, 1, 2 * PM)
    fresh = state_outer(DSSM // NS, 4, 0)(mixer_rows, conv_b16, conv_b16)
    state_in, gains, _ = pass_state(fresh, carry_gain, None, False, pairs)
    local = mixer_forward(
        skip_wide, conv_b16, conv_b16, conv_b16, mixer_rows, docs_column, docs_row
    )

    heads_own, heads_mirrored, log_x = attend_forward(
        group_blocks,
        pairs,
        key_side,
        turned_q,
        mirrored_q,
        query_side,
        out_pieces[1],
        gate_up_pieces[1],
        local,
    )
    mixer_w, attn_w, down_w = finish_shards(
        out_pieces,
        [mixer_out.shape[0], attn_out.shape[0], down_proj.shape[0]],
        log_x,
    )
    (gate_up_w,) = finish_shards(gate_up_pieces, [gate_up.shape[0]], log_x)
    heads_back = swap_mirrored(heads_mirrored.astype(jnp.bfloat16))
    heads_t = jnp.concatenate([heads_own.astype(jnp.bfloat16), heads_back], axis=2).reshape(
        QUERY_HEADS * HEAD_SIZE, rows
    )
    mixed = mixer_join(0)(conv_b16, mixer_rows, state_in, local)
    gated, gate_pull = jax.vjp(gate_norm, mixed, gate_z, mixer_g)
    gated_b = gated.astype(jnp.bfloat16)
    mamba = mixed_dot(gated_b, mixer_w)
    attn = lax.dot_general(
        heads_t, attn_w, (((0,), (0,)), ((), ())), preferred_element_type=jnp.float32
    )
    middle = source + attn + mamba
    normed2, ffn_pull = jax.vjp(rms_scale, middle, ffn_g)
    normed2_b = normed2.astype(jnp.bfloat16)
    gate_up_v = mixed_dot(normed2_b, gate_up_w)
    activated, act_pull = jax.vjp(swiglu, gate_up_v)
    activated_b = activated.astype(jnp.bfloat16)
    layer_out = (middle + mixed_dot(activated_b, down_w)).astype(jnp.bfloat16)

    out_low = cotangent[0]
    down_sum, down_beside, down_across, _ = weight_grad(activated_b, out_low)
    (gate_up_grad_v,) = act_pull(nt_dot(out_low, down_w))
    gate_up_low = gate_up_grad_v.astype(jnp.bfloat16)
    gate_up_sum, gate_up_beside, _, gate_up_sent = weight_grad(normed2_b, gate_up_low)
    gate_up_half, _, gate_up_give = ctx_half([gate_up_sum], model // shards)
    middle_norm_grad, ffn_gain_grad = ffn_pull(nt_dot(gate_up_low, gate_up_w))
    middle_grad = out_low.astype(jnp.float32) + middle_norm_grad
    middle_low = middle_grad.astype(jnp.bfloat16)
    heads_low = nt_dot(attn_w, middle_low).astype(jnp.bfloat16)
    heads_low = heads_low.reshape(QUERY_HEADS, HEAD_SIZE, rows)
    mirrored_low = swap_mirrored(heads_low[:, :, width:])
    gated_grad = nt_dot(middle_low, mixer_w)
    mixed_grad, gate_z_grad, mixer_gain_grad = gate_pull(gated_grad)
    upward = state_outer(DSSM // NS + 1, 2, 2)(
        mixer_rows, mixed_grad.astype(jnp.bfloat16), conv_b16, down_beside, gate_up_sent
    )
    state_out_grad, _, pair_total = pass_state(upward, None, gains, True)
    down_half, _, _ = ctx_half([tie(down_sum, upward)], model // shards)
    gate_z_low = gate_z_grad.astype(jnp.bfloat16)
    query_grad_own, query_grad_mirrored, pairs_grad = attend_backward(
        group_blocks,
        pairs,
        key_side,
        turned_q,
        mirrored_q,
        query_side,
        log_x,
        heads_own,
        heads_mirrored,
        heads_low,
        mirrored_low,
        gate_up_beside,
        down_across,
        pair_total,
    )
    mixer_products = split_products(gated_b, middle_low)
    attn_products = split_products(heads_t, middle_low, 0)
    shard_sizes = [mixer_out.shape[0], attn_out.shape[0]]

    def interleaved(parts):
        return jnp.concatenate(
            [
                part[start * size : (start + 1) * size]
                for start in range(parts[0].shape[0] // shard_sizes[0])
                for part, size in zip(parts, shard_sizes)
            ],
            axis=0,
        ).astype(jnp.bfloat16)

    mixer_attn_started = start_sum(
        *[interleaved(parts) for parts in zip(mixer_products, attn_products)], pairs_grad
    )
    in_z_started = start_sum(*split_products(normed_b, gate_z_low), pairs_grad)
    query_low_own, query_low_mirrored = (
        (turn(grad, *tables) * scale).astype(jnp.bfloat16)
        for grad, tables in (
            (query_grad_own, (cosine[:, :width], -sine[:, :width])),
            (query_grad_mirrored, (mirrored_cosine, -mirrored_sine)),
        )
    )
    query_low = jnp.concatenate(
        [query_low_own, swap_mirrored(query_low_mirrored)], axis=2
    ).reshape(QUERY_HEADS * HEAD_SIZE, rows)

    conv_grad, skip_parts = mixer_backward(
        skip_wide,
        conv_b16,
        conv_b16,
        conv_b16,
        mixer_rows,
        docs_column,
        docs_row,
        state_in,
        state_out_grad,
        mixed_grad,
        gate_up_give,
        in_z_started[1],
        down_half,
        mixer_attn_started[1],
    )
    ffn_half = jnp.concatenate([gate_up_half, down_half], axis=1)
    conv_grad = tie(conv_grad, ffn_half)
    ffn_summed = line_sum(ffn_half, 0)
    pair_grad = scatter_blocks(pairs_grad, conv_grad).astype(jnp.float32).transpose(0, 2, 1)
    skip_grad = jnp.sum(skip_parts.reshape(HM, PM), axis=1)
    extended_grad, conv_weight_grad, conv_bias_grad = conv_pull(conv_grad)
    from_above = from_behind(extended_grad[: KW - 1], "ctx", -1)
    pre_grad = extended_grad[KW - 1 :] + jnp.pad(from_above, ((rows - (KW - 1), 0), (0, 0)))
    pre_low = pre_grad.astype(jnp.bfloat16)
    mixer_attn_sum = finish_sum(mixer_attn_started, pre_low)
    in_sum_z = finish_sum(in_z_started, pre_low)
    mixer_half, _, _ = ctx_half([mixer_attn_sum, in_sum_z], model // shards)
    in_sum_pre, _, _, in_pre_sent = weight_grad(normed_b, pre_low)
    projected_low = jnp.concatenate([gate_z_low, pre_low], axis=1)
    normed_grad = nt_dot(projected_low, in_w)

    keys_low = turn(pair_grad[:, :HEAD_SIZE], cosine, -sine)
    keyval_low = jnp.concatenate(
        [
            keys_low.reshape(KEY_VALUE_HEADS * HEAD_SIZE, rows),
            pair_grad[:, HEAD_SIZE:].reshape(KEY_VALUE_HEADS * HEAD_SIZE, rows),
        ],
        axis=0,
    ).astype(jnp.bfloat16)
    attn_pair_low = tie(jnp.concatenate([query_low, keyval_low], axis=0).T, in_pre_sent, ffn_summed)
    attn_pair_sum = finish_sum(
        start_sum(*split_products(normed_b, attn_pair_low), mixer_half), None
    )
    normed_grad = normed_grad + nt_dot(attn_pair_low, attn_pair_w)
    source_grad, norm_grad = norm_pull(normed_grad)
    tokens_grad = (middle_grad + source_grad)[None]

    small_grad = pack_small(
        norm_grad, conv_weight_grad, conv_bias_grad, skip_grad, mixer_gain_grad, ffn_gain_grad, shards
    )
    small_share = sum_small(small_grad)
    last_half, _, _ = ctx_half([in_sum_pre, attn_pair_sum], model // shards)
    mixer_summed = line_sum(tie(mixer_half, ffn_summed), 2)
    gate_up_share, down_share = ctx_finish(
        tie(ffn_summed, last_half), [gate_up_sum.shape, down_sum.shape]
    )
    mixer_attn_share, in_share_z = ctx_finish(
        mixer_summed, [mixer_attn_sum.shape, in_sum_z.shape]
    )
    mixer_share = mixer_attn_share[: mixer_out.shape[0]]
    attn_share = mixer_attn_share[mixer_out.shape[0] :]
    in_share_pre, attn_pair_share = ctx_finish(
        line_sum(tie(last_half, mixer_summed), 3), [in_sum_pre.shape, attn_pair_sum.shape]
    )
    norm_share, conv_w_share, conv_b_share, skip_share, mixer_g_share, ffn_share = unpack_small(
        small_share, model, channels, HM, 1
    )
    return (
        layer_out[None],
        tokens_grad,
        norm_share,
        jnp.concatenate([in_share_z, in_share_pre], axis=1),
        conv_w_share,
        conv_b_share,
        skip_share,
        mixer_g_share,
        mixer_share,
        attn_pair_share[:, : QUERY_HEADS * HEAD_SIZE],
        attn_pair_share[:, QUERY_HEADS * HEAD_SIZE :],
        attn_share,
        ffn_share,
        gate_up_share,
        down_share,
    )


def solution(mesh):
    in_specs = (
        P("wshard", "ctx", None),
        P("wshard", "ctx", None),
        P("wshard", None),
        P("wshard", None, "ctx"),
        P("wshard"),
        P("wshard", None),
        P(None, "wshard"),
        P("wshard"),
        P("wshard"),
        P("wshard"),
        P("wshard", None),
        P("wshard", None),
        P("wshard", None),
        P("wshard", None),
        P("wshard"),
        P("wshard", None),
        P("wshard", None),
    )
    out_specs = (
        P("wshard", "ctx", None),
        P("wshard", "ctx", None),
        P("wshard"),
        P("wshard", None),
        P(None, "wshard"),
        P("wshard"),
        P("wshard"),
        P("wshard"),
        P("wshard", None),
        P("wshard", None),
        P("wshard", None),
        P("wshard", None),
        P("wshard"),
        P("wshard", None),
        P("wshard", None),
    )
    return jax.shard_map(
        per_device, mesh=mesh, in_specs=in_specs, out_specs=out_specs, check_vma=False
    )
```

```python
from functools import partial

import jax
import jax.numpy as jnp
from jax import lax
from jax.experimental import pallas as pl
from jax.experimental.pallas import tpu as pltpu
from jax.sharding import PartitionSpec as P

FF = 2048
QUERY_HEADS = 8
KEY_VALUE_HEADS = 2
HEAD_SIZE = 64
HM = 24
PM = 64
NS = 128
KW = 4
DSSM = 1536

eps_norm = 1e-05
rope_base = 100000000000.0
mask_fill_value = -1e30
highest = lax.Precision.HIGHEST
MESH_AXES = ("ctx", "wshard")
small_cost = pl.CostEstimate(flops=1024, bytes_accessed=1024, transcendentals=0)


def exchange(block, ctx_flip, shard_flip):
    blocks, shards = lax.axis_size("ctx"), lax.axis_size("wshard")
    route = [
        (c * shards + w, (c ^ ctx_flip) * shards + (w ^ shard_flip))
        for c in range(blocks)
        for w in range(shards)
    ]
    return lax.ppermute(block, MESH_AXES, route)


def from_behind(block, axis, distance):
    devices = range(lax.axis_size(axis))
    route = [(i - distance, i) for i in devices if i - distance in devices]
    return lax.ppermute(block, axis, route)


def swap_mirrored(block):
    count = lax.axis_size("ctx")
    return lax.ppermute(block, "ctx", [(i, count - 1 - i) for i in range(count)])


def tie_body(*refs):
    pass


def tie(value, *after):
    anywhere = pl.BlockSpec(memory_space=pl.ANY)
    return pl.pallas_call(
        tie_body,
        in_specs=[anywhere] * (1 + len(after)),
        out_specs=anywhere,
        out_shape=jax.ShapeDtypeStruct(value.shape, value.dtype),
        input_output_aliases={0: 0},
        cost_estimate=pl.CostEstimate(flops=0, bytes_accessed=0, transcendentals=0),
        name="tie",
    )(value, *after)


def assemble_body(spans, target_ref, *refs):
    out_ref = refs[-1]
    step = pl.program_id(0)
    for piece, (first, size) in zip(refs, spans):

        def put(piece=piece):
            out_ref[...] = piece[...]

        pl.when((step >= first) & (step < first + size))(put)


def assemble(pieces, rows, anchors=()):
    spans, offsets, targets = [], [], []
    for _, source, start, size in pieces:
        spans.append((len(targets), size // rows))
        offsets.append(source // rows)
        targets += [start // rows + at for at in range(size // rows)]
    columns, kind = pieces[0][0].shape[1], pieces[0][0].dtype

    def source_map(offset, first, size):
        return lambda i, target: (offset + jnp.clip(i - first, 0, size - 1), 0)

    return pl.pallas_call(
        partial(assemble_body, spans),
        grid_spec=pltpu.PrefetchScalarGridSpec(
            num_scalar_prefetch=1,
            grid=(len(targets),),
            in_specs=[
                pl.BlockSpec((rows, columns), source_map(offset, first, size))
                for offset, (first, size) in zip(offsets, spans)
            ]
            + [pl.BlockSpec(memory_space=pl.ANY)] * len(anchors),
            out_specs=pl.BlockSpec((rows, columns), lambda i, target: (target[i], 0)),
        ),
        out_shape=jax.ShapeDtypeStruct((rows * len(targets), columns), kind),
        compiler_params=pltpu.CompilerParams(
            dimension_semantics=("arbitrary",), vmem_limit_bytes=32 * 1024 * 1024
        ),
        cost_estimate=small_cost,
        name="assemble",
    )(jnp.stack([jnp.asarray(target, jnp.int32) for target in targets]), *[p[0] for p in pieces], *anchors)


def gather_first(shard, rows, anchors):
    part = rows // 4
    w = lax.axis_index("wshard")
    side = lax.axis_index("ctx") % 2
    direct = shard[2 * part :]
    across = exchange(lax.dynamic_slice_in_dim(shard, side * part, part, 0), 0, 2)
    across_direct = exchange(direct, 0, 2)
    beside = exchange(shard, 0, 1)
    across_relayed = exchange(across, 1, 0)
    far, far_direct, far_relayed = (
        exchange(piece, 0, 1) for piece in (across, across_direct, across_relayed)
    )
    pieces = [(shard, 0, w * rows, rows), (beside, 0, (w ^ 1) * rows, rows)]
    for flip, early, late, rest in (
        (2, across, across_relayed, across_direct),
        (3, far, far_relayed, far_direct),
    ):
        start = (w ^ flip) * rows
        pieces.append((early, 0, start + side * part, part))
        pieces.append((late, 0, start + (1 - side) * part, part))
        pieces.append((rest, 0, start + 2 * part, 2 * part))
    tails = [shard[rows:], beside[rows:], across_direct[2 * part :], far_direct[2 * part :]]
    tails = jnp.concatenate([tail[:1] for tail in tails], axis=0)
    small = jnp.concatenate(
        [lax.dynamic_slice_in_dim(tails, w ^ at, 1, 0) for at in range(4)], axis=0
    )
    return assemble(pieces, part, anchors), small, across_direct


def start_shards(stacked, after):
    stacked, _ = lax.optimization_barrier((stacked, after))
    return stacked, exchange(stacked, 0, 1), exchange(stacked, 0, 2)


def finish_shards(pieces, sizes, after):
    own, beside, across = pieces
    far = exchange(lax.optimization_barrier((across, after))[0], 0, 1)
    w = lax.axis_index("wshard")
    wholes, source = [], 0
    for size in sizes:
        wholes.append(
            assemble(
                [
                    (part, source, (w ^ flip) * size, size)
                    for flip, part in enumerate((own, beside, across, far))
                ],
                size,
            )
        )
        source += size
    return wholes


def add_low(first, *others):
    total = first.astype(jnp.float32)
    for other in others:
        total = total + other.astype(jnp.float32)
    return total.astype(jnp.bfloat16)


def lay_side_by_side(blocks, rows):
    parts = []
    for block in blocks:
        for start in range(0, block.shape[0], rows):
            part = block[start : start + rows]
            parts.append(jnp.pad(part, ((0, rows - part.shape[0]), (0, 0))))
    return jnp.concatenate(parts, axis=1)


def take_apart(array, shapes):
    rows, start, blocks = array.shape[0], 0, []
    for height, columns in shapes:
        parts = []
        for _ in range(0, height, rows):
            parts.append(array[: min(height, rows), start : start + columns])
            start += columns
        blocks.append(parts[0] if len(parts) == 1 else jnp.concatenate(parts, axis=0))
    return blocks


def ctx_half(blocks, rows):
    side = lax.axis_index("ctx") % 2
    whole = lay_side_by_side(blocks, rows)
    half = rows // 2
    give = lax.dynamic_slice_in_dim(whole, (1 - side) * half, half, 0)
    got = exchange(give, 1, 0)
    return add_low(lax.dynamic_slice_in_dim(whole, side * half, half, 0), got), got, give


def ctx_lines():
    count = lax.axis_size("ctx")
    return [list(range(start, count, 2)) for start in range(2)]


def ctx_finish(mine, shapes, turn_at):
    side = lax.axis_index("ctx") % 2
    lines = ctx_lines()
    if turn_at % 2:
        lines = lines[::-1]
    if turn_at // 2:
        lines = [line[::-1] for line in lines]
    mine = lax.psum(mine, "ctx", axis_index_groups=lines)
    summed = mine
    got = exchange(mine, 1, 0)
    whole = jnp.where(
        side == 0, jnp.concatenate([mine, got], axis=0), jnp.concatenate([got, mine], axis=0)
    ).astype(jnp.float32)
    return take_apart(whole, shapes), summed


def shard_pieces(array, axis):
    w = lax.axis_index("wshard")
    size = array.shape[axis] // 4

    def piece(flip):
        return lax.dynamic_slice_in_dim(array, (w ^ flip) * size, size, axis)

    return jnp.concatenate([piece(1), piece(3)], axis=axis), piece(2), piece(0)


def shard_sum(beside, across, own):
    rows = own.shape[0]
    got = exchange(beside.astype(jnp.bfloat16), 0, 1)
    sent = add_low(across, got[rows:])
    got_across = exchange(sent, 0, 2)
    return add_low(own, got[:rows], got_across), got, got_across, sent


def split_products(left, right, axis=1):
    return [
        lax.dot_general(
            piece, right, (((1 - axis,), (0,)), ((), ())), preferred_element_type=jnp.float32
        )
        for piece in shard_pieces(left, axis)
    ]


def weight_grad(left, right):
    return shard_sum(*split_products(left, right))


def start_sum(beside, across, own, after):
    rows = own.shape[0]
    got = exchange(beside.astype(jnp.bfloat16), 0, 1)
    got_across = exchange(tie(add_low(across, got[rows:]), after), 0, 2)
    return own, got, got_across


def finish_sum(started, after):
    own, got, got_across = started
    return add_low(own, got[: own.shape[0]], tie(got_across, after))


def sum_small(value):
    rows = value.shape[0] // 4
    for flip in (1, 2):
        value = value + exchange(value, 0, flip)
    value = lax.dynamic_slice_in_dim(value, lax.axis_index("wshard") * rows, rows, 0)
    bit = 1
    while bit < lax.axis_size("ctx"):
        value = value + exchange(value, bit, 0)
        bit *= 2
    return value


def scatter_blocks(blocks, after):
    position, bit = lax.axis_index("ctx"), 1
    while blocks.shape[0] > 1:
        up = (position // bit) % 2
        halves = blocks.reshape((blocks.shape[0] // 2, 2) + blocks.shape[1:])
        keep = lax.dynamic_index_in_dim(halves, up, 1, keepdims=False)
        give = lax.dynamic_index_in_dim(halves, 1 - up, 1, keepdims=False)
        got = exchange(give, bit, 0)
        if bit == 1:
            got = tie(got, after)
        blocks = add_low(keep, got)
        bit *= 2
    return blocks[0]


def mixed_dot(left, right):
    return jnp.dot(left, right, preferred_element_type=jnp.float32)


def rms_scale(value, gain):
    return value * lax.rsqrt(jnp.mean(value * value, axis=-1, keepdims=True) + eps_norm) * gain


def doc_numbers(lengths, position_index):
    ends = jnp.cumsum(lengths)[:-1]
    tally_count = jnp.sum((position_index[:, None] >= ends[None, :]).astype(jnp.int32), axis=1)
    return jnp.where(position_index >= 0, tally_count, -1)


def turn_tables(position_index):
    half = HEAD_SIZE // 2
    freq = rope_base ** (-jnp.arange(half, dtype=jnp.float32) / half)
    angle = freq[:, None] * position_index.astype(jnp.float32)[None, :]
    return jnp.cos(angle), jnp.sin(angle)


def turn(value, cosine, sine):
    half = value.shape[-2] // 2
    first = value[..., :half, :]
    second = value[..., half:, :]
    return jnp.concatenate(
        [first * cosine - second * sine, second * cosine + first * sine], axis=-2
    )


def conv_local(taps, extended, weight, bias):
    tally_count = extended.shape[0] - (KW - 1)
    total = bias[None, :]
    for tap in range(KW):
        total = (
            total + weight[tap][None, :] * extended[tap : tap + tally_count] * taps[tap][:, None]
        )
    return jax.nn.silu(total)


def gate_norm(mixed, gate_z, gain):
    return rms_scale(mixed * jax.nn.silu(gate_z), gain)


def swiglu(gate_up_v):
    return jax.nn.silu(gate_up_v[:, :FF]) * gate_up_v[:, FF:]


def split_three(value):
    high = value.astype(jnp.bfloat16)
    rest = value - high.astype(jnp.float32)
    middle = rest.astype(jnp.bfloat16)
    low = (rest - middle.astype(jnp.float32)).astype(jnp.bfloat16)
    return [high, middle, low]


def nt_dot(left, right):
    return lax.dot_general(left, right, (((1,), (1,)), ((), ())), preferred_element_type=jnp.float32)


def causal_tile(scores, group, width):
    rows = lax.broadcasted_iota(jnp.int32, scores.shape, 0)
    columns = lax.broadcasted_iota(jnp.int32, scores.shape, 1)
    return jnp.where(rows <= lax.rem(columns, width) + group * width, scores, mask_fill_value)


def load_extended(extended, group, lower, value_ref, side, extra):
    width = value_ref.shape[2]
    extended[group] = jnp.zeros(extended.shape[1:], extended.dtype)
    for head in range(value_ref.shape[0]):
        here = slice(head * width, (head + 1) * width)
        extended[group, lower : lower + HEAD_SIZE, here] = value_ref[head]
    side = jnp.concatenate([side.astype(jnp.float32)] * value_ref.shape[0], axis=1)
    if extra is not None:
        row = lax.broadcasted_iota(jnp.int32, side.shape, 0)
        for at, part in enumerate(split_three(-extra)):
            side = jnp.where(row == 8 + at, part.astype(jnp.float32), side)
    extended[group, 128:144, :] = side.astype(extended.dtype)


def attend_forward_body(width, blocks, pair_ref, side_ref, query_a, query_b, query_side_ref, *refs):
    heads_refs, (log_ref, query_x, peak, total) = refs[-6:-4], refs[-4:]
    step = pl.program_id(1)

    @pl.when(step == 0)
    def start():
        for group, query_ref in enumerate((query_a, query_b)):
            load_extended(query_x, group, 0, query_ref, query_side_ref[group], None)
        peak[...] = jnp.full(peak.shape, mask_fill_value, jnp.float32)
        total[...] = jnp.zeros(total.shape, jnp.float32)

    @pl.when(step <= jnp.maximum(blocks[0], blocks[1]))
    def work():
        keys = jnp.concatenate([pair_ref[0, 0], side_ref[...]], axis=1)
        values = keys.T[HEAD_SIZE:144]

        def tile(group, masked):
            scores = mixed_dot(keys, query_x[group])
            if masked:
                scores = causal_tile(scores, group, width)
            old = peak[group]
            new = jnp.maximum(old, jnp.max(scores, axis=0, keepdims=True))
            probs = jnp.exp(scores - new)
            total[group] = total[group] * jnp.exp(old - new) + mixed_dot(
                values, probs.astype(jnp.bfloat16)
            )
            peak[group] = new

        for group in range(2):
            pl.when(step < blocks[group])(partial(tile, group, False))
            pl.when(step == blocks[group])(partial(tile, group, True))

    @pl.when(step == pl.num_programs(1) - 1)
    def finish():
        for group in range(2):
            weight = total[group, HEAD_SIZE + 8 : HEAD_SIZE + 9, :]
            heads = total[group, :HEAD_SIZE, :] / weight
            for head in range(heads.shape[1] // width):
                heads_refs[group][head] = heads[:, head * width : (head + 1) * width]
            log_ref[group, 0] = peak[group] + jnp.log(weight)


def attend_backward_body(
    width,
    blocks,
    pair_ref,
    side_ref,
    query_a,
    query_b,
    query_side_ref,
    log_ref,
    heads_a,
    heads_b,
    grad_a,
    grad_b,
    *refs,
):
    query_grad_refs, (pair_grad_ref, query_x, grad_x, pair_acc, query_acc) = refs[-7:-5], refs[-5:]
    step = pl.program_id(1)

    @pl.when(step == 0)
    def start():
        groups = ((query_a, heads_a, grad_a), (query_b, heads_b, grad_b))
        for group, (query_ref, heads_ref, grad_ref) in enumerate(groups):
            load_extended(query_x, group, 0, query_ref, query_side_ref[group], log_ref[group, 0])
            delta = [
                jnp.sum(heads_ref[head] * grad_ref[head].astype(jnp.float32), axis=0, keepdims=True)
                for head in range(heads_ref.shape[0])
            ]
            blank = jnp.zeros(query_side_ref.shape[1:], jnp.float32)
            load_extended(
                grad_x, group, HEAD_SIZE, grad_ref, blank, jnp.concatenate(delta, axis=1)
            )
        query_acc[...] = jnp.zeros(query_acc.shape, jnp.float32)

    pair_acc[...] = jnp.zeros(pair_acc.shape, jnp.float32)

    @pl.when(step <= jnp.maximum(blocks[0], blocks[1]))
    def work():
        pair = pair_ref[0, 0]
        keys = jnp.concatenate([pair, side_ref[...]], axis=1)
        turned = pair.T[:HEAD_SIZE]

        def tile(group, masked):
            scores = mixed_dot(keys, query_x[group])
            if masked:
                scores = causal_tile(scores, group, width)
            probs = jnp.exp(scores)
            low = (probs * mixed_dot(keys, grad_x[group])).astype(jnp.bfloat16)
            pair_acc[...] += nt_dot(low, query_x[group, :128, :]) + nt_dot(
                probs.astype(jnp.bfloat16), grad_x[group, :128, :]
            )
            query_acc[group] += mixed_dot(turned, low)

        for group in range(2):
            pl.when(step < blocks[group])(partial(tile, group, False))
            pl.when(step == blocks[group])(partial(tile, group, True))

    pair_grad_ref[0, 0] = pair_acc[...].astype(jnp.bfloat16)

    @pl.when(step == pl.num_programs(1) - 1)
    def finish():
        for group in range(2):
            for head in range(query_acc.shape[2] // width):
                query_grad_refs[group][head] = query_acc[group, :, head * width : (head + 1) * width]


def attention_calls(rows, count, anchors):
    width = rows // 2
    span = width * (QUERY_HEADS // KEY_VALUE_HEADS)

    def last(blocks):
        return jnp.maximum(blocks[0], blocks[1])

    pair_spec = pl.BlockSpec(
        (1, 1, rows, 128), lambda g, k, blocks: (jnp.minimum(k, last(blocks)), g, 0, 0)
    )
    side_spec = pl.BlockSpec((rows, 128), lambda g, k, blocks: (jnp.minimum(k, last(blocks)), 0))

    heads_per_group = QUERY_HEADS // KEY_VALUE_HEADS
    own = pl.BlockSpec((heads_per_group, HEAD_SIZE, width), lambda g, k, blocks: (g, 0, 0))
    half_spec = own
    log_spec = pl.BlockSpec((2, 1, 1, span), lambda g, k, blocks: (0, g, 0, 0))
    query_side_spec = pl.BlockSpec((2, 16, width), lambda g, k, blocks: (0, 0, 0))
    half_shape = jax.ShapeDtypeStruct((QUERY_HEADS, HEAD_SIZE, width), jnp.float32)

    anywhere = pl.BlockSpec(memory_space=pl.ANY)
    params = pltpu.CompilerParams(
        dimension_semantics=("arbitrary", "arbitrary"), vmem_limit_bytes=48 * 1024 * 1024
    )
    forward = pl.pallas_call(
        partial(attend_forward_body, width),
        grid_spec=pltpu.PrefetchScalarGridSpec(
            num_scalar_prefetch=1,
            grid=(KEY_VALUE_HEADS, count),
            in_specs=[pair_spec, side_spec, own, half_spec, query_side_spec]
            + [anywhere] * anchors[0],
            out_specs=[half_spec, half_spec, log_spec],
            scratch_shapes=[
                pltpu.VMEM((2, 256, span), jnp.bfloat16),
                pltpu.VMEM((2, 1, span), jnp.float32),
                pltpu.VMEM((2, 144 - HEAD_SIZE, span), jnp.float32),
            ],
        ),
        out_shape=[
            half_shape,
            half_shape,
            jax.ShapeDtypeStruct((2, KEY_VALUE_HEADS, 1, span), jnp.float32),
        ],
        compiler_params=params,
        cost_estimate=small_cost,
        name="attend_forward",
    )
    backward = pl.pallas_call(
        partial(attend_backward_body, width),
        grid_spec=pltpu.PrefetchScalarGridSpec(
            num_scalar_prefetch=1,
            grid=(KEY_VALUE_HEADS, count),
            in_specs=[
                pair_spec,
                side_spec,
                own,
                half_spec,
                query_side_spec,
                log_spec,
                half_spec,
                half_spec,
                own,
                half_spec,
            ]
            + [anywhere] * anchors[1],
            out_specs=[
                half_spec,
                half_spec,
                pl.BlockSpec((1, 1, rows, 128), lambda g, k, blocks: (k, g, 0, 0)),
            ],
            scratch_shapes=[
                pltpu.VMEM((2, 256, span), jnp.bfloat16),
                pltpu.VMEM((2, 256, span), jnp.bfloat16),
                pltpu.VMEM((rows, 128), jnp.float32),
                pltpu.VMEM((2, HEAD_SIZE, span), jnp.float32),
            ],
        ),
        out_shape=[
            half_shape,
            half_shape,
            jax.ShapeDtypeStruct((count, KEY_VALUE_HEADS, rows, 128), jnp.bfloat16),
        ],
        compiler_params=params,
        cost_estimate=small_cost,
        name="attend_backward",
    )
    return forward, backward


def pick(pair):
    lane = lax.broadcasted_iota(jnp.int32, (pair.shape[0], 2 * PM), 1)
    return jnp.where(lane < PM, pair[:, 0:1], pair[:, 1:2])


def outer_body(kind, rows_ref, left_ref, right_ref, *refs):
    out_ref = refs[-1]
    for at in range(rows_ref.shape[0]):
        scale = pick(rows_ref[at].T[:, kind : kind + 2])
        left = left_ref[:, at * 128 : (at + 1) * 128].astype(jnp.float32) * scale
        out_ref[at * 128 : (at + 1) * 128, :] = lax.dot_general(
            left.astype(jnp.bfloat16),
            right_ref[...],
            (((0,), (0,)), ((), ())),
            preferred_element_type=jnp.float32,
        ).astype(out_ref.dtype)


def join_body(c_ref, rows_ref, state_ref, local_ref, *refs):
    out_ref = refs[-1]
    for at in range(rows_ref.shape[0]):
        here = slice(at * 2 * PM, (at + 1) * 2 * PM)
        inner = nt_dot(c_ref[...], state_ref[here, :])
        out_ref[:, here] = local_ref[:, here] + inner * pick(rows_ref[at].T[:, 2:4])


def mixed_body(
    skip_ref, x_ref, b_ref, c_ref, row_ref, docs_column, docs_row, out_ref, fill, products
):
    rows = x_ref.shape[0]
    half = rows // 2

    @pl.when(pl.program_id(0) == 0)
    def start():
        at = lax.broadcasted_iota(jnp.int32, (rows, rows), 0)
        source = lax.broadcasted_iota(jnp.int32, (rows, rows), 1)
        same = (at >= source) & (docs_column[...] == docs_row[...])
        fill[...] = jnp.where(same, 0.0, mask_fill_value)
        products[...] = nt_dot(c_ref[...], b_ref[...])

    x = x_ref[...]
    columns = row_ref[0].T
    lane = lax.broadcasted_iota(jnp.int32, (half, 2 * PM), 1)
    for block in range(2):
        here = slice(block * half, (block + 1) * half)
        width = (block + 1) * half
        parts = []
        for head in range(2):
            decay = jnp.exp(
                (columns[here, head : head + 1] - row_ref[0, head : head + 1, :width])
                + fill[here, :width]
            )
            weights = (products[here, :width] * decay).astype(jnp.bfloat16)
            parts.append(mixed_dot(weights, x[:width]))
        local = jnp.where(lane < PM, parts[0], parts[1])
        out_ref[here, :] = local + x[here].astype(jnp.float32) * skip_ref[0]


def mixed_grad_body(
    skip_ref,
    x_ref,
    b_ref,
    c_ref,
    row_ref,
    docs_column,
    docs_row,
    state_ref,
    state_grad_ref,
    grad_ref,
    *refs,
):
    out_ref, skip_grad_ref, fill, products, scores, b_grad, c_grad = refs[-7:]
    rows = x_ref.shape[0]
    half = rows // 2
    step = pl.program_id(0)
    pairs = HM // 2

    @pl.when(step == 0)
    def start():
        source = lax.broadcasted_iota(jnp.int32, (rows, rows), 0)
        at = lax.broadcasted_iota(jnp.int32, (rows, rows), 1)
        same = (at >= source) & (docs_column[...] == docs_row[...])
        fill[...] = jnp.where(same, 0.0, mask_fill_value)
        products[...] = nt_dot(b_ref[...], c_ref[...])
        scores[...] = jnp.zeros(scores.shape, jnp.float32)
        b_grad[...] = jnp.zeros(b_grad.shape, jnp.float32)
        c_grad[...] = jnp.zeros(c_grad.shape, jnp.float32)

    @pl.when(step < pairs)
    def work():
        x = x_ref[...]
        x_f = x.astype(jnp.float32)
        grad = grad_ref[...]
        low = grad.astype(jnp.bfloat16)
        lane = lax.broadcasted_iota(jnp.int32, (half, 2 * PM), 1)
        lane_all = lax.broadcasted_iota(jnp.int32, (rows, 2 * PM), 1)
        skip_grad_ref[0] = jnp.sum(grad * x_f, axis=0, keepdims=True)
        state_grad = state_grad_ref[...]
        columns = row_ref[0].T
        tail = pick(columns[:, 4:6])
        b_grad[...] += mixed_dot((x_f * tail).astype(jnp.bfloat16), state_grad)
        entered = (low.astype(jnp.float32) * pick(columns[:, 2:4])).astype(jnp.bfloat16)
        c_grad[...] += mixed_dot(entered, state_ref[...])
        passed = nt_dot(b_ref[...], state_grad) * tail + grad * skip_ref[0]
        chosen = [
            jnp.where((lane_all < PM) == (head == 0), x_f, 0.0).astype(jnp.bfloat16)
            for head in range(2)
        ]
        for block in range(2):
            here = slice(block * half, (block + 1) * half)
            start_at = block * half
            parts = []
            for head in range(2):
                decay = jnp.exp(
                    (row_ref[0, head : head + 1, start_at:] - columns[here, head : head + 1])
                    + fill[here, start_at:]
                )
                weights = (products[here, start_at:] * decay).astype(jnp.bfloat16)
                parts.append(mixed_dot(weights, low[start_at:]))
                scores[here, start_at:] += nt_dot(chosen[head][here], low[start_at:]) * decay
            out_ref[here, :] = jnp.where(lane < PM, parts[0], parts[1]) + passed[here]

    @pl.when(step == pairs)
    def give_b():
        out_ref[...] = b_grad[...] + mixed_dot(scores[...].astype(jnp.bfloat16), c_ref[...])

    @pl.when(step == pairs + 1)
    def give_c():
        out_ref[...] = c_grad[...] + lax.dot_general(
            scores[...].astype(jnp.bfloat16),
            b_ref[...],
            (((0,), (0,)), ((), ())),
            preferred_element_type=jnp.float32,
        )


def mixer_calls(rows, anchors):
    pairs = HM // 2
    wide = 2 * PM
    params = pltpu.CompilerParams(
        dimension_semantics=("arbitrary",), vmem_limit_bytes=48 * 1024 * 1024
    )

    def capped(p):
        return jnp.minimum(p, pairs - 1)

    anywhere = pl.BlockSpec(memory_space=pl.ANY)

    def join(after):
        each = 4
        wide_spec = pl.BlockSpec((rows, each * wide), lambda p: (0, p))
        return pl.pallas_call(
            join_body,
            grid=(pairs // each,),
            in_specs=[
                pl.BlockSpec((rows, NS), lambda p: (0, DSSM // NS + 1)),
                pl.BlockSpec((each, 8, rows), lambda p: (p, 0, 0)),
                pl.BlockSpec((each * wide, NS), lambda p: (p, 0)),
                wide_spec,
            ]
            + [anywhere] * after,
            out_specs=wide_spec,
            out_shape=jax.ShapeDtypeStruct((rows, DSSM), jnp.float32),
            compiler_params=params,
            cost_estimate=small_cost,
            name="mixer_join",
        )

    def outer(right_at, kind, after):
        each = 2
        return pl.pallas_call(
            partial(outer_body, kind),
            grid=(pairs // each,),
            in_specs=[
                pl.BlockSpec((each, 8, rows), lambda p: (p, 0, 0)),
                pl.BlockSpec((rows, each * wide), lambda p: (0, p)),
                pl.BlockSpec((rows, NS), lambda p: (0, right_at)),
            ]
            + [anywhere] * after,
            out_specs=pl.BlockSpec((each * wide, NS), lambda p: (p, 0)),
            out_shape=jax.ShapeDtypeStruct((DSSM, NS), jnp.bfloat16),
            compiler_params=params,
            cost_estimate=small_cost,
            name="state_outer",
        )

    x_spec = pl.BlockSpec((rows, wide), lambda p: (0, capped(p)))
    b_spec = pl.BlockSpec((rows, NS), lambda p: (0, DSSM // NS))
    c_spec = pl.BlockSpec((rows, NS), lambda p: (0, DSSM // NS + 1))
    row_spec = pl.BlockSpec((1, 8, rows), lambda p: (capped(p), 0, 0))
    skip_spec = pl.BlockSpec((1, 1, wide), lambda p: (capped(p), 0, 0))
    state_spec = pl.BlockSpec((wide, NS), lambda p: (capped(p), 0))
    docs_specs = [pl.BlockSpec((rows, 1), lambda p: (0, 0)), pl.BlockSpec((1, rows), lambda p: (0, 0))]
    square = pltpu.VMEM((rows, rows), jnp.float32)
    narrow = pltpu.VMEM((rows, NS), jnp.float32)
    forward = pl.pallas_call(
        mixed_body,
        grid=(pairs,),
        in_specs=[skip_spec, x_spec, b_spec, c_spec, row_spec] + docs_specs,
        out_specs=pl.BlockSpec((rows, wide), lambda p: (0, p)),
        out_shape=jax.ShapeDtypeStruct((rows, DSSM), jnp.float32),
        scratch_shapes=[square, square],
        compiler_params=params,
        cost_estimate=small_cost,
        name="mixer_forward",
    )
    backward = pl.pallas_call(
        mixed_grad_body,
        grid=(pairs + 2,),
        in_specs=[skip_spec, x_spec, b_spec, c_spec, row_spec]
        + docs_specs
        + [state_spec, state_spec, x_spec]
        + [anywhere] * anchors,
        out_specs=[
            pl.BlockSpec((rows, wide), lambda p: (0, p)),
            pl.BlockSpec((1, 1, wide), lambda p: (capped(p), 0, 0)),
        ],
        out_shape=[
            jax.ShapeDtypeStruct((rows, DSSM + 2 * NS), jnp.float32),
            jax.ShapeDtypeStruct((pairs, 1, wide), jnp.float32),
        ],
        scratch_shapes=[square, square, square, narrow, narrow],
        compiler_params=params,
        cost_estimate=small_cost,
        name="mixer_backward",
    )
    return outer, join, forward, backward


def gain_rows(gain):
    return jnp.pad(jnp.stack(split_three(gain)), ((0, 13), (0, NS - HM)))


def read_gain(rows):
    return jnp.sum(rows[..., :3, :HM].astype(jnp.float32), axis=-2)


def pass_state(part, gain, gains, reverse, after=None):
    count, position = lax.axis_size("ctx"), lax.axis_index("ctx")
    side, line_at = position % 2, position // 2
    is_first = (side == 1) if reverse else (side == 0)

    def by_head(array):
        return array.reshape(array.shape[:-2] + (HM, PM, NS)).astype(jnp.float32)

    got = exchange(part if gains else jnp.concatenate([part, gain_rows(gain)], axis=0), 1, 0)
    if gains:
        gain, other, line_gains = gains
    else:
        other = read_gain(got[DSSM:])
    own_f, got_f = by_head(part), by_head(got[:DSSM])
    first = jnp.where(is_first, own_f, got_f)
    second = jnp.where(is_first, got_f, own_f)
    first_gain = jnp.where(is_first, gain, other)[:, None, None]
    second_gain = jnp.where(is_first, other, gain)[:, None, None]
    total = (second_gain * first + second).astype(jnp.bfloat16).reshape(DSSM, NS)
    if not gains:
        total = jnp.concatenate([total, gain_rows(gain * other)], axis=0)
    if after is not None:
        total = tie(total, after)
    totals = lax.all_gather(total, "ctx", axis_index_groups=ctx_lines())
    if not gains:
        line_gains = read_gain(totals[:, DSSM:])
    totals = by_head(totals[:, :DSSM])
    factor = jnp.ones((HM,), jnp.float32)
    entering = jnp.zeros((HM, PM, NS), jnp.float32)
    lines = range(count // 2)
    for at in lines if reverse else reversed(lines):
        reached = at > line_at if reverse else at < line_at
        entering = entering + jnp.where(reached, factor, 0.0)[:, None, None] * totals[at]
        factor = factor * jnp.where(reached, line_gains[at], 1.0)
    state = jnp.where(is_first, entering, first_gain * entering + first)
    return state.astype(jnp.bfloat16).reshape(DSSM, NS), (gain, other, line_gains), total


def pack_small(norm, conv_weight, conv_bias, skip, mixer, ffn, shards):
    pieces = [
        norm.reshape(shards, -1),
        conv_weight.reshape(KW, shards, -1).transpose(1, 0, 2).reshape(shards, -1),
        conv_bias.reshape(shards, -1),
        mixer.reshape(shards, -1),
        ffn.reshape(shards, -1),
        skip.reshape(shards, -1),
    ]
    packed = jnp.concatenate(pieces, axis=1)
    packed = jnp.pad(packed, ((0, 0), (0, 4096 - packed.shape[1])))
    return packed.reshape(shards * 32, 128)


def unpack_small(packed, model, channels, heads, shards):
    packed = packed.reshape(shards, 4096)
    sizes = [model, KW * channels, channels, DSSM, model, heads]
    parts, start = [], 0
    for size in sizes:
        width = size // 4
        parts.append(packed[:, start : start + width])
        start += width
    norm, conv_weight, conv_bias, mixer, ffn, skip = parts
    conv_weight = conv_weight.reshape(shards, KW, -1).transpose(1, 0, 2).reshape(KW, -1)
    return (
        norm.reshape(-1),
        conv_weight,
        conv_bias.reshape(-1),
        skip.reshape(-1),
        mixer.reshape(-1),
        ffn.reshape(-1),
    )


def per_device(
    tokens,
    cotangent,
    doc_lengths,
    decay,
    norm_gain,
    in_proj,
    conv_weight,
    conv_bias,
    skip_gain,
    mixer_gain,
    mixer_out,
    query_proj,
    key_value_projection,
    attn_out,
    ffn_gain,
    gate_up,
    down_proj,
):
    rows, model = tokens.shape[1:]
    width = rows // 2
    shards = lax.axis_size("wshard")
    channels = conv_bias.shape[0] * shards
    count, block_at = lax.axis_size("ctx"), lax.axis_index("ctx")
    sequence_total = rows * count
    heads_per_group = QUERY_HEADS // KEY_VALUE_HEADS
    scale = HEAD_SIZE ** (-0.5)
    attend_forward, attend_backward = attention_calls(rows, count, (3, 3))
    state_outer, mixer_join, mixer_forward, mixer_backward = mixer_calls(rows, 4)

    lengths = doc_lengths[0]
    doc_count = lengths.shape[0]
    position_index = block_at * rows + jnp.arange(rows, dtype=jnp.int32)
    docs = doc_numbers(lengths, position_index)
    doc_prev = doc_numbers(lengths, position_index[:1] - 1)[0]
    log_decay = jnp.log(decay[0])
    mirrored = count - 1 - block_at
    group_blocks = jnp.stack([block_at, mirrored]).astype(jnp.int32)
    group_positions = jnp.stack(
        [
            block_at * rows + jnp.arange(width, dtype=jnp.int32),
            mirrored * rows + width + jnp.arange(width, dtype=jnp.int32),
        ]
    )
    group_docs = jnp.stack([doc_numbers(lengths, group_positions[at]) for at in range(2)])
    key_docs = doc_numbers(lengths, jnp.arange(sequence_total, dtype=jnp.int32))
    lane = jnp.arange(128)[None, :]
    key_side = ((key_docs[:, None] == lane) | ((lane >= 8) & (lane < 11))).astype(jnp.bfloat16)
    side_row = jnp.arange(16)[None, :, None]
    query_side = jnp.where(
        (side_row == group_docs[:, None, :]) | (side_row >= doc_count), 0.0, mask_fill_value
    ).astype(jnp.bfloat16)

    order = jnp.arange(rows)
    running = jnp.dot(
        log_decay, (order[:, None] <= order[None, :]).astype(jnp.float32), precision=highest
    )
    entry = jnp.where((docs == doc_prev)[None, :], jnp.exp(running), 0.0)
    tail = jnp.where((docs == docs[-1])[None, :], jnp.exp(running[:, -1:] - running), 0.0)
    carry_gain = jnp.where(docs[-1] == doc_prev, jnp.exp(running[:, -1]), 0.0)

    mixer_rows = (
        jnp.stack([running, entry, tail, jnp.zeros_like(tail)])
        .reshape(4, HM // 2, 2, rows)
        .transpose(1, 0, 2, 3)
        .reshape(HM // 2, 8, rows)
    )
    taps = jnp.stack(
        [
            (doc_numbers(lengths, position_index - (KW - 1) + tap) == docs).astype(jnp.float32)
            for tap in range(KW)
        ]
    )
    docs_column, docs_row = docs[:, None], docs[None, :]
    cosine, sine = turn_tables(position_index)
    mirrored_cosine, mirrored_sine = turn_tables(group_positions[1])
    prepared = lax.optimization_barrier(
        (
            key_side,
            query_side,
            mixer_rows,
            taps,
            docs_column,
            docs_row,
            cosine,
            sine,
            mirrored_cosine,
            mirrored_sine,
            group_blocks,
        )
    )
    (
        key_side,
        query_side,
        mixer_rows,
        taps,
        docs_column,
        docs_row,
        cosine,
        sine,
        mirrored_cosine,
        mirrored_sine,
        group_blocks,
    ) = prepared
    packed = pack_small(norm_gain, conv_weight, conv_bias, skip_gain, mixer_gain, ffn_gain, 1)
    first_shard = jnp.concatenate([in_proj, query_proj, key_value_projection], axis=1)
    packed = jnp.pad(packed.reshape(1, -1), ((0, 15), (0, first_shard.shape[1] - 4096)))
    first_w, small, arrived = gather_first(
        jnp.concatenate([first_shard, packed], axis=0), in_proj.shape[0], prepared
    )
    norm_w, conv_w, conv_b, skip_w, mixer_g, ffn_g = (
        part.astype(jnp.float32)
        for part in unpack_small(small[:, :4096], model, channels, HM, shards)
    )
    projected_width = in_proj.shape[1]
    in_w, attn_pair_w = first_w[:, :projected_width], first_w[:, projected_width:]
    out_pieces = start_shards(
        jnp.concatenate([mixer_out, attn_out, down_proj], axis=0), arrived
    )
    gate_up_pieces = start_shards(gate_up, arrived)
    source = tokens[0].astype(jnp.float32)
    normed, norm_pull = jax.vjp(rms_scale, source, norm_w)
    normed_b = normed.astype(jnp.bfloat16)
    projected = mixed_dot(normed_b, first_w)

    query_width = QUERY_HEADS * HEAD_SIZE
    attn_inputs = projected[:, projected_width:].T
    turned_q = turn(
        attn_inputs[:query_width].reshape(QUERY_HEADS, HEAD_SIZE, rows), cosine, sine
    ).astype(jnp.bfloat16)
    key_value_pair = attn_inputs[query_width:].reshape(2, KEY_VALUE_HEADS, HEAD_SIZE, rows)
    keys_b = turn(key_value_pair[0], cosine, sine).astype(jnp.bfloat16)
    values_b = key_value_pair[1].astype(jnp.bfloat16)
    pairs = lax.all_gather(
        jnp.concatenate([keys_b, values_b], axis=1).transpose(0, 2, 1), "ctx"
    )
    turned_q = turned_q * jnp.asarray(scale, jnp.bfloat16)
    mirrored_q = swap_mirrored(turned_q[:, :, width:])

    gate_z = projected[:, :DSSM]
    pre_b = projected[:, DSSM:projected_width].astype(jnp.bfloat16)
    rim = from_behind(pre_b[rows - (KW - 1) :], "ctx", 1)
    extended = jnp.concatenate([rim, pre_b], axis=0).astype(jnp.float32)
    conv_f, conv_pull = jax.vjp(partial(conv_local, taps), extended, conv_w, conv_b)
    conv_b16 = conv_f.astype(jnp.bfloat16)
    skip_wide = jnp.repeat(skip_w, PM).reshape(HM // 2, 1, 2 * PM)
    fresh = state_outer(DSSM // NS, 4, 0)(mixer_rows, conv_b16, conv_b16)
    state_in, gains, _ = pass_state(fresh, carry_gain, None, False, pairs)
    local = mixer_forward(
        skip_wide, conv_b16, conv_b16, conv_b16, mixer_rows, docs_column, docs_row
    )

    heads_own, heads_mirrored, log_x = attend_forward(
        group_blocks,
        pairs,
        key_side,
        turned_q,
        mirrored_q,
        query_side,
        out_pieces[1],
        gate_up_pieces[1],
        local,
    )
    mixer_w, attn_w, down_w = finish_shards(
        out_pieces,
        [mixer_out.shape[0], attn_out.shape[0], down_proj.shape[0]],
        log_x,
    )
    (gate_up_w,) = finish_shards(gate_up_pieces, [gate_up.shape[0]], log_x)
    heads_back = swap_mirrored(heads_mirrored.astype(jnp.bfloat16))
    heads_t = jnp.concatenate([heads_own.astype(jnp.bfloat16), heads_back], axis=2).reshape(
        QUERY_HEADS * HEAD_SIZE, rows
    )
    mixed = mixer_join(0)(conv_b16, mixer_rows, state_in, local)
    gated, gate_pull = jax.vjp(gate_norm, mixed, gate_z, mixer_g)
    gated_b = gated.astype(jnp.bfloat16)
    mamba = mixed_dot(gated_b, mixer_w)
    attn = lax.dot_general(
        heads_t, attn_w, (((0,), (0,)), ((), ())), preferred_element_type=jnp.float32
    )
    middle = source + attn + mamba
    normed2, ffn_pull = jax.vjp(rms_scale, middle, ffn_g)
    normed2_b = normed2.astype(jnp.bfloat16)
    gate_up_v = mixed_dot(normed2_b, gate_up_w)
    activated, act_pull = jax.vjp(swiglu, gate_up_v)
    activated_b = activated.astype(jnp.bfloat16)
    layer_out = (middle + mixed_dot(activated_b, down_w)).astype(jnp.bfloat16)

    out_low = cotangent[0]
    down_sum, down_beside, down_across, _ = weight_grad(activated_b, out_low)
    (gate_up_grad_v,) = act_pull(nt_dot(out_low, down_w))
    gate_up_low = gate_up_grad_v.astype(jnp.bfloat16)
    gate_up_sum, gate_up_beside, _, gate_up_sent = weight_grad(normed2_b, gate_up_low)
    gate_up_half, gate_up_got, gate_up_give = ctx_half([gate_up_sum], model // shards)
    middle_norm_grad, ffn_gain_grad = ffn_pull(nt_dot(gate_up_low, gate_up_w))
    middle_grad = out_low.astype(jnp.float32) + middle_norm_grad
    middle_low = middle_grad.astype(jnp.bfloat16)
    heads_low = nt_dot(attn_w, middle_low).astype(jnp.bfloat16)
    heads_low = heads_low.reshape(QUERY_HEADS, HEAD_SIZE, rows)
    mirrored_low = swap_mirrored(heads_low[:, :, width:])
    gated_grad = nt_dot(middle_low, mixer_w)
    mixed_grad, gate_z_grad, mixer_gain_grad = gate_pull(gated_grad)
    upward = state_outer(DSSM // NS + 1, 2, 2)(
        mixer_rows, mixed_grad.astype(jnp.bfloat16), conv_b16, down_beside, gate_up_sent
    )
    state_out_grad, _, pair_total = pass_state(upward, None, gains, True)
    down_half, down_got, _ = ctx_half([tie(down_sum, upward)], model // shards)
    gate_z_low = gate_z_grad.astype(jnp.bfloat16)
    query_grad_own, query_grad_mirrored, pairs_grad = attend_backward(
        group_blocks,
        pairs,
        key_side,
        turned_q,
        mirrored_q,
        query_side,
        log_x,
        heads_own,
        heads_mirrored,
        heads_low,
        mirrored_low,
        gate_up_beside,
        down_across,
        pair_total,
    )
    mixer_products = split_products(gated_b, middle_low)
    attn_products = split_products(heads_t, middle_low, 0)
    shard_sizes = [mixer_out.shape[0], attn_out.shape[0]]

    def interleaved(parts):
        return jnp.concatenate(
            [
                part[start * size : (start + 1) * size]
                for start in range(parts[0].shape[0] // shard_sizes[0])
                for part, size in zip(parts, shard_sizes)
            ],
            axis=0,
        ).astype(jnp.bfloat16)

    mixer_attn_started = start_sum(
        *[interleaved(parts) for parts in zip(mixer_products, attn_products)], pairs_grad
    )
    in_z_started = start_sum(*split_products(normed_b, gate_z_low), pairs_grad)
    query_low_own, query_low_mirrored = (
        (turn(grad, *tables) * scale).astype(jnp.bfloat16)
        for grad, tables in (
            (query_grad_own, (cosine[:, :width], -sine[:, :width])),
            (query_grad_mirrored, (mirrored_cosine, -mirrored_sine)),
        )
    )
    query_low = jnp.concatenate(
        [query_low_own, swap_mirrored(query_low_mirrored)], axis=2
    ).reshape(QUERY_HEADS * HEAD_SIZE, rows)

    conv_grad, skip_parts = mixer_backward(
        skip_wide,
        conv_b16,
        conv_b16,
        conv_b16,
        mixer_rows,
        docs_column,
        docs_row,
        state_in,
        state_out_grad,
        mixed_grad,
        gate_up_give,
        in_z_started[1],
        down_got,
        mixer_attn_started[1],
    )
    pair_grad = scatter_blocks(pairs_grad, conv_grad).astype(jnp.float32).transpose(0, 2, 1)
    skip_grad = jnp.sum(skip_parts.reshape(HM, PM), axis=1)
    extended_grad, conv_weight_grad, conv_bias_grad = conv_pull(conv_grad)
    from_above = from_behind(extended_grad[: KW - 1], "ctx", -1)
    pre_grad = extended_grad[KW - 1 :] + jnp.pad(from_above, ((rows - (KW - 1), 0), (0, 0)))
    pre_low = tie(pre_grad.astype(jnp.bfloat16), gate_up_got)
    mixer_attn_sum = finish_sum(mixer_attn_started, pre_low)
    in_sum_z = finish_sum(in_z_started, pre_low)
    mixer_half, _, _ = ctx_half([mixer_attn_sum, in_sum_z], model // shards)
    in_sum_pre = weight_grad(normed_b, pre_low)[0]
    projected_low = jnp.concatenate([gate_z_low, pre_low], axis=1)
    normed_grad = nt_dot(projected_low, in_w)

    keys_low = turn(pair_grad[:, :HEAD_SIZE], cosine, -sine)
    keyval_low = jnp.concatenate(
        [
            keys_low.reshape(KEY_VALUE_HEADS * HEAD_SIZE, rows),
            pair_grad[:, HEAD_SIZE:].reshape(KEY_VALUE_HEADS * HEAD_SIZE, rows),
        ],
        axis=0,
    ).astype(jnp.bfloat16)
    attn_pair_low = jnp.concatenate([query_low, keyval_low], axis=0).T
    attn_pair_sum = weight_grad(normed_b, attn_pair_low)[0]
    normed_grad = normed_grad + nt_dot(attn_pair_low, attn_pair_w)
    source_grad, norm_grad = norm_pull(normed_grad)
    tokens_grad = (middle_grad + source_grad)[None]

    small_grad = pack_small(
        norm_grad, conv_weight_grad, conv_bias_grad, skip_grad, mixer_gain_grad, ffn_gain_grad, shards
    )
    small_share = sum_small(small_grad)
    last_half, _, _ = ctx_half([in_sum_pre, attn_pair_sum], model // shards)
    (gate_up_share, down_share, mixer_attn_share, in_share_z), summed = ctx_finish(
        jnp.concatenate([gate_up_half, down_half, mixer_half], axis=1),
        [gate_up_sum.shape, down_sum.shape, mixer_attn_sum.shape, in_sum_z.shape],
        0,
    )
    mixer_share = mixer_attn_share[: mixer_out.shape[0]]
    attn_share = mixer_attn_share[mixer_out.shape[0] :]
    (in_share_pre, attn_pair_share), _ = ctx_finish(
        tie(last_half, summed),
        [in_sum_pre.shape, attn_pair_sum.shape],
        3,
    )
    norm_share, conv_w_share, conv_b_share, skip_share, mixer_g_share, ffn_share = unpack_small(
        small_share, model, channels, HM, 1
    )
    return (
        layer_out[None],
        tokens_grad,
        norm_share,
        jnp.concatenate([in_share_z, in_share_pre], axis=1),
        conv_w_share,
        conv_b_share,
        skip_share,
        mixer_g_share,
        mixer_share,
        attn_pair_share[:, : QUERY_HEADS * HEAD_SIZE],
        attn_pair_share[:, QUERY_HEADS * HEAD_SIZE :],
        attn_share,
        ffn_share,
        gate_up_share,
        down_share,
    )


def solution(mesh):
    in_specs = (
        P("wshard", "ctx", None),
        P("wshard", "ctx", None),
        P("wshard", None),
        P("wshard", None, "ctx"),
        P("wshard"),
        P("wshard", None),
        P(None, "wshard"),
        P("wshard"),
        P("wshard"),
        P("wshard"),
        P("wshard", None),
        P("wshard", None),
        P("wshard", None),
        P("wshard", None),
        P("wshard"),
        P("wshard", None),
        P("wshard", None),
    )
    out_specs = (
        P("wshard", "ctx", None),
        P("wshard", "ctx", None),
        P("wshard"),
        P("wshard", None),
        P(None, "wshard"),
        P("wshard"),
        P("wshard"),
        P("wshard"),
        P("wshard", None),
        P("wshard", None),
        P("wshard", None),
        P("wshard", None),
        P("wshard"),
        P("wshard", None),
        P("wshard", None),
    )
    return jax.shard_map(
        per_device, mesh=mesh, in_specs=in_specs, out_specs=out_specs, check_vma=False
    )
```
